32 devices in a mesh: ctx: 8 (over z, y), tp: 2 (over x), fs: 2 (over core).
Axes of the slice: x: 2, y: 2, z: 4, core: 2. Of those that a mesh axis runs over, the one named last changes fastest.
Arguments:
- tokens: bfloat16 [2, 8192, 1024], P('fs', 'ctx'), may hold values from -6 to 6
- cotangent: bfloat16 [2, 8192, 1024], P('fs', 'ctx'), may hold values from -6 to 6
- lengths: int32 [2, 3], P('fs'), may hold values from 512 to 4096, as said below
- order: int32 [2, 8192], P('fs'), may hold values from 0 to 8191, as said below
- mixer_gain: bfloat16 [1024], P('fs'), may hold values from 0.5 to 1.5
- w_query: bfloat16 [1024, 1024], P('fs', 'tp'), may hold values from -0.1875 to 0.1875
- w_key: bfloat16 [1024, 1024], P('fs', 'tp'), may hold values from -0.1875 to 0.1875
- w_value: bfloat16 [1024, 2048], P('fs', 'tp'), may hold values from -0.1875 to 0.1875
- w_outgate: bfloat16 [1024, 2048], P('fs', 'tp'), may hold values from -0.1875 to 0.1875
- w_decay: bfloat16 [1024, 8], P('fs', 'tp'), may hold values from -0.1875 to 0.1875
- w_beta: bfloat16 [1024, 8], P('fs', 'tp'), may hold values from -0.1875 to 0.1875
- conv_query: bfloat16 [1024, 4], P(('tp', 'fs')), may hold values from -3 to 3
- conv_key: bfloat16 [1024, 4], P(('tp', 'fs')), may hold values from -3 to 3
- conv_value: bfloat16 [2048, 4], P(('tp', 'fs')), may hold values from -3 to 3
- decay_log: float32 [8], P('tp'), may hold values from -5 to 1
- decay_bias: float32 [8], P('tp'), may hold values from -4 to 0
- out_gain: bfloat16 [256], P('fs'), may hold values from 0.5 to 1.5
- w_output: bfloat16 [2048, 1024], P(('tp', 'fs')), may hold values from -0.25 to 0.25
- mlp_gain: bfloat16 [1024], P('fs'), may hold values from 0.5 to 1.5
- w_gate: bfloat16 [1024, 2816], P('fs', 'tp'), may hold values from -0.1875 to 0.1875
- w_up: bfloat16 [1024, 2816], P('fs', 'tp'), may hold values from -0.1875 to 0.1875
- w_down: bfloat16 [2816, 1024], P(('tp', 'fs')), may hold values from -0.21875 to 0.21875
Outputs:
- block_out: bfloat16 [2, 8192, 1024], P('fs', 'ctx')
- grad_tokens: bfloat16 [2, 8192, 1024], P('fs', 'ctx')
- grad_mixer_gain: float32 [1024], P('fs')
- grad_query: float32 [1024, 1024], P('fs', 'tp')
- grad_key: float32 [1024, 1024], P('fs', 'tp')
- grad_value: float32 [1024, 2048], P('fs', 'tp')
- grad_outgate: float32 [1024, 2048], P('fs', 'tp')
- grad_decay: float32 [1024, 8], P('fs', 'tp')
- grad_beta: float32 [1024, 8], P('fs', 'tp')
- grad_conv_query: float32 [1024, 4], P(('tp', 'fs'))
- grad_conv_key: float32 [1024, 4], P(('tp', 'fs'))
- grad_conv_value: float32 [2048, 4], P(('tp', 'fs'))
- grad_decay_log: float32 [8], P('tp')
- grad_decay_bias: float32 [8], P('tp')
- grad_out_gain: float32 [256], P('fs')
- grad_output: float32 [2048, 1024], P(('tp', 'fs'))
- grad_mlp_gain: float32 [1024], P('fs')
- grad_gate: float32 [1024, 2816], P('fs', 'tp')
- grad_up: float32 [1024, 2816], P('fs', 'tp')
- grad_down: float32 [2816, 1024], P(('tp', 'fs'))
The draws below stay inside these ranges and needn't reach their ends.
Inputs may be any that keep to these rules, and one draw needn't show every extreme that they name: `lengths`: each pack holds 3 sequences laid end to end that fill all 8192 places; in every pack exactly one, which one drawn, has the length 4096. `order`: each row is a permutation of the 8192 places. Of the tokens at given places i * 1024 to (i + 1) * 1024 - 1, exactly 128 lie at packed places j * 1024 to (j + 1) * 1024 - 1, for every i and j.
All inputs are finite; a program needn't handle non-finite values.
Results may differ from the reference program's by a relative error of at most 0.014.
Values may be sent and summed in bfloat16 or wider, within the bound.
A program may use at most 448 MiB of HBM per device.

```python
import jax
import jax.numpy as jnp
from jax import lax

D = 1024
H = 8
DK = 128
DV = 256
FF = 2816
CONV = 4
BLOCK = 64
TOK_DEV = 1024
TOKENS = 8192
MAXLEN = 4096
BATCH = 2


def draw_lengths(key, part):
    group_count = TOKENS // MAXLEN
    low_len = MAXLEN // 8
    high_len = MAXLEN - MAXLEN // 8

    def per_batch(batch_key):
        pick_key, lead_key, split_key = jax.random.split(batch_key, 3)
        longest = jax.random.randint(pick_key, (), 0, group_count - 1)
        leading = jax.random.randint(lead_key, (), low_len, high_len)
        cuts = jax.random.randint(split_key, (group_count - 1,), low_len, high_len)
        group_ids = jnp.arange(group_count - 1)
        firsts = jnp.where(group_ids == longest, MAXLEN, cuts)
        seconds = jnp.where(group_ids == longest, 0, MAXLEN - cuts)
        middle = jnp.stack([firsts, seconds], axis=1).reshape(-1)
        placing = jnp.argsort((middle == 0).astype(jnp.int32), stable=True)
        packed = middle[placing][:2 * group_count - 3]
        return jnp.concatenate([leading[None], packed, (MAXLEN - leading)[None]]).astype(jnp.int32)
    return jax.vmap(per_batch)(jax.random.split(jax.random.fold_in(key, 11), BATCH))


def draw_order(key, part):
    group_count = TOKENS // TOK_DEV
    per_peer = TOK_DEV // group_count

    def shuffled(sub_key):
        return jax.random.permutation(sub_key, TOK_DEV).astype(jnp.int32)

    def per_batch(batch_key):
        send_key, land_key = jax.random.split(batch_key)
        send_perm = jax.vmap(shuffled)(jax.random.split(send_key, group_count))
        land_perm = jax.vmap(shuffled)(jax.random.split(land_key, group_count))
        source = jnp.arange(group_count, dtype=jnp.int32)[:, None]
        local_iota = jnp.arange(TOK_DEV, dtype=jnp.int32)[None, :]
        target = send_perm // per_peer
        within = send_perm % per_peer
        landing = land_perm[target, source * per_peer + within]
        owner = target * TOK_DEV + landing
        given = source * TOK_DEV + local_iota
        return jnp.zeros((TOKENS,), jnp.int32).at[owner.reshape(-1)].set(given.reshape(-1))
    return jax.vmap(per_batch)(jax.random.split(jax.random.fold_in(key, 23), BATCH))


def block_levels(own_key, dims, pieces, smallest, largest):
    factor_of = 1.0
    for position, parts in pieces:
        draws = jax.random.uniform(jax.random.fold_in(jax.random.fold_in(own_key, 6), position), (parts,), jnp.float32, smallest / len(pieces), largest / len(pieces))
        factor_of = factor_of * jnp.repeat(jnp.exp(draws), dims[position] // parts).reshape((-1,) + (1,) * (len(dims) - 1 - position))
    return factor_of


def scatter_about(key, extent, scale, limit, shards=(), kind=jnp.bfloat16):
    drawn = jax.random.normal(key, extent, jnp.float32) * scale
    if len(shards) > 0:
        drawn = block_levels(key, extent, shards, -0.22, 0.18) * drawn
    return jnp.clip(drawn, min=-limit, max=limit).astype(kind)


def setup_inputs(seed: int = 0) -> dict:
    arg_keys = jax.random.split(jax.random.key(seed), 23)
    tokens = scatter_about(arg_keys[0], (BATCH, TOKENS, D), 1.0, 6.0, ((0, 2), (1, 8)))
    cotangent = scatter_about(arg_keys[1], (BATCH, TOKENS, D), 1.0, 6.0, ((0, 2), (1, 8)))
    lengths = draw_lengths(jax.random.fold_in(arg_keys[22], 71), 0)
    order = draw_order(jax.random.fold_in(arg_keys[22], 71), 0)
    mixer_gain = jnp.clip(1.0 + 0.1 * jax.random.normal(arg_keys[4], (D,), jnp.float32), 0.5, 1.5).astype(jnp.bfloat16)
    w_query = scatter_about(arg_keys[5], (D, H * DK), D ** -0.5, 0.1875, ((0, 2), (1, 2)))
    w_key = scatter_about(arg_keys[6], (D, H * DK), D ** -0.5, 0.1875, ((0, 2), (1, 2)))
    w_value = scatter_about(arg_keys[7], (D, H * DV), D ** -0.5, 0.1875, ((0, 2), (1, 2)))
    w_outgate = scatter_about(arg_keys[8], (D, H * DV), D ** -0.5, 0.1875, ((0, 2), (1, 2)))
    w_decay = scatter_about(arg_keys[9], (D, H), D ** -0.5, 0.1875, ((0, 2), (1, 2)))
    w_beta = scatter_about(arg_keys[10], (D, H), D ** -0.5, 0.1875, ((0, 2), (1, 2)))
    conv_query = scatter_about(arg_keys[11], (H * DK, CONV), CONV ** -0.5, 3.0, ((0, 4),))
    conv_key = scatter_about(arg_keys[12], (H * DK, CONV), CONV ** -0.5, 3.0, ((0, 4),))
    conv_value = scatter_about(arg_keys[13], (H * DV, CONV), CONV ** -0.5, 3.0, ((0, 4),))
    decay_log = jnp.clip(-5.0 + 6.0 * jax.random.uniform(arg_keys[14], (H,), jnp.float32) ** block_levels(arg_keys[14], (H,), ((0, 2),), -0.2, 0.2), -5.0, 1.0)
    decay_bias = jnp.clip(-4.0 + 4.0 * jax.random.uniform(arg_keys[15], (H,), jnp.float32) ** block_levels(arg_keys[15], (H,), ((0, 2),), -0.2, 0.2), -4.0, 0.0)
    out_gain = jnp.clip(1.0 + 0.1 * jax.random.normal(arg_keys[16], (DV,), jnp.float32), 0.5, 1.5).astype(jnp.bfloat16)
    w_output = scatter_about(arg_keys[17], (H * DV, D), (H * DV // 4) ** -0.5, 0.25, ((0, 4),))
    mlp_gain = jnp.clip(1.0 + 0.1 * jax.random.normal(arg_keys[18], (D,), jnp.float32), 0.5, 1.5).astype(jnp.bfloat16)
    w_gate = scatter_about(arg_keys[19], (D, FF), D ** -0.5, 0.1875, ((0, 2), (1, 2)))
    w_up = scatter_about(arg_keys[20], (D, FF), D ** -0.5, 0.1875, ((0, 2), (1, 2)))
    w_down = scatter_about(arg_keys[21], (FF, D), (FF // 4) ** -0.5, 0.21875, ((0, 4),))
    return dict(tokens=tokens, cotangent=cotangent, lengths=lengths, order=order, mixer_gain=mixer_gain, w_query=w_query, w_key=w_key, w_value=w_value, w_outgate=w_outgate, w_decay=w_decay, w_beta=w_beta, conv_query=conv_query, conv_key=conv_key, conv_value=conv_value, decay_log=decay_log, decay_bias=decay_bias, out_gain=out_gain, w_output=w_output, mlp_gain=mlp_gain, w_gate=w_gate, w_up=w_up, w_down=w_down)


epsilon = 1e-06
precision_highest = lax.Precision.HIGHEST

@jax.custom_vjp
def low(v):
    return lax.optimization_barrier(v.astype(jnp.bfloat16)).astype(jnp.float32)

@jax.custom_vjp
def low_back(v):
    return v

def low_keep(v):
    return (low(v), None)

def low_pass(kept, grad):
    return (grad,)

def back_keep(v):
    return (v, None)

def back_low(kept, grad):
    return (low(grad),)
low.defvjp(low_keep, low_pass)
low_back.defvjp(back_keep, back_low)

def matmul(left, right):
    return jnp.dot(left, right, precision=precision_highest)

def rms_norm(values, gain_vec):
    return values * lax.rsqrt(lax.optimization_barrier(jnp.mean(values * values, axis=-1, keepdims=True)) + epsilon) * gain_vec

def unit_rows(values):
    return values * lax.rsqrt(lax.optimization_barrier(jnp.sum(values * values, axis=-1, keepdims=True)) + epsilon)

def causal_mix(projected, weight, tap_valid):
    row_count = projected.shape[0]
    taps = weight.shape[1]
    padded = jnp.pad(projected, ((taps - 1, 0), (0, 0)))
    summed = jnp.zeros_like(projected)
    for tap_index in range(taps):
        summed = summed + padded[tap_index:tap_index + row_count] * weight[:, tap_index] * tap_valid[:, taps - 1 - tap_index][:, None]
    return summed

def delta_step(memory_state, step_data):
    query_rows, key_vectors, value_vecs, beta_vals, decay_vals = step_data
    recalled_values = jnp.einsum('qcg,qc->qg', memory_state, key_vectors, precision=precision_highest)
    erased = memory_state - beta_vals[:, None, None] * key_vectors[:, :, None] * recalled_values[:, None, :]
    memory_state = decay_vals[:, None, None] * erased + beta_vals[:, None, None] * key_vectors[:, :, None] * value_vecs[:, None, :]
    return (memory_state, jnp.einsum('qcg,qc->qg', memory_state, query_rows, precision=precision_highest))

def delta_rule(query_rows, key_vectors, value_vecs, beta_vals, decay_vals):
    row_count, head_count, key_width = key_vectors.shape
    block_count = row_count // BLOCK

    def run_block(memory_state, element):
        return lax.scan(delta_step, memory_state, element)
    shaped = (query_rows.reshape(block_count, BLOCK, head_count, -1), key_vectors.reshape(block_count, BLOCK, head_count, -1), value_vecs.reshape(block_count, BLOCK, head_count, -1), beta_vals.reshape(block_count, BLOCK, head_count), decay_vals.reshape(block_count, BLOCK, head_count))
    start_memory = jnp.zeros((head_count, key_width, value_vecs.shape[-1]), jnp.float32)
    final_memory, outputs = lax.scan(jax.checkpoint(run_block), start_memory, shaped)
    return outputs.reshape(row_count, head_count, -1)

def block_layer(inputs, params, tap_valid, keep_gate):
    mixer_gain, w_query, w_key, w_value, w_outgate, w_decay, w_beta, conv_query, conv_key, conv_value, decay_log, decay_bias, out_gain, w_output, mlp_gain, w_gate, w_up, w_down = params
    row_count = inputs.shape[0]
    head_count = decay_log.shape[0]
    normed = low(rms_norm(inputs, mixer_gain))
    query_proj = low_back(matmul(normed, w_query))
    key_proj = low_back(matmul(normed, w_key))
    value_proj = low_back(matmul(normed, w_value))
    outgate_proj = low_back(matmul(normed, w_outgate))
    decay_proj = low_back(matmul(normed, w_decay))
    beta_proj = low_back(matmul(normed, w_beta))
    query_rows = unit_rows(jax.nn.silu(causal_mix(query_proj, conv_query, tap_valid)).reshape(row_count, head_count, -1))
    query_rows = query_rows * query_rows.shape[-1] ** (-0.5)
    key_vectors = unit_rows(jax.nn.silu(causal_mix(key_proj, conv_key, tap_valid)).reshape(row_count, head_count, -1))
    value_vecs = jax.nn.silu(causal_mix(value_proj, conv_value, tap_valid)).reshape(row_count, head_count, -1)
    beta_vals = jax.nn.sigmoid(beta_proj)
    decay_vals = jnp.exp(-jnp.exp(decay_log) * jax.nn.softplus(decay_proj + decay_bias)) * keep_gate[:, None]
    heads_out = delta_rule(query_rows, key_vectors, value_vecs, beta_vals, decay_vals)
    gating = jax.nn.silu(outgate_proj.reshape(row_count, head_count, -1))
    mixer_rows = low((rms_norm(heads_out, out_gain) * gating).reshape(row_count, -1))
    middle = inputs + low_back(matmul(mixer_rows, w_output))
    normed_two = low(rms_norm(middle, mlp_gain))
    gate_proj = low_back(matmul(normed_two, w_gate))
    up_proj = low_back(matmul(normed_two, w_up))
    hidden = low(jax.nn.silu(gate_proj) * up_proj)
    return middle + low_back(matmul(hidden, w_down))

def reference(tokens, cotangent, lengths, order, mixer_gain, w_query, w_key, w_value, w_outgate, w_decay, w_beta, conv_query, conv_key, conv_value, decay_log, decay_bias, out_gain, w_output, mlp_gain, w_gate, w_up, w_down):
    params = tuple((weight.astype(jnp.float32) for weight in (mixer_gain, w_query, w_key, w_value, w_outgate, w_decay, w_beta, conv_query, conv_key, conv_value, decay_log, decay_bias, out_gain, w_output, mlp_gain, w_gate, w_up, w_down)))
    totals = None
    results = []
    grads_in = []
    for batch_index in range(tokens.shape[0]):
        arrange = order[batch_index]
        seq_lengths = lengths[batch_index]
        offsets = jnp.cumsum(seq_lengths) - seq_lengths
        row_count = arrange.shape[0]
        positions = jnp.arange(row_count, dtype=jnp.int32)
        seq_number = lax.optimization_barrier(jnp.sum((offsets[None, :] <= positions[:, None]).astype(jnp.int32), axis=1))
        padded = jnp.concatenate([jnp.zeros((CONV - 1,), jnp.int32), seq_number])
        tap_valid = jnp.stack([(padded[CONV - 1 - tap_lag:CONV - 1 - tap_lag + row_count] == seq_number).astype(jnp.float32) for tap_lag in range(CONV)], axis=1)
        keep_gate = 1.0 - jnp.any(offsets[None, :] == positions[:, None], axis=1).astype(jnp.float32)
        inputs = tokens[batch_index].astype(jnp.float32)[arrange]

        def forward(layer_in, layer_params):
            return block_layer(layer_in, layer_params, tap_valid, keep_gate)
        result, pull_back = jax.vjp(forward, inputs, params)
        grad_in, grad_params = pull_back(cotangent[batch_index].astype(jnp.float32)[arrange])
        results.append(jnp.zeros_like(result).at[arrange].set(result))
        grads_in.append(jnp.zeros_like(grad_in).at[arrange].set(grad_in))
        if totals is None:
            totals = grad_params
        else:
            totals = tuple((first + second for first, second in zip(totals, grad_params)))
    block_out = jnp.stack(results).astype(jnp.bfloat16)
    grad_tokens = jnp.stack(grads_in).astype(jnp.bfloat16)
    return (block_out, grad_tokens, totals[0], totals[1], totals[2], totals[3], totals[4], totals[5], totals[6], totals[7], totals[8], totals[9], totals[10], totals[11], totals[12], totals[13], totals[14], totals[15], totals[16], totals[17])
```

```python
import functools

import jax
import jax.numpy as jnp
from jax import lax
from jax.experimental import pallas as pl
from jax.experimental.pallas import tpu as pltpu
from jax.sharding import PartitionSpec as P

TAPS = 4
CHUNK = 128
EPS = 1e-6
LANES = 128
START, VALID, AHEAD = 8, 8, 11
HI = lax.Precision.HIGHEST
bf16 = jnp.bfloat16
f32 = jnp.float32
MIB = 1024 * 1024


def mm(a, b):
    return jnp.dot(a.astype(bf16), b.astype(bf16), preferred_element_type=f32)


def mm_nt(a, b):
    return lax.dot_general(
        a.astype(bf16), b.astype(bf16), (((1,), (1,)), ((), ())), preferred_element_type=f32
    )


def mm_tn(a, b):
    return lax.dot_general(
        a.astype(bf16), b.astype(bf16), (((0,), (0,)), ((), ())), preferred_element_type=f32
    )


def mm_hi(a, b):
    return jnp.dot(a, b, precision=HI, preferred_element_type=f32)


def silu(x):
    return x * jax.nn.sigmoid(x)


def silu_grad(x):
    s = jax.nn.sigmoid(x)
    return s * (1.0 + x * (1.0 - s))


def softplus(x):
    return jnp.maximum(x, 0.0) + jnp.log1p(jnp.exp(-jnp.abs(x)))


def grid_of(rows, cols):
    return (
        lax.broadcasted_iota(jnp.int32, (rows, cols), 0),
        lax.broadcasted_iota(jnp.int32, (rows, cols), 1),
    )


def lower_inverses(systems):
    size = systems[0].shape[0]
    row, col = grid_of(size, size)
    eye = (row == col).astype(f32)
    first = ((row >> 1) == (col >> 1)) & (row > col)
    inverses = [eye - jnp.where(first, low, 0.0) for low in systems]
    level = 1
    while (1 << level) < size:
        block = (
            ((row >> (level + 1)) == (col >> (level + 1)))
            & (((row >> level) & 1) == 1)
            & (((col >> level) & 1) == 0)
        )
        parts = [mm(jnp.where(block, low, 0.0), inv) for low, inv in zip(systems, inverses)]
        inverses = [inv - mm(inv, part) for inv, part in zip(inverses, parts)]
        level += 1
    return inverses


def chunk_gates(cum, heads):
    size = cum.shape[0]
    row, col = grid_of(size, size)
    across = jnp.transpose(cum)
    seg_col = cum[:, START : START + 1]
    linked = (row >= col) & (seg_col == across[START : START + 1, :])
    from_start = seg_col == 0.0
    to_end = seg_col == cum[size - 1 : size, START : START + 1]
    out = []
    for h in range(heads):
        down = cum[:, h : h + 1]
        gap = jnp.where(linked, down - across[h : h + 1, :], 0.0)
        decay = jnp.where(linked, jnp.exp(gap), 0.0)
        entry = jnp.where(from_start, jnp.exp(down), 0.0)
        last = cum[size - 1 : size, h : h + 1]
        tail = jnp.where(to_end, jnp.exp(jnp.where(to_end, last - down, 0.0)), 0.0)
        out.append((decay, entry, tail, entry[size - 1 : size, :]))
    return out


def unit_scale(x):
    return lax.rsqrt(jnp.sum(x * x, axis=-1, keepdims=True) + EPS)


def forward_kernel(
    heads, dk, dv,
    proj, ab, flags, halo, taps, head,
    conv, local, qa, states, tinv, uval, wkey, qeff, ktail, cum_out, last,
    ext, state,
):
    step = pl.program_id(0)
    size = proj.shape[0]
    width = proj.shape[1]

    @pl.when(step == 0)
    def _():
        ext[0:8, :] = halo[...]
        row, col = grid_of(dk, dk)
        for h in range(heads):
            state[h, :, 0:dv] = jnp.zeros((dk, dv), f32)
            state[h, :, dv : dv + dk] = (row == col).astype(f32)

    @pl.when(step > 0)
    def _():
        ext[0:8, :] = ext[size : size + 8, :]

    ext[8 : 8 + size, :] = proj[...]
    fl = flags[...]
    valid = [jnp.broadcast_to(fl[:, VALID + s : VALID + s + 1], (size, LANES)) for s in (1, 2, 3)]
    for lo in range(0, width, LANES):
        at = slice(lo, lo + LANES)
        total = ext[8 : 8 + size, at] * taps[3:4, at]
        for s in (1, 2, 3):
            total += ext[8 - s : 8 - s + size, at] * taps[3 - s : 4 - s, at] * valid[s - 1]
        conv[:, at] = total

    raw = ab[...]
    lane = lax.broadcasted_iota(jnp.int32, (size, LANES), 1)
    log_decay = -jnp.exp(head[0:1, :]) * softplus(raw + head[1:2, :])
    row, col = grid_of(size, size)
    cum = mm_hi((row >= col).astype(f32), jnp.where(lane < heads, log_decay, fl))
    cum_out[...] = cum
    beta_all = jax.nn.sigmoid(raw)
    gates = chunk_gates(cum, heads)

    every = range(heads)
    betas = [beta_all[:, heads + h : heads + h + 1] for h in every]
    queries, keys, values = [], [], []
    for h in every:
        q = silu(conv[:, h * dk : (h + 1) * dk])
        k = silu(conv[:, (heads + h) * dk : (heads + h + 1) * dk])
        base = 2 * heads * dk + h * dv
        queries.append(q * unit_scale(q) * dk**-0.5)
        keys.append(k * unit_scale(k))
        values.append(silu(conv[:, base : base + dv]))
    keys16 = [k.astype(bf16) for k in keys]
    kk = [mm_nt(k, k) for k in keys16]
    qk = [mm_nt(q, k) for q, k in zip(queries, keys16)]
    strict = row > col
    systems = [jnp.where(strict, betas[h] * gates[h][0] * kk[h], 0.0) for h in every]
    inverses = lower_inverses(systems)
    solved = []
    for h in every:
        right = jnp.concatenate([betas[h] * values[h], (betas[h] * gates[h][1]) * keys[h]], axis=1)
        solved.append(mm(inverses[h], right))
    mixed = [mm(gates[h][0] * qk[h], solved[h]) for h in every]
    for h in every:
        before = state[h]
        before16 = before.astype(bf16)
        states[0, h] = before16
        w = solved[h][:, dv:].astype(bf16)
        q_now = (gates[h][1] * queries[h] - mixed[h][:, dv:]).astype(bf16)
        k_end = (gates[h][2] * keys[h]).astype(bf16)
        both = mm(jnp.concatenate([q_now, w], axis=0), before16)
        local[:, h * dv : (h + 1) * dv] = mixed[h][:, :dv] + both[:size, :dv]
        qa[:, h * dk : (h + 1) * dk] = both[:size, dv:].astype(bf16)
        fed = jnp.concatenate(
            [solved[h][:, :dv] - both[size:, :dv], -both[size:, dv:]], axis=1
        )
        after = gates[h][3] * before + mm_tn(k_end, fed)
        state[h] = after
        last[h] = after.astype(bf16)
        tinv[:, h * size : (h + 1) * size] = inverses[h].astype(bf16)
        uval[:, h * dv : (h + 1) * dv] = solved[h][:, :dv].astype(bf16)
        wkey[:, h * dk : (h + 1) * dk] = w
        qeff[:, h * dk : (h + 1) * dk] = q_now
        ktail[:, h * dk : (h + 1) * dk] = k_end


def vmem(limit=56):
    return pltpu.CompilerParams(vmem_limit_bytes=limit * MIB, dimension_semantics=("arbitrary",))


def whole(shape):
    return pl.BlockSpec(shape, lambda n: (0,) * len(shape))


def delta_forward(proj, flags, halo, taps, head, heads, dk, dv):
    rows = proj.shape[0]
    size = CHUNK
    steps = rows // size
    width = 2 * heads * dk + heads * dv
    ab_at = (width + heads * dv) // LANES

    def rowwise(cols):
        return pl.BlockSpec((size, cols), lambda n: (n, 0))

    outs = [
        ((rows, width), f32, rowwise(width)),
        ((rows, heads * dv), f32, rowwise(heads * dv)),
        ((rows, heads * dk), bf16, rowwise(heads * dk)),
        ((steps, heads, dk, dv + dk), bf16, pl.BlockSpec((1, heads, dk, dv + dk), lambda n: (n, 0, 0, 0))),
        ((rows, heads * size), bf16, rowwise(heads * size)),
        ((rows, heads * dv), bf16, rowwise(heads * dv)),
        ((rows, heads * dk), bf16, rowwise(heads * dk)),
        ((rows, heads * dk), bf16, rowwise(heads * dk)),
        ((rows, heads * dk), bf16, rowwise(heads * dk)),
        ((rows, LANES), f32, rowwise(LANES)),
        ((heads, dk, dv + dk), bf16, whole((heads, dk, dv + dk))),
    ]
    return pl.pallas_call(
        functools.partial(forward_kernel, heads, dk, dv),
        grid=(steps,),
        in_specs=[
            rowwise(width),
            pl.BlockSpec((size, LANES), lambda n: (n, ab_at)),
            rowwise(LANES),
            whole((8, width)),
            whole((8, width)),
            whole((8, LANES)),
        ],
        out_specs=[spec for _, _, spec in outs],
        out_shape=[jax.ShapeDtypeStruct(shape, kind) for shape, kind, _ in outs],
        scratch_shapes=[
            pltpu.VMEM((size + 8, width), f32),
            pltpu.VMEM((heads, dk, dv + dk), f32),
        ],
        compiler_params=vmem(),
        cost_estimate=pl.CostEstimate(
            flops=rows * heads * 2 * (16 * size * size + 8 * dk * (dv + dk)),
            bytes_accessed=rows * width * 14,
            transcendentals=rows * width * 2,
        ),
    )(proj, proj, flags, halo, taps, head)


def mix_kernel(heads, dk, dv, local, qa, entering, zgate, gain, wout, y_out, part_out):
    for h in range(heads):
        at = slice(h * dv, (h + 1) * dv)
        o = local[:, at] + mm(qa[:, h * dk : (h + 1) * dk], entering[h])
        so = lax.rsqrt(jnp.mean(o * o, axis=-1, keepdims=True) + EPS)
        y_out[:, at] = (o * so * gain[0:1, :] * silu(zgate[:, at])).astype(bf16)
    part_out[...] = mm(y_out[...], wout[...]).astype(part_out.dtype)


def delta_mix(local, qa, entering, proj, gain, wout, heads, dk, dv):
    rows = local.shape[0]
    size = 2 * CHUNK
    model = wout.shape[1]
    z_at = (2 * heads * dk + heads * dv) // (heads * dv)

    def rowwise(cols, at=0):
        return pl.BlockSpec((size, cols), lambda n: (n, at))

    return pl.pallas_call(
        functools.partial(mix_kernel, heads, dk, dv),
        grid=(rows // size,),
        in_specs=[
            rowwise(heads * dv),
            rowwise(heads * dk),
            whole((heads, dk, dv)),
            rowwise(heads * dv, z_at),
            whole((8, dv)),
            whole(wout.shape),
        ],
        out_specs=[rowwise(heads * dv), rowwise(model)],
        out_shape=[
            jax.ShapeDtypeStruct((rows, heads * dv), bf16),
            jax.ShapeDtypeStruct((rows, model), bf16),
        ],
        compiler_params=vmem(),
        cost_estimate=pl.CostEstimate(
            flops=2 * rows * heads * dv * (model + dk),
            bytes_accessed=rows * heads * dv * 14,
            transcendentals=rows * heads * dv,
        ),
    )(local, qa, entering, proj, gain, wout)


def back_kernel(
    heads, dk, dv,
    er, local, qa, entering, zgate, gain, wout, qeff, wkey, ktail, cum,
    dz_out, do_out, gain_out, first, state, gain_sum,
):
    step = pl.program_id(0)
    size = er.shape[0]

    @pl.when(step == 0)
    def _():
        state[...] = jnp.zeros_like(state)
        gain_sum[...] = jnp.zeros_like(gain_sum)

    dy = mm_nt(er[...], wout[...])
    ends = cum[size - 1 : size, :]
    for h in range(heads):
        at = slice(h * dv, (h + 1) * dv)
        kat = slice(h * dk, (h + 1) * dk)
        z = zgate[:, at]
        sig = jax.nn.sigmoid(z)
        act = z * sig
        o = local[:, at] + mm(qa[:, kat], entering[h])
        so = lax.rsqrt(jnp.mean(o * o, axis=-1, keepdims=True) + EPS)
        normed = o * so
        g = dy[:, at]
        scaled = gain[0:1, :] * g
        gain_sum[0:1, :] += jnp.sum(g * normed * act, axis=0, keepdims=True)
        dz_out[:, at] = (scaled * normed * (sig * (1.0 + z * (1.0 - sig)))).astype(bf16)
        back = scaled * act
        dots = jnp.mean(back * o, axis=-1, keepdims=True)
        do = (so * back - o * (so * so * so * dots)).astype(bf16)
        do_out[:, at] = do
        after = state[h]
        kept = jnp.where(ends[:, START : START + 1] == 0.0, jnp.exp(ends[:, h : h + 1]), 0.0)
        pulled = mm(ktail[:, kat], after)
        now = kept * after + mm_tn(
            jnp.concatenate([qeff[:, kat], wkey[:, kat]], axis=0),
            jnp.concatenate([do, (-pulled).astype(bf16)], axis=0),
        )
        state[h] = now
        first[h] = now.astype(bf16)
    gain_out[...] = gain_sum[...]


def delta_back(er, local, qa, entering, proj, gain, wout, qeff, wkey, ktail, cum, heads, dk, dv):
    rows, model = er.shape
    size = CHUNK
    steps = rows // size
    z_at = (2 * heads * dk + heads * dv) // (heads * dv)

    def rowwise(cols, at=0):
        return pl.BlockSpec((size, cols), lambda n: (steps - 1 - n, at))

    outs = [
        ((rows, heads * dv), bf16, rowwise(heads * dv)),
        ((rows, heads * dv), bf16, rowwise(heads * dv)),
        ((8, dv), f32, whole((8, dv))),
        ((heads, dk, dv), bf16, whole((heads, dk, dv))),
    ]
    return pl.pallas_call(
        functools.partial(back_kernel, heads, dk, dv),
        grid=(steps,),
        in_specs=[
            rowwise(model),
            rowwise(heads * dv),
            rowwise(heads * dk),
            whole((heads, dk, dv)),
            rowwise(heads * dv, z_at),
            whole((8, dv)),
            whole(wout.shape),
            rowwise(heads * dk),
            rowwise(heads * dk),
            rowwise(heads * dk),
            rowwise(LANES),
        ],
        out_specs=[spec for _, _, spec in outs],
        out_shape=[jax.ShapeDtypeStruct(shape, kind) for shape, kind, _ in outs],
        scratch_shapes=[pltpu.VMEM((heads, dk, dv), f32), pltpu.VMEM((8, dv), f32)],
        compiler_params=vmem(),
        cost_estimate=pl.CostEstimate(
            flops=2 * rows * heads * dv * (model + 4 * dk),
            bytes_accessed=rows * heads * dv * 18,
            transcendentals=rows * heads * dv,
        ),
    )(er, local, qa, entering, proj, gain, wout, qeff, wkey, ktail, cum)


def grad_kernel(
    heads, dk, dv,
    proj, conv, ab, flags, cum_in, halo, taps, head, do_in, tinv, uval, wkey, states, entering, leaving,
    dproj, dab, tail_rows, head_rows, dtaps, dhead,
    state, ext, tap_sum, head_sum,
):
    step = pl.program_id(0)
    steps = pl.num_programs(0)
    size = proj.shape[0]
    width = proj.shape[1]
    every = range(heads)

    @pl.when(step == 0)
    def _():
        state[...] = leaving[...].astype(f32)
        ext[size : size + 8, :] = jnp.zeros((8, width), f32)
        tap_sum[...] = jnp.zeros_like(tap_sum)
        head_sum[...] = jnp.zeros_like(head_sum)

    @pl.when(step > 0)
    def _():
        ext[size : size + 8, :] = ext[0:8, :]

    fl = flags[...]
    raw = ab[...]
    beta_all = jax.nn.sigmoid(raw)
    cum = cum_in[...]
    gates = chunk_gates(cum, heads)
    row, col = grid_of(size, size)
    strict = row > col
    betas = [beta_all[:, heads + h : heads + h + 1] for h in every]

    cq = [conv[:, h * dk : (h + 1) * dk] for h in every]
    ck = [conv[:, (heads + h) * dk : (heads + h + 1) * dk] for h in every]
    vbase = 2 * heads * dk
    sq = [silu(c) for c in cq]
    sk = [silu(c) for c in ck]
    rq = [unit_scale(s) for s in sq]
    rk = [unit_scale(s) for s in sk]
    queries = [s * r * dk**-0.5 for s, r in zip(sq, rq)]
    keys = [s * r for s, r in zip(sk, rk)]
    q16 = [q.astype(bf16) for q in queries]
    k16 = [k.astype(bf16) for k in keys]
    kk = [mm_nt(k, k) for k in k16]
    qk = [mm_nt(q, k) for q, k in zip(q16, k16)]
    attend = [gates[h][0] * qk[h] for h in every]
    weak = [jnp.where(strict, gates[h][0] * kk[h], 0.0) for h in every]

    dsum_row = jnp.zeros((LANES, size), f32)
    dsum_col = jnp.zeros((size, LANES), f32)
    end_add = jnp.zeros((1, LANES), f32)
    dbeta_all = jnp.zeros((size, LANES), f32)
    lane = lax.broadcasted_iota(jnp.int32, (size, LANES), 1)
    lane_row = lax.broadcasted_iota(jnp.int32, (1, LANES), 1)
    sub = lax.broadcasted_iota(jnp.int32, (LANES, size), 0)

    starts, users, dos, dstates, dks16 = [], [], [], [], []
    for h in every:
        entry16 = entering[h]
        start = states[0, h, :, 0:dv].astype(f32) + mm(states[0, h, :, dv : dv + dk], entry16)
        start16 = start.astype(bf16)
        both = mm(jnp.concatenate([wkey[:, h * dk : (h + 1) * dk], k16[h]], axis=0), start16)
        starts.append((start, start16, both[size:]))
        users.append((uval[:, h * dv : (h + 1) * dv].astype(f32) - both[:size]).astype(bf16))
        dos.append(do_in[:, h * dv : (h + 1) * dv])
        dstates.append(state[h])
    d16 = [d.astype(bf16) for d in dstates]
    du = [
        mm_tn(attend[h], dos[h]) + mm(gates[h][2] * keys[h], d16[h]) for h in every
    ]
    dright = [mm_tn(tinv[:, h * size : (h + 1) * size], du[h]) for h in every]
    for h in every:
        decay, entry, tail, kept = gates[h]
        beta = betas[h]
        start, start16, recalled = starts[h]
        dr = dright[h]
        pair = jnp.concatenate([dos[h], dr.astype(bf16)], axis=0)
        wide = mm_nt(pair, jnp.concatenate([users[h], start16], axis=0))
        dattend = wide[:size, :size]
        dqe = wide[:size, size:]
        dlow = -wide[size:, :size]
        dke = -beta * wide[size:, size:]
        user_end = mm_nt(users[h], d16[h])
        state[h] = kept * dstates[h] + mm_tn(
            jnp.concatenate([entry * queries[h], -(beta * entry) * keys[h]], axis=0), pair
        )
        dqk = dattend * decay
        dkk = jnp.where(strict, dlow * decay, 0.0) * beta
        stack = jnp.concatenate([dqk, dkk], axis=0).astype(bf16)
        ahead = mm(stack, k16[h])
        behind = mm_tn(stack, jnp.concatenate([q16[h], k16[h]], axis=0))
        dq = ahead[:size] + entry * dqe
        dk_ = ahead[size:] + behind + entry * dke + tail * user_end
        base = vbase + h * dv
        cv = conv[:, base : base + dv]
        sigv = jax.nn.sigmoid(cv)
        value = cv * sigv
        ext[0:size, base : base + dv] = (beta * dr) * (sigv * (1.0 + cv * (1.0 - sigv)))
        dbeta = jnp.sum(dr * (value - entry * recalled), axis=-1, keepdims=True) + jnp.sum(
            dlow * weak[h], axis=-1, keepdims=True
        )
        lowmask = dlow * weak[h] * beta
        paired = dattend * attend[h] + lowmask
        dentry = jnp.sum(dqe * queries[h] + dke * keys[h], axis=-1, keepdims=True)
        dtail = jnp.sum(user_end * keys[h], axis=-1, keepdims=True) * tail
        dkept = jnp.sum(
            jnp.sum(start * dstates[h], axis=1, keepdims=True), axis=0, keepdims=True
        )
        col_add = jnp.sum(paired, axis=-1, keepdims=True) + dentry * entry - dtail
        dsum_col = jnp.where(lane == h, col_add, dsum_col)
        dsum_row = jnp.where(sub == h, jnp.sum(paired, axis=0, keepdims=True), dsum_row)
        end_add = jnp.where(
            lane_row == h, jnp.sum(dtail, axis=0, keepdims=True) + dkept * kept, end_add
        )
        dbeta_all = jnp.where(lane == heads + h, dbeta, dbeta_all)
        inner = jnp.sum(dq * sq[h], axis=-1, keepdims=True)
        scale = dk**-0.5 * rq[h]
        ds = scale * dq - sq[h] * (scale * rq[h] * rq[h] * inner)
        ext[0:size, h * dk : (h + 1) * dk] = ds * silu_grad(cq[h])
        inner = jnp.sum(dk_ * sk[h], axis=-1, keepdims=True)
        ds = rk[h] * dk_ - sk[h] * (rk[h] * rk[h] * rk[h] * inner)
        ext[0:size, (heads + h) * dk : (heads + h + 1) * dk] = ds * silu_grad(ck[h])

    dcum = dsum_col - jnp.transpose(dsum_row)
    final = lax.broadcasted_iota(jnp.int32, (size, LANES), 0) == size - 1
    dcum = dcum + jnp.where(final, end_add, 0.0)
    dlog = mm_hi((row <= col).astype(f32), dcum) * (1.0 - fl[:, START : START + 1])
    rate = jnp.exp(head[0:1, :])
    shifted = raw + head[1:2, :]
    dap = dlog * (-rate) * jax.nn.sigmoid(shifted)
    dbp = dbeta_all * beta_all * (1.0 - beta_all)
    dab[...] = jnp.where(lane < heads, dap, jnp.where(lane < 2 * heads, dbp, 0.0)).astype(bf16)
    head_sum[0:1, :] += jnp.sum(dlog * (-rate) * softplus(shifted), axis=0, keepdims=True)
    head_sum[1:2, :] += jnp.sum(dap, axis=0, keepdims=True)
    dhead[...] = head_sum[...]

    later = [jnp.broadcast_to(fl[:, AHEAD + s : AHEAD + s + 1], (size, LANES)) for s in (1, 2, 3)]
    for lo in range(0, width, LANES):
        at = slice(lo, lo + LANES)
        here = proj[:, at]
        own = ext[0:size, at]
        total = own * taps[3:4, at]
        tap_sum[3:4, at] += jnp.sum(own * here, axis=0, keepdims=True)
        for s in (1, 2, 3):
            moved = ext[s : s + size, at] * later[s - 1]
            total += moved * taps[3 - s : 4 - s, at]
            tap_sum[3 - s : 4 - s, at] += jnp.sum(moved * here, axis=0, keepdims=True)
        dproj[:, at] = total.astype(bf16)

        @pl.when(step == 0)
        def _():
            tail_rows[:, at] = total[size - 8 : size, :]

    @pl.when(step == steps - 1)
    def _():
        head_rows[...] = ext[0:8, :]
        sub8 = lax.broadcasted_iota(jnp.int32, (8, width), 0)
        for s in (1, 2, 3):
            ok = (sub8 < s).astype(f32) * fl[0:8, VALID + s : VALID + s + 1]
            before = pltpu.roll(halo[...], s, 0)
            tap_sum[3 - s : 4 - s, :] += jnp.sum(
                ext[0:8, :] * before * ok, axis=0, keepdims=True
            )

    dtaps[...] = tap_sum[...]


def delta_grad(
    proj, conv, flags, cum, halo, taps, head, do, tinv, uval, wkey, states, entering, leaving,
    heads, dk, dv,
):
    rows = proj.shape[0]
    size = CHUNK
    steps = rows // size
    width = 2 * heads * dk + heads * dv
    ab_at = (width + heads * dv) // LANES

    def rowwise(cols, at=0):
        return pl.BlockSpec((size, cols), lambda n: (steps - 1 - n, at))

    outs = [
        ((rows, width), bf16, rowwise(width)),
        ((rows, LANES), bf16, rowwise(LANES)),
        ((8, width), f32, whole((8, width))),
        ((8, width), f32, whole((8, width))),
        ((8, width), f32, whole((8, width))),
        ((8, LANES), f32, whole((8, LANES))),
    ]
    return pl.pallas_call(
        functools.partial(grad_kernel, heads, dk, dv),
        grid=(steps,),
        in_specs=[
            rowwise(width),
            rowwise(width),
            rowwise(LANES, ab_at),
            rowwise(LANES),
            rowwise(LANES),
            whole((8, width)),
            whole((8, width)),
            whole((8, LANES)),
            rowwise(heads * dv),
            rowwise(heads * size),
            rowwise(heads * dv),
            rowwise(heads * dk),
            pl.BlockSpec((1, heads, dk, dv + dk), lambda n: (steps - 1 - n, 0, 0, 0)),
            whole((heads, dk, dv)),
            whole((heads, dk, dv)),
        ],
        out_specs=[spec for _, _, spec in outs],
        out_shape=[jax.ShapeDtypeStruct(shape, kind) for shape, kind, _ in outs],
        scratch_shapes=[
            pltpu.VMEM((heads, dk, dv), f32),
            pltpu.VMEM((size + 8, width), f32),
            pltpu.VMEM((8, width), f32),
            pltpu.VMEM((8, LANES), f32),
        ],
        compiler_params=vmem(),
        cost_estimate=pl.CostEstimate(
            flops=rows * heads * 2 * (10 * size * dv + 8 * dk * dv),
            bytes_accessed=rows * width * 16,
            transcendentals=rows * width * 2,
        ),
    )(
        proj, conv, proj, flags, cum, halo, taps, head, do, tinv, uval, wkey, states, entering,
        leaving,
    )


def shifted(value, axis, distance):
    count = lax.axis_size(axis)
    route = [(i, i + distance) for i in range(count) if 0 <= i + distance < count]
    return lax.ppermute(value, axis, route)


def heads_mm(a, b):
    return jnp.einsum("hij,hjk->hik", a, b, preferred_element_type=f32)


def heads_mm_tn(a, b):
    return jnp.einsum("hji,hjk->hik", a, b, preferred_element_type=f32)


def entering_state(own, dv, reach):
    runs = []
    run = own
    distance = 1
    while distance < reach:
        runs.append(run[:, :, dv:])
        before = shifted(run, "ctx", distance)
        joined = heads_mm(run[:, :, dv:], before)
        run = jnp.concatenate(
            [run[:, :, :dv].astype(f32) + joined[:, :, :dv], joined[:, :, dv:]], axis=-1
        ).astype(bf16)
        distance *= 2
    entering = shifted(run[:, :, :dv], "ctx", 1)
    ahead = [part if j == 0 else shifted(part, "ctx", 1 - 2**j) for j, part in enumerate(runs)]
    return entering, ahead


def leaving_grad(own, ahead):
    run = own
    for j, maps in enumerate(ahead):
        later = shifted(run, "ctx", -(2**j))
        run = (run.astype(f32) + heads_mm_tn(maps, later)).astype(bf16)
    return shifted(run, "ctx", -1)


def summed_over_tp(part):
    count = lax.axis_size("tp")
    total = part.astype(f32)
    for d in range(1, count):
        route = [(i, (i + d) % count) for i in range(count)]
        total = total + lax.ppermute(part, "tp", route).astype(f32)
    return total


def reduced(grad):
    part = lax.psum_scatter(grad, "fs", scatter_dimension=0, tiled=True)
    part = lax.psum_scatter(part, "ctx", scatter_dimension=0, tiled=True)
    return lax.all_gather(part, "ctx", axis=0, tiled=True).astype(f32)


def per_device(
    tokens, cotangent, lengths, order, mixer_gain, w_query, w_key, w_value, w_outgate, w_decay,
    w_beta, conv_query, conv_key, conv_value, decay_log, decay_bias, out_gain, w_output, mlp_gain,
    w_gate, w_up, w_down,
):
    rows, model = tokens.shape[1:]
    ctx = lax.axis_size("ctx")
    fs = lax.axis_size("fs")
    me = lax.axis_index("ctx")
    heads = decay_log.shape[0]
    dk = w_query.shape[1] // heads
    dv = w_value.shape[1] // heads
    key_cols, value_cols = heads * dk, heads * dv
    width = 2 * key_cols + value_cols
    hidden_cols = w_gate.shape[1]
    total = order.shape[1]
    peer = rows // ctx
    halo_rows = TAPS - 1
    sequences = lengths.shape[1]
    longest = 2 * total // (sequences + 1)
    reach = min(ctx - 1, -(-longest // rows))

    order_row = order[0]
    source_all = order_row // rows
    mine = (source_all == me).reshape(ctx, rows)
    upto = (jnp.arange(rows)[:, None] <= jnp.arange(rows)[None, :]).astype(bf16)
    rank_all = jnp.dot(mine.astype(bf16), upto, preferred_element_type=f32).astype(jnp.int32) - 1
    slots = jnp.arange(peer, dtype=jnp.int32)
    picked = mine[:, None, :] & (rank_all[:, None, :] == slots[None, :, None])
    local_all = (order_row - me * rows).reshape(ctx, 1, rows)
    send_order = jnp.sum(jnp.where(picked, local_all, 0), axis=2).reshape(rows)
    given = lax.dynamic_slice_in_dim(order_row, me * rows, rows)
    source = given // rows
    from_each = source[None, :] == jnp.arange(ctx, dtype=jnp.int32)[:, None]
    rank_here = jnp.dot(from_each.astype(bf16), upto, preferred_element_type=f32) - 1.0
    rank_here = jnp.sum(jnp.where(from_each, rank_here, 0.0), axis=0).astype(jnp.int32)
    recv_slot = source * peer + rank_here
    iota = jnp.arange(rows, dtype=jnp.int32)
    gather_send = (send_order[:, None] == iota[None, :]).astype(bf16)
    gather_recv = (recv_slot[:, None] == iota[None, :]).astype(bf16)

    def moved(maps, values, transposed=False):
        return lax.dot_general(
            maps, values, (((0 if transposed else 1,), (0,)), ((), ())), preferred_element_type=f32
        ).astype(bf16)

    def to_packed(values):
        arrived = lax.all_to_all(
            moved(gather_send, values), "ctx", split_axis=0, concat_axis=0, tiled=True
        )
        return moved(gather_recv, arrived)

    def to_given(values):
        arrived = lax.all_to_all(
            moved(gather_recv, values, True), "ctx", split_axis=0, concat_axis=0, tiled=True
        )
        return moved(gather_send, arrived, True)

    resident = to_packed(tokens[0])
    e = to_packed(cotangent[0])

    offsets = jnp.cumsum(lengths[0]) - lengths[0]
    positions = me * rows - halo_rows + jnp.arange(rows + 2 * halo_rows, dtype=jnp.int32)
    number = jnp.sum((offsets[None, :] <= positions[:, None]).astype(jnp.int32), axis=1)
    here = number[halo_rows : halo_rows + rows]
    fresh = jnp.any(offsets[None, :] == positions[halo_rows : halo_rows + rows, None], axis=1)
    columns = [jnp.zeros((rows,), f32)] * START + [fresh.astype(f32)]
    for s in range(1, TAPS):
        columns.append((number[halo_rows - s : halo_rows - s + rows] == here).astype(f32))
    for s in range(1, TAPS):
        columns.append((number[halo_rows + s : halo_rows + s + rows] == here).astype(f32))
    flags = jnp.stack(columns, axis=1)
    flags = jnp.pad(flags, ((0, 0), (0, LANES - flags.shape[1])))

    pad = jnp.zeros((w_decay.shape[0], LANES - 2 * heads), bf16)
    w_in = jnp.concatenate([w_query, w_key, w_value, w_outgate, w_decay, w_beta, pad], axis=1)
    w_in = lax.all_gather(w_in, "fs", axis=0, tiled=True)
    w_wide = lax.all_gather(jnp.concatenate([w_gate, w_up], axis=1), "fs", axis=0, tiled=True)
    w_down = lax.all_gather(w_down, "fs", axis=0, tiled=True)
    w_output = lax.all_gather(w_output, "fs", axis=0, tiled=True)
    small = jnp.concatenate(
        [
            conv_query.T.reshape(-1),
            conv_key.T.reshape(-1),
            conv_value.T.reshape(-1),
            mixer_gain,
            mlp_gain,
            out_gain,
        ]
    )
    small = lax.all_gather(small, "fs", axis=0).astype(f32)
    pieces, at = [], 0
    for channels in (conv_query.shape[0], conv_key.shape[0], conv_value.shape[0]):
        part = small[:, at : at + TAPS * channels].reshape(fs, TAPS, channels)
        pieces.append(part.transpose(1, 0, 2).reshape(TAPS, fs * channels))
        at += TAPS * channels
    taps = jnp.pad(jnp.concatenate(pieces, axis=1), ((0, 8 - TAPS), (0, 0)))
    gains = []
    for size in (mixer_gain.shape[0], mlp_gain.shape[0], out_gain.shape[0]):
        gains.append(small[:, at : at + size].reshape(-1))
        at += size
    gain_one, gain_two, gain_out = gains
    gain_rows = jnp.broadcast_to(gain_out[None, :], (8, dv))
    head = jnp.pad(
        jnp.stack([decay_log, decay_bias]), ((0, 6), (0, LANES - heads))
    )

    x = resident.astype(f32)
    inv_one = lax.rsqrt(jnp.mean(x * x, axis=-1, keepdims=True) + EPS)
    n1 = (x * inv_one * gain_one).astype(bf16)
    proj = jnp.dot(n1, w_in, preferred_element_type=f32)
    halo = shifted(proj[rows - 8 :, :width], "ctx", 1)
    conv, local, qa, states, tinv, uval, wkey, qeff, ktail, cum, last = delta_forward(
        proj, flags, halo, taps, head, heads, dk, dv
    )
    entering, ahead = entering_state(last, dv, reach)
    y1, part = delta_mix(local, qa, entering, proj, gain_rows, w_output, heads, dk, dv)

    r = x + summed_over_tp(part)
    inv_two = lax.rsqrt(jnp.mean(r * r, axis=-1, keepdims=True) + EPS)
    n2 = (r * inv_two * gain_two).astype(bf16)
    wide = jnp.dot(n2, w_wide, preferred_element_type=f32)
    gp, up = wide[:, :hidden_cols], wide[:, hidden_cols:]
    act = silu(gp)
    hid = (act * up).astype(bf16)
    down = jnp.dot(hid, w_down, preferred_element_type=f32).astype(bf16)
    dhid = lax.dot_general(e, w_down, (((1,), (1,)), ((), ())), preferred_element_type=f32)
    dwide = jnp.concatenate(
        [(dhid * up * silu_grad(gp)).astype(bf16), (dhid * act).astype(bf16)], axis=1
    )
    dn2 = lax.dot_general(dwide, w_wide, (((1,), (1,)), ((), ())), preferred_element_type=f32)
    dn2 = summed_over_tp(dn2.astype(bf16))
    block_out = to_given((r + summed_over_tp(down)).astype(bf16))
    grad_mlp_gain = jnp.sum(dn2 * r * inv_two, axis=0)
    scaled = gain_two * dn2
    dr = (
        e.astype(f32)
        + inv_two * scaled
        - r * (inv_two * inv_two * inv_two * jnp.mean(scaled * r, axis=-1, keepdims=True))
    )
    er = dr.astype(bf16)

    dz, do, dgain_out, first = delta_back(
        er, local, qa, entering, proj, gain_rows, w_output, qeff, wkey, ktail, cum, heads, dk, dv
    )
    leaving = leaving_grad(first, ahead)
    dproj, dab, tail_rows, head_rows, dtaps, dhead = delta_grad(
        proj, conv, flags, cum, halo, taps, head, do, tinv, uval, wkey, states, entering, leaving,
        heads, dk, dv,
    )
    next_rows = shifted(head_rows, "ctx", -1)
    extra = jnp.zeros_like(tail_rows)
    for s in range(1, TAPS):
        part_s = jnp.concatenate([jnp.zeros((8 - s, width), f32), next_rows[:s]], axis=0)
        extra = extra + part_s * taps[TAPS - 1 - s] * flags[rows - 8 :, AHEAD + s][:, None]
    dproj = lax.dynamic_update_slice(dproj, (tail_rows + extra).astype(bf16), (rows - 8, 0))
    dall = jnp.concatenate([dproj, dz, dab], axis=1)
    dn1 = lax.dot_general(dall, w_in, (((1,), (1,)), ((), ())), preferred_element_type=f32)
    dn1 = summed_over_tp(dn1.astype(bf16))
    grad_mixer_gain = jnp.sum(dn1 * x * inv_one, axis=0)
    scaled = gain_one * dn1
    grad_in = (
        dr
        + inv_one * scaled
        - x * (inv_one * inv_one * inv_one * jnp.mean(scaled * x, axis=-1, keepdims=True))
    ).astype(bf16)
    grad_tokens = to_given(grad_in)

    def outer(a, b):
        return lax.dot_general(a, b, (((0,), (0,)), ((), ())), preferred_element_type=f32)

    def halves(grad):
        return grad.reshape(fs, grad.shape[0] // fs, *grad.shape[1:])

    g_wide = reduced(outer(n2, dwide).astype(bf16))
    g_rows = jnp.concatenate([halves(outer(hid, e)), halves(outer(y1, er))], axis=1)
    g_rows = reduced(g_rows.reshape(-1, model).astype(bf16))
    g_in = reduced(outer(n1, dall).astype(bf16))
    down_rows = hidden_cols // fs

    def tap_part(lo, channels):
        return dtaps[:TAPS, lo : lo + channels].reshape(TAPS, fs, -1).transpose(1, 0, 2).reshape(fs, -1)

    share = lax.psum(jnp.sum(dgain_out, axis=0).astype(bf16), "tp").astype(f32)
    rates = jnp.broadcast_to(dhead[:2, :heads].reshape(1, 2 * heads), (fs, 2 * heads))
    little = jnp.concatenate(
        [
            tap_part(0, key_cols),
            tap_part(key_cols, key_cols),
            tap_part(2 * key_cols, value_cols),
            halves(grad_mixer_gain),
            halves(grad_mlp_gain),
            halves(share),
            rates,
        ],
        axis=1,
    )
    little = lax.psum_scatter(little, "fs", scatter_dimension=0, tiled=True)
    little = lax.psum(little, "ctx")[0]
    taken, at = [], 0
    for channels in (conv_query.shape[0], conv_key.shape[0], conv_value.shape[0]):
        taken.append(little[at : at + TAPS * channels].reshape(TAPS, channels).T)
        at += TAPS * channels
    for size in (mixer_gain.shape[0], mlp_gain.shape[0], out_gain.shape[0], heads, heads):
        taken.append(little[at : at + size])
        at += size
    g_cq, g_ck, g_cv, g_mixer, g_mlp, g_out_gain, g_log, g_bias = taken
    ends = [key_cols, 2 * key_cols, width, width + value_cols, width + value_cols + heads]
    g_query, g_key, g_value, g_outgate, g_decay, g_beta = (
        g_in[:, lo:hi] for lo, hi in zip([0] + ends, ends + [ends[-1] + heads])
    )
    return (
        block_out[None],
        grad_tokens[None],
        g_mixer,
        g_query,
        g_key,
        g_value,
        g_outgate,
        g_decay,
        g_beta,
        g_cq,
        g_ck,
        g_cv,
        g_log,
        g_bias,
        g_out_gain,
        g_rows[down_rows:],
        g_mlp,
        g_wide[:, :hidden_cols],
        g_wide[:, hidden_cols:],
        g_rows[:down_rows],
    )


def solution(mesh):
    split = P("fs", "ctx", None)
    cols = P("fs", "tp")
    both = P(("tp", "fs"), None)
    in_specs = (
        split, split, P("fs", None), P("fs", None), P("fs"),
        cols, cols, cols, cols, cols, cols,
        both, both, both, P("tp"), P("tp"), P("fs"), both, P("fs"), cols, cols, both,
    )
    out_specs = (
        split, split, P("fs"),
        cols, cols, cols, cols, cols, cols,
        both, both, both, P("tp"), P("tp"), P("fs"), both, P("fs"), cols, cols, both,
    )
    return jax.shard_map(
        per_device, mesh=mesh, in_specs=in_specs, out_specs=out_specs, check_vma=False
    )
```

```python
import functools

import jax
import jax.numpy as jnp
from jax import lax
from jax.experimental import pallas as pl
from jax.experimental.pallas import tpu as pltpu
from jax.sharding import PartitionSpec as P

TAPS = 4
CHUNK = 128
EPS = 1e-6
LANES = 128
START, VALID, AHEAD = 8, 8, 11
HI = lax.Precision.HIGHEST
bf16 = jnp.bfloat16
f32 = jnp.float32
MIB = 1024 * 1024


def mm(a, b):
    return jnp.dot(a.astype(bf16), b.astype(bf16), preferred_element_type=f32)


def mm_nt(a, b):
    return lax.dot_general(
        a.astype(bf16), b.astype(bf16), (((1,), (1,)), ((), ())), preferred_element_type=f32
    )


def mm_tn(a, b):
    return lax.dot_general(
        a.astype(bf16), b.astype(bf16), (((0,), (0,)), ((), ())), preferred_element_type=f32
    )


def mm_hi(a, b):
    return jnp.dot(a, b, precision=HI, preferred_element_type=f32)


def silu(x):
    return x * jax.nn.sigmoid(x)


def silu_grad(x):
    s = jax.nn.sigmoid(x)
    return s * (1.0 + x * (1.0 - s))


def softplus(x):
    return jnp.maximum(x, 0.0) + jnp.log1p(jnp.exp(-jnp.abs(x)))


def grid_of(rows, cols):
    return (
        lax.broadcasted_iota(jnp.int32, (rows, cols), 0),
        lax.broadcasted_iota(jnp.int32, (rows, cols), 1),
    )


def lower_inverses(systems):
    size = systems[0].shape[0]
    row, col = grid_of(size, size)
    eye = (row == col).astype(f32)
    first = ((row >> 1) == (col >> 1)) & (row > col)
    inverses = [eye - jnp.where(first, low, 0.0) for low in systems]
    level = 1
    while (1 << level) < size:
        block = (
            ((row >> (level + 1)) == (col >> (level + 1)))
            & (((row >> level) & 1) == 1)
            & (((col >> level) & 1) == 0)
        )
        parts = [mm(jnp.where(block, low, 0.0), inv) for low, inv in zip(systems, inverses)]
        inverses = [inv - mm(inv, part) for inv, part in zip(inverses, parts)]
        level += 1
    return inverses


def chunk_gates(cum, heads):
    size = cum.shape[0]
    row, col = grid_of(size, size)
    across = jnp.transpose(cum)
    seg_col = cum[:, START : START + 1]
    linked = (row >= col) & (seg_col == across[START : START + 1, :])
    from_start = seg_col == 0.0
    to_end = seg_col == cum[size - 1 : size, START : START + 1]
    out = []
    for h in range(heads):
        down = cum[:, h : h + 1]
        gap = jnp.where(linked, down - across[h : h + 1, :], 0.0)
        decay = jnp.where(linked, jnp.exp(gap), 0.0)
        entry = jnp.where(from_start, jnp.exp(down), 0.0)
        last = cum[size - 1 : size, h : h + 1]
        tail = jnp.where(to_end, jnp.exp(jnp.where(to_end, last - down, 0.0)), 0.0)
        out.append((decay, entry, tail, entry[size - 1 : size, :]))
    return out


def unit_scale(x):
    return lax.rsqrt(jnp.sum(x * x, axis=-1, keepdims=True) + EPS)


def forward_kernel(
    heads, dk, dv,
    proj, ab, flags, halo, taps, head,
    conv, local, qa, states, tinv, uval, wkey, qeff, ktail, cum_out, last,
    ext, state,
):
    step = pl.program_id(0)
    size = proj.shape[0]
    width = proj.shape[1]

    @pl.when(step == 0)
    def _():
        ext[0:8, :] = halo[...]
        row, col = grid_of(dk, dk)
        for h in range(heads):
            state[h, :, 0:dv] = jnp.zeros((dk, dv), f32)
            state[h, :, dv : dv + dk] = (row == col).astype(f32)

    @pl.when(step > 0)
    def _():
        ext[0:8, :] = ext[size : size + 8, :]

    ext[8 : 8 + size, :] = proj[...]
    fl = flags[...]
    valid = [jnp.broadcast_to(fl[:, VALID + s : VALID + s + 1], (size, LANES)) for s in (1, 2, 3)]
    for lo in range(0, width, LANES):
        at = slice(lo, lo + LANES)
        total = ext[8 : 8 + size, at] * taps[3:4, at]
        for s in (1, 2, 3):
            total += ext[8 - s : 8 - s + size, at] * taps[3 - s : 4 - s, at] * valid[s - 1]
        conv[:, at] = total

    raw = ab[...]
    lane = lax.broadcasted_iota(jnp.int32, (size, LANES), 1)
    log_decay = -jnp.exp(head[0:1, :]) * softplus(raw + head[1:2, :])
    row, col = grid_of(size, size)
    cum = mm_hi((row >= col).astype(f32), jnp.where(lane < heads, log_decay, fl))
    cum_out[...] = cum
    beta_all = jax.nn.sigmoid(raw)
    gates = chunk_gates(cum, heads)

    every = range(heads)
    betas = [beta_all[:, heads + h : heads + h + 1] for h in every]
    queries, keys, values = [], [], []
    for h in every:
        q = silu(conv[:, h * dk : (h + 1) * dk])
        k = silu(conv[:, (heads + h) * dk : (heads + h + 1) * dk])
        base = 2 * heads * dk + h * dv
        queries.append(q * unit_scale(q) * dk**-0.5)
        keys.append(k * unit_scale(k))
        values.append(silu(conv[:, base : base + dv]))
    keys16 = [k.astype(bf16) for k in keys]
    kk = [mm_nt(k, k) for k in keys16]
    qk = [mm_nt(q, k) for q, k in zip(queries, keys16)]
    strict = row > col
    systems = [jnp.where(strict, betas[h] * gates[h][0] * kk[h], 0.0) for h in every]
    inverses = lower_inverses(systems)
    solved = []
    for h in every:
        right = jnp.concatenate([betas[h] * values[h], (betas[h] * gates[h][1]) * keys[h]], axis=1)
        solved.append(mm(inverses[h], right))
    mixed = [mm(gates[h][0] * qk[h], solved[h]) for h in every]
    for h in every:
        before = state[h]
        before16 = before.astype(bf16)
        states[0, h] = before16
        w = solved[h][:, dv:].astype(bf16)
        q_now = (gates[h][1] * queries[h] - mixed[h][:, dv:]).astype(bf16)
        k_end = (gates[h][2] * keys[h]).astype(bf16)
        both = mm(jnp.concatenate([q_now, w], axis=0), before16)
        local[:, h * dv : (h + 1) * dv] = mixed[h][:, :dv] + both[:size, :dv]
        qa[:, h * dk : (h + 1) * dk] = both[:size, dv:].astype(bf16)
        fed = jnp.concatenate(
            [solved[h][:, :dv] - both[size:, :dv], -both[size:, dv:]], axis=1
        )
        after = gates[h][3] * before + mm_tn(k_end, fed)
        state[h] = after
        last[h] = after.astype(bf16)
        tinv[:, h * size : (h + 1) * size] = inverses[h].astype(bf16)
        uval[:, h * dv : (h + 1) * dv] = solved[h][:, :dv].astype(bf16)
        wkey[:, h * dk : (h + 1) * dk] = w
        qeff[:, h * dk : (h + 1) * dk] = q_now
        ktail[:, h * dk : (h + 1) * dk] = k_end


def vmem(limit=56):
    return pltpu.CompilerParams(vmem_limit_bytes=limit * MIB, dimension_semantics=("arbitrary",))


def whole(shape):
    return pl.BlockSpec(shape, lambda n: (0,) * len(shape))


def delta_forward(proj, flags, halo, taps, head, heads, dk, dv):
    rows = proj.shape[0]
    size = CHUNK
    steps = rows // size
    width = 2 * heads * dk + heads * dv
    ab_at = (width + heads * dv) // LANES

    def rowwise(cols):
        return pl.BlockSpec((size, cols), lambda n: (n, 0))

    outs = [
        ((rows, width), f32, rowwise(width)),
        ((rows, heads * dv), f32, rowwise(heads * dv)),
        ((rows, heads * dk), bf16, rowwise(heads * dk)),
        ((steps, heads, dk, dv + dk), bf16, pl.BlockSpec((1, heads, dk, dv + dk), lambda n: (n, 0, 0, 0))),
        ((rows, heads * size), bf16, rowwise(heads * size)),
        ((rows, heads * dv), bf16, rowwise(heads * dv)),
        ((rows, heads * dk), bf16, rowwise(heads * dk)),
        ((rows, heads * dk), bf16, rowwise(heads * dk)),
        ((rows, heads * dk), bf16, rowwise(heads * dk)),
        ((rows, LANES), f32, rowwise(LANES)),
        ((heads, dk, dv + dk), bf16, whole((heads, dk, dv + dk))),
    ]
    return pl.pallas_call(
        functools.partial(forward_kernel, heads, dk, dv),
        grid=(steps,),
        in_specs=[
            rowwise(width),
            pl.BlockSpec((size, LANES), lambda n: (n, ab_at)),
            rowwise(LANES),
            whole((8, width)),
            whole((8, width)),
            whole((8, LANES)),
        ],
        out_specs=[spec for _, _, spec in outs],
        out_shape=[jax.ShapeDtypeStruct(shape, kind) for shape, kind, _ in outs],
        scratch_shapes=[
            pltpu.VMEM((size + 8, width), f32),
            pltpu.VMEM((heads, dk, dv + dk), f32),
        ],
        compiler_params=vmem(),
        cost_estimate=pl.CostEstimate(
            flops=rows * heads * 40 * size * (dv + dk + size + size),
            bytes_accessed=rows * width * 14,
            transcendentals=rows * width * 2,
        ),
    )(proj, proj, flags, halo, taps, head)


def mix_kernel(heads, dk, dv, local, qa, entering, zgate, gain, wout, y_out, part_out):
    for h in range(heads):
        at = slice(h * dv, (h + 1) * dv)
        o = local[:, at] + mm(qa[:, h * dk : (h + 1) * dk], entering[h])
        so = lax.rsqrt(jnp.mean(o * o, axis=-1, keepdims=True) + EPS)
        y_out[:, at] = (o * so * gain[0:1, :] * silu(zgate[:, at])).astype(bf16)
    part_out[...] = mm(y_out[...], wout[...]).astype(part_out.dtype)


def delta_mix(local, qa, entering, proj, gain, wout, heads, dk, dv):
    rows = local.shape[0]
    size = 2 * CHUNK
    model = wout.shape[1]
    z_at = (2 * heads * dk + heads * dv) // (heads * dv)

    def rowwise(cols, at=0):
        return pl.BlockSpec((size, cols), lambda n: (n, at))

    return pl.pallas_call(
        functools.partial(mix_kernel, heads, dk, dv),
        grid=(rows // size,),
        in_specs=[
            rowwise(heads * dv),
            rowwise(heads * dk),
            whole((heads, dk, dv)),
            rowwise(heads * dv, z_at),
            whole((8, dv)),
            whole(wout.shape),
        ],
        out_specs=[rowwise(heads * dv), rowwise(model)],
        out_shape=[
            jax.ShapeDtypeStruct((rows, heads * dv), bf16),
            jax.ShapeDtypeStruct((rows, model), bf16),
        ],
        compiler_params=vmem(),
        cost_estimate=pl.CostEstimate(
            flops=10 * rows * heads * dv * model,
            bytes_accessed=rows * heads * dv * 14,
            transcendentals=rows * heads * dv,
        ),
    )(local, qa, entering, proj, gain, wout)


def back_kernel(
    heads, dk, dv,
    er, local, qa, entering, zgate, gain, wout, qeff, wkey, ktail, cum,
    dz_out, do_out, gain_out, first, state, gain_sum,
):
    step = pl.program_id(0)
    size = er.shape[0]

    @pl.when(step == 0)
    def _():
        state[...] = jnp.zeros_like(state)
        gain_sum[...] = jnp.zeros_like(gain_sum)

    dy = mm_nt(er[...], wout[...])
    ends = cum[size - 1 : size, :]
    for h in range(heads):
        at = slice(h * dv, (h + 1) * dv)
        kat = slice(h * dk, (h + 1) * dk)
        z = zgate[:, at]
        sig = jax.nn.sigmoid(z)
        act = z * sig
        o = local[:, at] + mm(qa[:, kat], entering[h])
        so = lax.rsqrt(jnp.mean(o * o, axis=-1, keepdims=True) + EPS)
        normed = o * so
        g = dy[:, at]
        scaled = gain[0:1, :] * g
        gain_sum[0:1, :] += jnp.sum(g * normed * act, axis=0, keepdims=True)
        dz_out[:, at] = (scaled * normed * (sig * (1.0 + z * (1.0 - sig)))).astype(bf16)
        back = scaled * act
        dots = jnp.mean(back * o, axis=-1, keepdims=True)
        do = (so * back - o * (so * so * so * dots)).astype(bf16)
        do_out[:, at] = do
        after = state[h]
        kept = jnp.where(ends[:, START : START + 1] == 0.0, jnp.exp(ends[:, h : h + 1]), 0.0)
        pulled = mm(ktail[:, kat], after)
        now = kept * after + mm_tn(
            jnp.concatenate([qeff[:, kat], wkey[:, kat]], axis=0),
            jnp.concatenate([do, (-pulled).astype(bf16)], axis=0),
        )
        state[h] = now
        first[h] = now.astype(bf16)
    gain_out[...] = gain_sum[...]


def delta_back(er, local, qa, entering, proj, gain, wout, qeff, wkey, ktail, cum, heads, dk, dv):
    rows, model = er.shape
    size = CHUNK
    steps = rows // size
    z_at = (2 * heads * dk + heads * dv) // (heads * dv)

    def rowwise(cols, at=0):
        return pl.BlockSpec((size, cols), lambda n: (steps - 1 - n, at))

    outs = [
        ((rows, heads * dv), bf16, rowwise(heads * dv)),
        ((rows, heads * dv), bf16, rowwise(heads * dv)),
        ((8, dv), f32, whole((8, dv))),
        ((heads, dk, dv), bf16, whole((heads, dk, dv))),
    ]
    return pl.pallas_call(
        functools.partial(back_kernel, heads, dk, dv),
        grid=(steps,),
        in_specs=[
            rowwise(model),
            rowwise(heads * dv),
            rowwise(heads * dk),
            whole((heads, dk, dv)),
            rowwise(heads * dv, z_at),
            whole((8, dv)),
            whole(wout.shape),
            rowwise(heads * dk),
            rowwise(heads * dk),
            rowwise(heads * dk),
            rowwise(LANES),
        ],
        out_specs=[spec for _, _, spec in outs],
        out_shape=[jax.ShapeDtypeStruct(shape, kind) for shape, kind, _ in outs],
        scratch_shapes=[pltpu.VMEM((heads, dk, dv), f32), pltpu.VMEM((8, dv), f32)],
        compiler_params=vmem(),
        cost_estimate=pl.CostEstimate(
            flops=20 * rows * heads * dv * model,
            bytes_accessed=rows * heads * dv * 18,
            transcendentals=rows * heads * dv,
        ),
    )(er, local, qa, entering, proj, gain, wout, qeff, wkey, ktail, cum)


def grad_kernel(
    heads, dk, dv,
    proj, conv, ab, flags, cum_in, halo, taps, head, do_in, tinv, uval, wkey, states, entering, leaving,
    dproj, dab, tail_rows, head_rows, dtaps, dhead,
    state, ext, tap_sum, head_sum,
):
    step = pl.program_id(0)
    steps = pl.num_programs(0)
    size = proj.shape[0]
    width = proj.shape[1]
    every = range(heads)

    @pl.when(step == 0)
    def _():
        state[...] = leaving[...].astype(f32)
        ext[size : size + 8, :] = jnp.zeros((8, width), f32)
        tap_sum[...] = jnp.zeros_like(tap_sum)
        head_sum[...] = jnp.zeros_like(head_sum)

    @pl.when(step > 0)
    def _():
        ext[size : size + 8, :] = ext[0:8, :]

    fl = flags[...]
    raw = ab[...]
    beta_all = jax.nn.sigmoid(raw)
    cum = cum_in[...]
    gates = chunk_gates(cum, heads)
    row, col = grid_of(size, size)
    strict = row > col
    betas = [beta_all[:, heads + h : heads + h + 1] for h in every]

    cq = [conv[:, h * dk : (h + 1) * dk] for h in every]
    ck = [conv[:, (heads + h) * dk : (heads + h + 1) * dk] for h in every]
    vbase = 2 * heads * dk
    sq = [silu(c) for c in cq]
    sk = [silu(c) for c in ck]
    rq = [unit_scale(s) for s in sq]
    rk = [unit_scale(s) for s in sk]
    queries = [s * r * dk**-0.5 for s, r in zip(sq, rq)]
    keys = [s * r for s, r in zip(sk, rk)]
    q16 = [q.astype(bf16) for q in queries]
    k16 = [k.astype(bf16) for k in keys]
    kk = [mm_nt(k, k) for k in k16]
    qk = [mm_nt(q, k) for q, k in zip(q16, k16)]
    attend = [gates[h][0] * qk[h] for h in every]
    weak = [jnp.where(strict, gates[h][0] * kk[h], 0.0) for h in every]

    dsum_row = jnp.zeros((LANES, size), f32)
    dsum_col = jnp.zeros((size, LANES), f32)
    end_add = jnp.zeros((1, LANES), f32)
    dbeta_all = jnp.zeros((size, LANES), f32)
    lane = lax.broadcasted_iota(jnp.int32, (size, LANES), 1)
    lane_row = lax.broadcasted_iota(jnp.int32, (1, LANES), 1)
    sub = lax.broadcasted_iota(jnp.int32, (LANES, size), 0)

    starts, users, dos, dstates, dks16 = [], [], [], [], []
    for h in every:
        entry16 = entering[h]
        start = states[0, h, :, 0:dv].astype(f32) + mm(states[0, h, :, dv : dv + dk], entry16)
        start16 = start.astype(bf16)
        both = mm(jnp.concatenate([wkey[:, h * dk : (h + 1) * dk], k16[h]], axis=0), start16)
        starts.append((start, start16, both[size:]))
        users.append((uval[:, h * dv : (h + 1) * dv].astype(f32) - both[:size]).astype(bf16))
        dos.append(do_in[:, h * dv : (h + 1) * dv])
        dstates.append(state[h])
    d16 = [d.astype(bf16) for d in dstates]
    du = [
        mm_tn(attend[h], dos[h]) + mm(gates[h][2] * keys[h], d16[h]) for h in every
    ]
    dright = [mm_tn(tinv[:, h * size : (h + 1) * size], du[h]) for h in every]
    for h in every:
        decay, entry, tail, kept = gates[h]
        beta = betas[h]
        start, start16, recalled = starts[h]
        dr = dright[h]
        pair = jnp.concatenate([dos[h], dr.astype(bf16)], axis=0)
        wide = mm_nt(pair, jnp.concatenate([users[h], start16], axis=0))
        dattend = wide[:size, :size]
        dqe = wide[:size, size:]
        dlow = -wide[size:, :size]
        dke = -beta * wide[size:, size:]
        user_end = mm_nt(users[h], d16[h])
        state[h] = kept * dstates[h] + mm_tn(
            jnp.concatenate([entry * queries[h], -(beta * entry) * keys[h]], axis=0), pair
        )
        dqk = dattend * decay
        dkk = jnp.where(strict, dlow * decay, 0.0) * beta
        stack = jnp.concatenate([dqk, dkk], axis=0).astype(bf16)
        ahead = mm(stack, k16[h])
        behind = mm_tn(stack, jnp.concatenate([q16[h], k16[h]], axis=0))
        dq = ahead[:size] + entry * dqe
        dk_ = ahead[size:] + behind + entry * dke + tail * user_end
        base = vbase + h * dv
        cv = conv[:, base : base + dv]
        sigv = jax.nn.sigmoid(cv)
        value = cv * sigv
        ext[0:size, base : base + dv] = (beta * dr) * (sigv * (1.0 + cv * (1.0 - sigv)))
        dbeta = jnp.sum(dr * (value - entry * recalled), axis=-1, keepdims=True) + jnp.sum(
            dlow * weak[h], axis=-1, keepdims=True
        )
        lowmask = dlow * weak[h] * beta
        paired = dattend * attend[h] + lowmask
        dentry = jnp.sum(dqe * queries[h] + dke * keys[h], axis=-1, keepdims=True)
        dtail = jnp.sum(user_end * keys[h], axis=-1, keepdims=True) * tail
        dkept = jnp.sum(
            jnp.sum(start * dstates[h], axis=1, keepdims=True), axis=0, keepdims=True
        )
        col_add = jnp.sum(paired, axis=-1, keepdims=True) + dentry * entry - dtail
        dsum_col = jnp.where(lane == h, col_add, dsum_col)
        dsum_row = jnp.where(sub == h, jnp.sum(paired, axis=0, keepdims=True), dsum_row)
        end_add = jnp.where(
            lane_row == h, jnp.sum(dtail, axis=0, keepdims=True) + dkept * kept, end_add
        )
        dbeta_all = jnp.where(lane == heads + h, dbeta, dbeta_all)
        inner = jnp.sum(dq * sq[h], axis=-1, keepdims=True)
        scale = dk**-0.5 * rq[h]
        ds = scale * dq - sq[h] * (scale * rq[h] * rq[h] * inner)
        ext[0:size, h * dk : (h + 1) * dk] = ds * silu_grad(cq[h])
        inner = jnp.sum(dk_ * sk[h], axis=-1, keepdims=True)
        ds = rk[h] * dk_ - sk[h] * (rk[h] * rk[h] * rk[h] * inner)
        ext[0:size, (heads + h) * dk : (heads + h + 1) * dk] = ds * silu_grad(ck[h])

    dcum = dsum_col - jnp.transpose(dsum_row)
    final = lax.broadcasted_iota(jnp.int32, (size, LANES), 0) == size - 1
    dcum = dcum + jnp.where(final, end_add, 0.0)
    dlog = mm_hi((row <= col).astype(f32), dcum) * (1.0 - fl[:, START : START + 1])
    rate = jnp.exp(head[0:1, :])
    shifted = raw + head[1:2, :]
    dap = dlog * (-rate) * jax.nn.sigmoid(shifted)
    dbp = dbeta_all * beta_all * (1.0 - beta_all)
    dab[...] = jnp.where(lane < heads, dap, jnp.where(lane < 2 * heads, dbp, 0.0)).astype(bf16)
    head_sum[0:1, :] += jnp.sum(dlog * (-rate) * softplus(shifted), axis=0, keepdims=True)
    head_sum[1:2, :] += jnp.sum(dap, axis=0, keepdims=True)
    dhead[...] = head_sum[...]

    later = [jnp.broadcast_to(fl[:, AHEAD + s : AHEAD + s + 1], (size, LANES)) for s in (1, 2, 3)]
    for lo in range(0, width, LANES):
        at = slice(lo, lo + LANES)
        here = proj[:, at]
        own = ext[0:size, at]
        total = own * taps[3:4, at]
        tap_sum[3:4, at] += jnp.sum(own * here, axis=0, keepdims=True)
        for s in (1, 2, 3):
            moved = ext[s : s + size, at] * later[s - 1]
            total += moved * taps[3 - s : 4 - s, at]
            tap_sum[3 - s : 4 - s, at] += jnp.sum(moved * here, axis=0, keepdims=True)
        dproj[:, at] = total.astype(bf16)

        @pl.when(step == 0)
        def _():
            tail_rows[:, at] = total[size - 8 : size, :]

    @pl.when(step == steps - 1)
    def _():
        head_rows[...] = ext[0:8, :]
        sub8 = lax.broadcasted_iota(jnp.int32, (8, width), 0)
        for s in (1, 2, 3):
            ok = (sub8 < s).astype(f32) * fl[0:8, VALID + s : VALID + s + 1]
            before = pltpu.roll(halo[...], s, 0)
            tap_sum[3 - s : 4 - s, :] += jnp.sum(
                ext[0:8, :] * before * ok, axis=0, keepdims=True
            )

    dtaps[...] = tap_sum[...]


def delta_grad(
    proj, conv, flags, cum, halo, taps, head, do, tinv, uval, wkey, states, entering, leaving,
    heads, dk, dv,
):
    rows = proj.shape[0]
    size = CHUNK
    steps = rows // size
    width = 2 * heads * dk + heads * dv
    ab_at = (width + heads * dv) // LANES

    def rowwise(cols, at=0):
        return pl.BlockSpec((size, cols), lambda n: (steps - 1 - n, at))

    outs = [
        ((rows, width), bf16, rowwise(width)),
        ((rows, LANES), bf16, rowwise(LANES)),
        ((8, width), f32, whole((8, width))),
        ((8, width), f32, whole((8, width))),
        ((8, width), f32, whole((8, width))),
        ((8, LANES), f32, whole((8, LANES))),
    ]
    return pl.pallas_call(
        functools.partial(grad_kernel, heads, dk, dv),
        grid=(steps,),
        in_specs=[
            rowwise(width),
            rowwise(width),
            rowwise(LANES, ab_at),
            rowwise(LANES),
            rowwise(LANES),
            whole((8, width)),
            whole((8, width)),
            whole((8, LANES)),
            rowwise(heads * dv),
            rowwise(heads * size),
            rowwise(heads * dv),
            rowwise(heads * dk),
            pl.BlockSpec((1, heads, dk, dv + dk), lambda n: (steps - 1 - n, 0, 0, 0)),
            whole((heads, dk, dv)),
            whole((heads, dk, dv)),
        ],
        out_specs=[spec for _, _, spec in outs],
        out_shape=[jax.ShapeDtypeStruct(shape, kind) for shape, kind, _ in outs],
        scratch_shapes=[
            pltpu.VMEM((heads, dk, dv), f32),
            pltpu.VMEM((size + 8, width), f32),
            pltpu.VMEM((8, width), f32),
            pltpu.VMEM((8, LANES), f32),
        ],
        compiler_params=vmem(),
        cost_estimate=pl.CostEstimate(
            flops=rows * heads * 200 * size * (dv + dk + size),
            bytes_accessed=rows * width * 16,
            transcendentals=rows * width * 2,
        ),
    )(
        proj, conv, proj, flags, cum, halo, taps, head, do, tinv, uval, wkey, states, entering,
        leaving,
    )


def shifted(value, axis, distance):
    count = lax.axis_size(axis)
    route = [(i, i + distance) for i in range(count) if 0 <= i + distance < count]
    return lax.ppermute(value, axis, route)


def heads_mm(a, b):
    return jnp.einsum("hij,hjk->hik", a, b, preferred_element_type=f32)


def heads_mm_tn(a, b):
    return jnp.einsum("hji,hjk->hik", a, b, preferred_element_type=f32)


def entering_state(own, dv, reach):
    runs = []
    run = own
    distance = 1
    while distance < reach:
        runs.append(run[:, :, dv:])
        before = shifted(run, "ctx", distance)
        joined = heads_mm(run[:, :, dv:], before)
        run = jnp.concatenate(
            [run[:, :, :dv].astype(f32) + joined[:, :, :dv], joined[:, :, dv:]], axis=-1
        ).astype(bf16)
        distance *= 2
    entering = shifted(run[:, :, :dv], "ctx", 1)
    ahead = [part if j == 0 else shifted(part, "ctx", 1 - 2**j) for j, part in enumerate(runs)]
    return entering, ahead


def leaving_grad(own, ahead):
    run = own
    for j, maps in enumerate(ahead):
        later = shifted(run, "ctx", -(2**j))
        run = (run.astype(f32) + heads_mm_tn(maps, later)).astype(bf16)
    return shifted(run, "ctx", -1)


def summed_over_tp(part):
    count = lax.axis_size("tp")
    total = part.astype(f32)
    for d in range(1, count):
        route = [(i, (i + d) % count) for i in range(count)]
        total = total + lax.ppermute(part, "tp", route).astype(f32)
    return total


def swapped(value, axis, bit):
    return lax.ppermute(value, axis, [(i, i ^ bit) for i in range(lax.axis_size(axis))])


def sum_kernel(plan, *refs):
    count = len(plan)
    grads, outs = refs[:count], refs[count : 2 * count]
    refs = refs[2 * count :]
    own, fs_in, in_y, in_m, in_h, full = (refs[i * count : (i + 1) * count] for i in range(6))
    load_sem, send_sem, recv_sem = refs[6 * count :]
    fs = lax.axis_index("fs")
    me = lax.axis_index("ctx")
    y = lax.rem(me, 2)
    z = lax.div(me, 2)
    hub = lax.div(z, 2)
    inner = lax.rem(lax.div(z + 1, 2), 2)
    mate = z + 1 - 2 * lax.rem(z, 2)
    core = {"fs": 1 - fs}
    beside = {"ctx": z * 2 + 1 - y}
    paired = {"ctx": mate * 2 + y}
    across = {"ctx": (3 - z) * 2 + y}
    barrier = pltpu.get_barrier_semaphore()
    for partner in (core, beside, paired, across):
        pl.semaphore_signal(barrier, inc=1, device_id=partner, device_id_type=pl.DeviceIdType.MESH)
    pl.semaphore_wait(barrier, 4)

    segments = []
    for i, widths in enumerate(plan):
        lo = 0
        for w in widths:
            segments.append((i, slice(lo, lo + w)))
            lo += w
    total = len(segments)

    def rows(start, n):
        return pl.ds(pl.multiple_of(start, 16), n)

    def stages(g):
        i, at = segments[g]
        half = own[i].shape[0]
        q, e = half // 2, half // 4
        y_first = g % 2 == 0

        def remote(slot, src, dst, partner):
            return pltpu.make_async_remote_copy(
                src_ref=src,
                dst_ref=dst,
                send_sem=send_sem.at[g, slot],
                recv_sem=recv_sem.at[g, slot],
                device_id=partner,
                device_id_type=pl.DeviceIdType.MESH,
            )

        def moved(slot, source, target, start, n, partner):
            return remote(
                slot, source[i].at[rows(start, n), at], target[i].at[rows(start, n), at], partner
            )

        def add(target, one, two, start, n):
            step = 32 if n % 32 == 0 else 16

            def body(j, carry):
                r = rows(start + j * step, step)
                total = one[i][r, at].astype(f32) + two[i][r, at].astype(f32)
                target[i][r, at] = total.astype(bf16)
                return carry

            lax.fori_loop(0, n // step, body, 0)

        load = pltpu.make_async_copy(
            grads[i].at[rows(fs * half, half), at], own[i].at[:, at], load_sem.at[g]
        )
        unload = pltpu.make_async_copy(full[i].at[:, at], outs[i].at[:, at], load_sem.at[total + g])
        fs_copy = remote(0, grads[i].at[rows((1 - fs) * half, half), at], fs_in[i].at[:, at], core)
        if y_first:
            mine = y * q
            low_copy = moved(1, own, in_y, (1 - y) * q, q, beside)
            mate_copy = moved(2, own, in_m, mine, q, paired)
            hub_copy = moved(3, own, in_h, mine + (1 - hub) * e, e, across)
            back_hub = moved(4, full, full, mine + hub * e, e, across)
            back_low = moved(5, full, full, mine, q, beside)
            back_mate = moved(6, full, full, mine, q, paired)
        else:
            mine = hub * q
            mate_copy = moved(2, own, in_m, 0, half, paired)
            hub_copy = moved(3, own, in_h, (1 - hub) * q, q, across)
            low_copy = moved(1, own, in_y, mine + (1 - y) * e, e, beside)
            back_low = moved(5, full, full, mine + y * e, e, beside)
            back_hub = moved(4, full, full, mine, q, across)
            back_mate = moved(6, full, full, 0, half, paired)

        def begin():
            fs_copy.start()
            load.start()

        def finish():
            @pl.when(inner == 0)
            def _():
                mate_copy.wait_send()

            @pl.when(inner == 1)
            def _():
                back_mate.wait_send()

            unload.wait()

        def cores():
            load.wait()
            fs_copy.wait()
            add(own, own, fs_in, 0, half)

        if y_first:

            def s0():
                cores()
                low_copy.start()

            def s1():
                low_copy.wait()
                add(own, own, in_y, mine, q)

                @pl.when(inner == 0)
                def _():
                    mate_copy.start()

            def s2():
                @pl.when(inner == 1)
                def _():
                    mate_copy.wait_recv()
                    add(own, own, in_m, mine, q)
                    hub_copy.start()

            def s3():
                @pl.when(inner == 1)
                def _():
                    hub_copy.wait()
                    add(full, own, in_h, mine + hub * e, e)
                    back_hub.start()

            def s4():
                @pl.when(inner == 1)
                def _():
                    back_hub.wait()
                    back_mate.start()
                    back_low.start()

            def s5():
                @pl.when(inner == 0)
                def _():
                    back_mate.wait_recv()
                    back_low.start()

            def s6():
                back_low.wait()
                unload.start()

        else:

            def s0():
                cores()

                @pl.when(inner == 0)
                def _():
                    mate_copy.start()

            def s1():
                @pl.when(inner == 1)
                def _():
                    mate_copy.wait_recv()
                    add(own, own, in_m, 0, half)
                    hub_copy.start()

            def s2():
                @pl.when(inner == 1)
                def _():
                    hub_copy.wait()
                    add(own, own, in_h, mine, q)
                    low_copy.start()

            def s3():
                @pl.when(inner == 1)
                def _():
                    low_copy.wait()
                    add(full, own, in_y, mine + y * e, e)
                    back_low.start()

            def s4():
                @pl.when(inner == 1)
                def _():
                    back_low.wait()
                    back_hub.start()

            def s5():
                @pl.when(inner == 1)
                def _():
                    back_hub.wait()
                    back_mate.start()
                    unload.start()

            def s6():
                @pl.when(inner == 0)
                def _():
                    back_mate.wait_recv()
                    unload.start()

        return begin, (s0, s1, s2, s3, s4, s5, s6), finish

    work = [stages(g) for g in range(total)]
    for begin, _, _ in work:
        begin()
    for t in range(total + 6):
        for stage in range(7):
            if 0 <= t - stage < total:
                work[t - stage][1][stage]()
    for _, _, finish in work:
        finish()


def segment_widths(cols, rows, target=128 * 1024):
    tiles = cols // LANES
    parts = max(1, min(tiles, round(rows * cols / target)))
    return tuple((tiles * (j + 1) // parts - tiles * j // parts) * LANES for j in range(parts))


def reduced(grads, collective_id, micros):
    if lax.axis_size("ctx") != 8 or lax.axis_size("fs") != 2:
        parts = [lax.psum_scatter(g, "fs", scatter_dimension=0, tiled=True) for g in grads]
        return [lax.psum(part, "ctx") for part in parts]
    shapes = [(g.shape[0] // 2, g.shape[1]) for g in grads]
    plan = tuple(segment_widths(cols, half) for half, cols in shapes)
    total = sum(len(widths) for widths in plan)
    return pl.pallas_call(
        functools.partial(sum_kernel, plan),
        in_specs=[pl.BlockSpec(memory_space=pl.ANY)] * len(grads),
        out_specs=[pl.BlockSpec(memory_space=pl.ANY)] * len(grads),
        out_shape=[jax.ShapeDtypeStruct(shape, bf16) for shape in shapes],
        scratch_shapes=[pltpu.VMEM(shape, bf16) for shape in shapes] * 6
        + [
            pltpu.SemaphoreType.DMA((2 * total,)),
            pltpu.SemaphoreType.DMA((total, 7)),
            pltpu.SemaphoreType.DMA((total, 7)),
        ],
        compiler_params=pltpu.CompilerParams(
            collective_id=collective_id, has_side_effects=True, vmem_limit_bytes=56 * MIB
        ),
        cost_estimate=pl.CostEstimate(
            flops=micros * 10**9, bytes_accessed=4 * sum(g.size for g in grads), transcendentals=0
        ),
    )(*grads)


def scattered(grad):
    return lax.psum_scatter(grad, ("fs", "ctx"), scatter_dimension=0, tiled=True)


def reduced_little(little):
    mine = lax.axis_index("fs")
    give = lax.dynamic_slice_in_dim(little, 1 - mine, 1, 0)
    keep = lax.dynamic_slice_in_dim(little, mine, 1, 0)
    total = (keep + swapped(give, "fs", 1))[0]
    bit = 1
    while bit < lax.axis_size("ctx"):
        total = total + swapped(total, "ctx", bit)
        bit *= 2
    return total


def per_device(
    tokens, cotangent, lengths, order, mixer_gain, w_query, w_key, w_value, w_outgate, w_decay,
    w_beta, conv_query, conv_key, conv_value, decay_log, decay_bias, out_gain, w_output, mlp_gain,
    w_gate, w_up, w_down,
):
    rows, model = tokens.shape[1:]
    ctx = lax.axis_size("ctx")
    fs = lax.axis_size("fs")
    me = lax.axis_index("ctx")
    heads = decay_log.shape[0]
    dk = w_query.shape[1] // heads
    dv = w_value.shape[1] // heads
    key_cols, value_cols = heads * dk, heads * dv
    width = 2 * key_cols + value_cols
    hidden_cols = w_gate.shape[1]
    total = order.shape[1]
    peer = rows // ctx
    halo_rows = TAPS - 1
    sequences = lengths.shape[1]
    longest = 2 * total // (sequences + 1)
    reach = min(ctx - 1, -(-longest // rows))

    order_row = order[0]
    source_all = order_row // rows
    mine = (source_all == me).reshape(ctx, rows)
    upto = (jnp.arange(rows)[:, None] <= jnp.arange(rows)[None, :]).astype(bf16)
    rank_all = jnp.dot(mine.astype(bf16), upto, preferred_element_type=f32).astype(jnp.int32) - 1
    slots = jnp.arange(peer, dtype=jnp.int32)
    picked = mine[:, None, :] & (rank_all[:, None, :] == slots[None, :, None])
    local_all = (order_row - me * rows).reshape(ctx, 1, rows)
    send_order = jnp.sum(jnp.where(picked, local_all, 0), axis=2).reshape(rows)
    given = lax.dynamic_slice_in_dim(order_row, me * rows, rows)
    source = given // rows
    from_each = source[None, :] == jnp.arange(ctx, dtype=jnp.int32)[:, None]
    rank_here = jnp.dot(from_each.astype(bf16), upto, preferred_element_type=f32) - 1.0
    rank_here = jnp.sum(jnp.where(from_each, rank_here, 0.0), axis=0).astype(jnp.int32)
    recv_slot = source * peer + rank_here
    iota = jnp.arange(rows, dtype=jnp.int32)
    gather_send = (send_order[:, None] == iota[None, :]).astype(bf16)
    gather_recv = (recv_slot[:, None] == iota[None, :]).astype(bf16)

    def moved(maps, values, transposed=False):
        return lax.dot_general(
            maps, values, (((0 if transposed else 1,), (0,)), ((), ())), preferred_element_type=f32
        ).astype(bf16)

    def to_packed(values):
        arrived = lax.all_to_all(
            moved(gather_send, values), "ctx", split_axis=0, concat_axis=0, tiled=True
        )
        return moved(gather_recv, arrived)

    def to_given(values):
        arrived = lax.all_to_all(
            moved(gather_recv, values, True), "ctx", split_axis=0, concat_axis=0, tiled=True
        )
        return moved(gather_send, arrived, True)

    resident = to_packed(tokens[0])

    offsets = jnp.cumsum(lengths[0]) - lengths[0]
    positions = me * rows - halo_rows + jnp.arange(rows + 2 * halo_rows, dtype=jnp.int32)
    number = jnp.sum((offsets[None, :] <= positions[:, None]).astype(jnp.int32), axis=1)
    here = number[halo_rows : halo_rows + rows]
    fresh = jnp.any(offsets[None, :] == positions[halo_rows : halo_rows + rows, None], axis=1)
    columns = [jnp.zeros((rows,), f32)] * START + [fresh.astype(f32)]
    for s in range(1, TAPS):
        columns.append((number[halo_rows - s : halo_rows - s + rows] == here).astype(f32))
    for s in range(1, TAPS):
        columns.append((number[halo_rows + s : halo_rows + s + rows] == here).astype(f32))
    flags = jnp.stack(columns, axis=1)
    flags = jnp.pad(flags, ((0, 0), (0, LANES - flags.shape[1])))

    pad = jnp.zeros((w_decay.shape[0], LANES - 2 * heads), bf16)
    w_in = jnp.concatenate([w_query, w_key, w_value, w_outgate, w_decay, w_beta, pad], axis=1)
    w_in = lax.all_gather(w_in, "fs", axis=0, tiled=True)
    w_wide = lax.all_gather(jnp.concatenate([w_gate, w_up], axis=1), "fs", axis=0, tiled=True)
    w_down = lax.all_gather(w_down, "fs", axis=0, tiled=True)
    w_output = lax.all_gather(w_output, "fs", axis=0, tiled=True)
    small = jnp.concatenate(
        [
            conv_query.T.reshape(-1),
            conv_key.T.reshape(-1),
            conv_value.T.reshape(-1),
            mixer_gain,
            mlp_gain,
            out_gain,
        ]
    )
    small = lax.all_gather(small, "fs", axis=0).astype(f32)
    pieces, at = [], 0
    for channels in (conv_query.shape[0], conv_key.shape[0], conv_value.shape[0]):
        part = small[:, at : at + TAPS * channels].reshape(fs, TAPS, channels)
        pieces.append(part.transpose(1, 0, 2).reshape(TAPS, fs * channels))
        at += TAPS * channels
    taps = jnp.pad(jnp.concatenate(pieces, axis=1), ((0, 8 - TAPS), (0, 0)))
    gains = []
    for size in (mixer_gain.shape[0], mlp_gain.shape[0], out_gain.shape[0]):
        gains.append(small[:, at : at + size].reshape(-1))
        at += size
    gain_one, gain_two, gain_out = gains
    gain_rows = jnp.broadcast_to(gain_out[None, :], (8, dv))
    head = jnp.pad(
        jnp.stack([decay_log, decay_bias]), ((0, 6), (0, LANES - heads))
    )

    x = resident.astype(f32)
    inv_one = lax.rsqrt(jnp.mean(x * x, axis=-1, keepdims=True) + EPS)
    n1 = (x * inv_one * gain_one).astype(bf16)
    proj = jnp.dot(n1, w_in, preferred_element_type=f32)
    halo = shifted(proj[rows - 8 :, :width], "ctx", 1)
    conv, local, qa, states, tinv, uval, wkey, qeff, ktail, cum, last = delta_forward(
        proj, flags, halo, taps, head, heads, dk, dv
    )
    entering, ahead = entering_state(last, dv, reach)
    entering, cot = lax.optimization_barrier((entering, cotangent[0]))
    e = to_packed(cot)
    y1, part = delta_mix(local, qa, entering, proj, gain_rows, w_output, heads, dk, dv)

    r = x + summed_over_tp(part)
    inv_two = lax.rsqrt(jnp.mean(r * r, axis=-1, keepdims=True) + EPS)
    n2 = (r * inv_two * gain_two).astype(bf16)
    wide = jnp.dot(n2, w_wide, preferred_element_type=f32)
    gp, up = wide[:, :hidden_cols], wide[:, hidden_cols:]
    act = silu(gp)
    hid = (act * up).astype(bf16)
    down = jnp.dot(hid, w_down, preferred_element_type=f32).astype(bf16)
    dhid = lax.dot_general(e, w_down, (((1,), (1,)), ((), ())), preferred_element_type=f32)
    dwide = jnp.concatenate(
        [(dhid * up * silu_grad(gp)).astype(bf16), (dhid * act).astype(bf16)], axis=1
    )
    dn2 = lax.dot_general(dwide, w_wide, (((1,), (1,)), ((), ())), preferred_element_type=f32)
    dn2 = summed_over_tp(dn2.astype(bf16))
    def outer(a, b):
        return lax.dot_general(
            a, b, (((0,), (0,)), ((), ())), preferred_element_type=f32
        ).astype(bf16)

    def halves(grad):
        return grad.reshape(fs, grad.shape[0] // fs, *grad.shape[1:])

    half = model // fs
    g_down = outer(hid, e)
    down_rows = hidden_cols // fs
    pieces = []
    for f in range(fs):
        pieces.append(outer(dwide, n2[:, f * half : (f + 1) * half]))
        rows_f = g_down[f * down_rows : (f + 1) * down_rows]
        pieces += [rows_f[:, j * half : (j + 1) * half] for j in range(fs)]
    dn2, down, mlp_cat = lax.optimization_barrier((dn2, down, jnp.concatenate(pieces, axis=0)))
    mlp_share = scattered(mlp_cat)
    result = (r + summed_over_tp(down)).astype(bf16)
    grad_mlp_gain = jnp.sum(dn2 * r * inv_two, axis=0)
    scaled = gain_two * dn2
    dr = (
        e.astype(f32)
        + inv_two * scaled
        - r * (inv_two * inv_two * inv_two * jnp.mean(scaled * r, axis=-1, keepdims=True))
    )
    er = dr.astype(bf16)

    dz, do, dgain_out, first = delta_back(
        er, local, qa, entering, proj, gain_rows, w_output, qeff, wkey, ktail, cum, heads, dk, dv
    )
    leaving = leaving_grad(first, ahead)
    block_out = to_given(result)
    g_z = outer(n1, dz)
    g_o = outer(y1, er)
    dproj, dab, tail_rows, head_rows, dtaps, dhead = delta_grad(
        proj, conv, flags, cum, halo, taps, head, do, tinv, uval, wkey, states, entering, leaving,
        heads, dk, dv,
    )
    dproj, mlp_share = lax.optimization_barrier((dproj, mlp_share))
    g_mlp_all = lax.all_gather(mlp_share, "ctx", axis=0, tiled=True)
    next_rows = shifted(head_rows, "ctx", -1)
    extra = jnp.zeros_like(tail_rows)
    for s in range(1, TAPS):
        part_s = jnp.concatenate([jnp.zeros((8 - s, width), f32), next_rows[:s]], axis=0)
        extra = extra + part_s * taps[TAPS - 1 - s] * flags[rows - 8 :, AHEAD + s][:, None]
    dproj = lax.dynamic_update_slice(dproj, (tail_rows + extra).astype(bf16), (rows - 8, 0))
    dall = jnp.concatenate([dproj, dz, dab], axis=1)
    dn1 = lax.dot_general(dall, w_in, (((1,), (1,)), ((), ())), preferred_element_type=f32)
    dn1 = summed_over_tp(dn1.astype(bf16))
    g_in = outer(n1, jnp.concatenate([dproj, dab], axis=1))
    g_in, g_z, g_o = reduced([g_in, g_z, g_o], 1, 110)
    dn1, g_in, g_z, g_o = lax.optimization_barrier((dn1, g_in, g_z, g_o))
    g_wide = jnp.swapaxes(g_mlp_all[: 2 * hidden_cols], 0, 1)
    g_down = g_mlp_all[2 * hidden_cols :].reshape(fs, down_rows, half)
    g_down = jnp.concatenate([g_down[j] for j in range(fs)], axis=1)
    grad_mixer_gain = jnp.sum(dn1 * x * inv_one, axis=0)
    scaled = gain_one * dn1
    grad_in = (
        dr
        + inv_one * scaled
        - x * (inv_one * inv_one * inv_one * jnp.mean(scaled * x, axis=-1, keepdims=True))
    ).astype(bf16)
    grad_tokens = to_given(grad_in)

    def tap_part(lo, channels):
        return dtaps[:TAPS, lo : lo + channels].reshape(TAPS, fs, -1).transpose(1, 0, 2).reshape(fs, -1)

    share = summed_over_tp(jnp.sum(dgain_out, axis=0).astype(bf16))
    rates = jnp.broadcast_to(dhead[:2, :heads].reshape(1, 2 * heads), (fs, 2 * heads))
    little = jnp.concatenate(
        [
            tap_part(0, key_cols),
            tap_part(key_cols, key_cols),
            tap_part(2 * key_cols, value_cols),
            halves(grad_mixer_gain),
            halves(grad_mlp_gain),
            halves(share),
            rates,
        ],
        axis=1,
    )
    little = reduced_little(little)
    taken, at = [], 0
    for channels in (conv_query.shape[0], conv_key.shape[0], conv_value.shape[0]):
        taken.append(little[at : at + TAPS * channels].reshape(TAPS, channels).T)
        at += TAPS * channels
    for size in (mixer_gain.shape[0], mlp_gain.shape[0], out_gain.shape[0], heads, heads):
        taken.append(little[at : at + size])
        at += size
    g_cq, g_ck, g_cv, g_mixer, g_mlp, g_out_gain, g_log, g_bias = taken
    ends = [key_cols, 2 * key_cols, width, width + heads]
    g_query, g_key, g_value, g_decay, g_beta = (
        g_in[:, lo:hi].astype(f32) for lo, hi in zip([0] + ends, ends + [ends[-1] + heads])
    )
    return (
        block_out[None],
        grad_tokens[None],
        g_mixer,
        g_query,
        g_key,
        g_value,
        g_z.astype(f32),
        g_decay,
        g_beta,
        g_cq,
        g_ck,
        g_cv,
        g_log,
        g_bias,
        g_out_gain,
        g_o.astype(f32),
        g_mlp,
        g_wide[:, :hidden_cols].astype(f32),
        g_wide[:, hidden_cols:].astype(f32),
        g_down.astype(f32),
    )


def solution(mesh):
    split = P("fs", "ctx", None)
    cols = P("fs", "tp")
    both = P(("tp", "fs"), None)
    in_specs = (
        split, split, P("fs", None), P("fs", None), P("fs"),
        cols, cols, cols, cols, cols, cols,
        both, both, both, P("tp"), P("tp"), P("fs"), both, P("fs"), cols, cols, both,
    )
    out_specs = (
        split, split, P("fs"),
        cols, cols, cols, cols, cols, cols,
        both, both, both, P("tp"), P("tp"), P("fs"), both, P("fs"), cols, cols, both,
    )
    return jax.shard_map(
        per_device, mesh=mesh, in_specs=in_specs, out_specs=out_specs, check_vma=False
    )
```

```python
import functools

import jax
import jax.numpy as jnp
from jax import lax
from jax.experimental import pallas as pl
from jax.experimental.pallas import tpu as pltpu
from jax.sharding import PartitionSpec as P

TAPS = 4
CHUNK = 128
EPS = 1e-6
LANES = 128
START, VALID, AHEAD = 8, 8, 11
HI = lax.Precision.HIGHEST
bf16 = jnp.bfloat16
f32 = jnp.float32
MIB = 1024 * 1024


def mm(a, b):
    return jnp.dot(a.astype(bf16), b.astype(bf16), preferred_element_type=f32)


def mm_nt(a, b):
    return lax.dot_general(
        a.astype(bf16), b.astype(bf16), (((1,), (1,)), ((), ())), preferred_element_type=f32
    )


def mm_tn(a, b):
    return lax.dot_general(
        a.astype(bf16), b.astype(bf16), (((0,), (0,)), ((), ())), preferred_element_type=f32
    )


def mm_hi(a, b):
    return jnp.dot(a, b, precision=HI, preferred_element_type=f32)


def silu(x):
    return x * jax.nn.sigmoid(x)


def silu_grad(x):
    s = jax.nn.sigmoid(x)
    return s * (1.0 + x * (1.0 - s))


def softplus(x):
    return jnp.maximum(x, 0.0) + jnp.log1p(jnp.exp(-jnp.abs(x)))


def grid_of(rows, cols):
    return (
        lax.broadcasted_iota(jnp.int32, (rows, cols), 0),
        lax.broadcasted_iota(jnp.int32, (rows, cols), 1),
    )


def lower_inverses(systems):
    size = systems[0].shape[0]
    row, col = grid_of(size, size)
    eye = (row == col).astype(f32)
    first = ((row >> 1) == (col >> 1)) & (row > col)
    inverses = [eye - jnp.where(first, low, 0.0) for low in systems]
    level = 1
    while (1 << level) < size:
        block = (
            ((row >> (level + 1)) == (col >> (level + 1)))
            & (((row >> level) & 1) == 1)
            & (((col >> level) & 1) == 0)
        )
        parts = [mm(jnp.where(block, low, 0.0), inv) for low, inv in zip(systems, inverses)]
        inverses = [inv - mm(inv, part) for inv, part in zip(inverses, parts)]
        level += 1
    return inverses


def chunk_gates(cum, heads):
    size = cum.shape[0]
    row, col = grid_of(size, size)
    across = jnp.transpose(cum)
    seg_col = cum[:, START : START + 1]
    linked = (row >= col) & (seg_col == across[START : START + 1, :])
    from_start = seg_col == 0.0
    to_end = seg_col == cum[size - 1 : size, START : START + 1]
    out = []
    for h in range(heads):
        down = cum[:, h : h + 1]
        gap = jnp.where(linked, down - across[h : h + 1, :], 0.0)
        decay = jnp.where(linked, jnp.exp(gap), 0.0)
        entry = jnp.where(from_start, jnp.exp(down), 0.0)
        last = cum[size - 1 : size, h : h + 1]
        tail = jnp.where(to_end, jnp.exp(jnp.where(to_end, last - down, 0.0)), 0.0)
        out.append((decay, entry, tail, entry[size - 1 : size, :]))
    return out


def unit_scale(x):
    return lax.rsqrt(jnp.sum(x * x, axis=-1, keepdims=True) + EPS)


def forward_kernel(
    heads, dk, dv,
    proj, ab, flags, halo, taps, head,
    conv, local, qa, states, tinv, uval, wkey, qeff, ktail, cum_out, last,
    ext, state,
):
    step = pl.program_id(0)
    size = proj.shape[0]
    width = proj.shape[1]

    @pl.when(step == 0)
    def _():
        ext[0:8, :] = halo[...]
        row, col = grid_of(dk, dk)
        for h in range(heads):
            state[h, :, 0:dv] = jnp.zeros((dk, dv), f32)
            state[h, :, dv : dv + dk] = (row == col).astype(f32)

    @pl.when(step > 0)
    def _():
        ext[0:8, :] = ext[size : size + 8, :]

    ext[8 : 8 + size, :] = proj[...]
    fl = flags[...]
    valid = [jnp.broadcast_to(fl[:, VALID + s : VALID + s + 1], (size, LANES)) for s in (1, 2, 3)]
    for lo in range(0, width, LANES):
        at = slice(lo, lo + LANES)
        total = ext[8 : 8 + size, at] * taps[3:4, at]
        for s in (1, 2, 3):
            total += ext[8 - s : 8 - s + size, at] * taps[3 - s : 4 - s, at] * valid[s - 1]
        conv[:, at] = total

    raw = ab[...]
    lane = lax.broadcasted_iota(jnp.int32, (size, LANES), 1)
    log_decay = -jnp.exp(head[0:1, :]) * softplus(raw + head[1:2, :])
    row, col = grid_of(size, size)
    cum = mm_hi((row >= col).astype(f32), jnp.where(lane < heads, log_decay, fl))
    cum_out[...] = cum
    beta_all = jax.nn.sigmoid(raw)
    gates = chunk_gates(cum, heads)

    every = range(heads)
    betas = [beta_all[:, heads + h : heads + h + 1] for h in every]
    queries, keys, values = [], [], []
    for h in every:
        q = silu(conv[:, h * dk : (h + 1) * dk])
        k = silu(conv[:, (heads + h) * dk : (heads + h + 1) * dk])
        base = 2 * heads * dk + h * dv
        queries.append(q * unit_scale(q) * dk**-0.5)
        keys.append(k * unit_scale(k))
        values.append(silu(conv[:, base : base + dv]))
    keys16 = [k.astype(bf16) for k in keys]
    kk = [mm_nt(k, k) for k in keys16]
    qk = [mm_nt(q, k) for q, k in zip(queries, keys16)]
    strict = row > col
    systems = [jnp.where(strict, betas[h] * gates[h][0] * kk[h], 0.0) for h in every]
    inverses = lower_inverses(systems)
    solved = []
    for h in every:
        right = jnp.concatenate([betas[h] * values[h], (betas[h] * gates[h][1]) * keys[h]], axis=1)
        solved.append(mm(inverses[h], right))
    mixed = [mm(gates[h][0] * qk[h], solved[h]) for h in every]
    for h in every:
        before = state[h]
        before16 = before.astype(bf16)
        states[0, h] = before16
        w = solved[h][:, dv:].astype(bf16)
        q_now = (gates[h][1] * queries[h] - mixed[h][:, dv:]).astype(bf16)
        k_end = (gates[h][2] * keys[h]).astype(bf16)
        both = mm(jnp.concatenate([q_now, w], axis=0), before16)
        local[:, h * dv : (h + 1) * dv] = mixed[h][:, :dv] + both[:size, :dv]
        qa[:, h * dk : (h + 1) * dk] = both[:size, dv:].astype(bf16)
        fed = jnp.concatenate(
            [solved[h][:, :dv] - both[size:, :dv], -both[size:, dv:]], axis=1
        )
        after = gates[h][3] * before + mm_tn(k_end, fed)
        state[h] = after
        last[h] = after.astype(bf16)
        tinv[:, h * size : (h + 1) * size] = inverses[h].astype(bf16)
        uval[:, h * dv : (h + 1) * dv] = solved[h][:, :dv].astype(bf16)
        wkey[:, h * dk : (h + 1) * dk] = w
        qeff[:, h * dk : (h + 1) * dk] = q_now
        ktail[:, h * dk : (h + 1) * dk] = k_end


def vmem(limit=56):
    return pltpu.CompilerParams(vmem_limit_bytes=limit * MIB, dimension_semantics=("arbitrary",))


def whole(shape):
    return pl.BlockSpec(shape, lambda n: (0,) * len(shape))


def delta_forward(proj, flags, halo, taps, head, heads, dk, dv):
    rows = proj.shape[0]
    size = CHUNK
    steps = rows // size
    width = 2 * heads * dk + heads * dv
    ab_at = (width + heads * dv) // LANES

    def rowwise(cols):
        return pl.BlockSpec((size, cols), lambda n: (n, 0))

    outs = [
        ((rows, width), f32, rowwise(width)),
        ((rows, heads * dv), f32, rowwise(heads * dv)),
        ((rows, heads * dk), bf16, rowwise(heads * dk)),
        ((steps, heads, dk, dv + dk), bf16, pl.BlockSpec((1, heads, dk, dv + dk), lambda n: (n, 0, 0, 0))),
        ((rows, heads * size), bf16, rowwise(heads * size)),
        ((rows, heads * dv), bf16, rowwise(heads * dv)),
        ((rows, heads * dk), bf16, rowwise(heads * dk)),
        ((rows, heads * dk), bf16, rowwise(heads * dk)),
        ((rows, heads * dk), bf16, rowwise(heads * dk)),
        ((rows, LANES), f32, rowwise(LANES)),
        ((heads, dk, dv + dk), bf16, whole((heads, dk, dv + dk))),
    ]
    return pl.pallas_call(
        functools.partial(forward_kernel, heads, dk, dv),
        grid=(steps,),
        in_specs=[
            rowwise(width),
            pl.BlockSpec((size, LANES), lambda n: (n, ab_at)),
            rowwise(LANES),
            whole((8, width)),
            whole((8, width)),
            whole((8, LANES)),
        ],
        out_specs=[spec for _, _, spec in outs],
        out_shape=[jax.ShapeDtypeStruct(shape, kind) for shape, kind, _ in outs],
        scratch_shapes=[
            pltpu.VMEM((size + 8, width), f32),
            pltpu.VMEM((heads, dk, dv + dk), f32),
        ],
        compiler_params=vmem(),
        cost_estimate=pl.CostEstimate(
            flops=rows * heads * 40 * size * (dv + dk + size + size),
            bytes_accessed=rows * width * 14,
            transcendentals=rows * width * 2,
        ),
    )(proj, proj, flags, halo, taps, head)


def block_kernel(
    heads, dk, dv, tiles,
    local, qa, entering, zgate, gain, wout, res, e_now, gain_two, wwide, wdown, e_late,
    y_out, down_out, r_out, dr_out, er_out, gain_grad, grads_out,
    part_own, part_in, dn_own, dn_in, r_keep, hid_out, dwide_out, grads, stage, gain_sum,
    part_sems, dn_sems, out_sems,
):
    step = pl.program_id(0)
    hidden = wdown.shape[0]
    partner = {"tp": 1 - lax.axis_index("tp")}

    def swap(own, arrived, sems, t):
        return pltpu.make_async_remote_copy(
            src_ref=own.at[t],
            dst_ref=arrived.at[t],
            send_sem=sems.at[0, t],
            recv_sem=sems.at[1, t],
            device_id=partner,
            device_id_type=pl.DeviceIdType.MESH,
        )

    @pl.when(step == 0)
    def _():
        barrier = pltpu.get_barrier_semaphore()
        pl.semaphore_signal(barrier, inc=1, device_id=partner, device_id_type=pl.DeviceIdType.MESH)
        pl.semaphore_wait(barrier, 1)
        gain_sum[...] = jnp.zeros_like(gain_sum)

        def clear(i, carry):
            grads[pl.ds(pl.multiple_of(i * 128, 128), 128), :] = jnp.zeros((128, grads.shape[1]), f32)
            return carry

        lax.fori_loop(0, grads.shape[0] // 128, clear, 0)

    @pl.when(step < tiles)
    def _():
        for h in range(heads):
            at = slice(h * dv, (h + 1) * dv)
            o = local[:, at] + mm(qa[:, h * dk : (h + 1) * dk], entering[h])
            so = lax.rsqrt(jnp.mean(o * o, axis=-1, keepdims=True) + EPS)
            y_out[:, at] = (o * so * gain[0:1, :] * silu(zgate[:, at])).astype(bf16)
        part_own[step] = mm(y_out[...], wout[...]).astype(bf16)
        swap(part_own, part_in, part_sems, step).start()

    @pl.when((step >= 1) & (step <= tiles))
    def _():
        t = step - 1
        swap(part_own, part_in, part_sems, t).wait()
        r = res[...].astype(f32) + part_own[t].astype(f32) + part_in[t].astype(f32)
        r_keep[t] = r
        r_out[...] = r
        inv = lax.rsqrt(jnp.mean(r * r, axis=-1, keepdims=True) + EPS)
        n2 = (r * inv * gain_two[0:1, :]).astype(bf16)
        gp = mm(n2, wwide[:, 0:hidden])
        up = mm(n2, wwide[:, hidden : 2 * hidden])
        dhid = mm_nt(e_now[...], wdown[...])
        sig = jax.nn.sigmoid(gp)
        act = gp * sig
        hid_out[...] = (act * up).astype(bf16)
        dwide_out[:, 0:hidden] = (dhid * up * (sig * (1.0 + gp * (1.0 - sig)))).astype(bf16)
        dwide_out[:, hidden : 2 * hidden] = (dhid * act).astype(bf16)
        dn_own[t] = mm_nt(dwide_out[...], wwide[...]).astype(bf16)
        swap(dn_own, dn_in, dn_sems, t).start()
        down_out[...] = mm(hid_out[...], wdown[...]).astype(bf16)
        for lo in range(0, 2 * hidden, 2 * LANES):
            at = slice(lo, lo + 2 * LANES)
            grads[at, :] += mm_tn(dwide_out[:, at], n2)
        for lo in range(0, hidden, LANES):
            at = slice(lo, lo + LANES)
            grads[2 * hidden + lo : 2 * hidden + lo + LANES, :] += mm_tn(hid_out[:, at], e_now[...])

    @pl.when(step >= 2)
    def _():
        t = step - 2
        swap(dn_own, dn_in, dn_sems, t).wait()
        dn2 = dn_own[t].astype(f32) + dn_in[t].astype(f32)
        r = r_keep[t]
        inv = lax.rsqrt(jnp.mean(r * r, axis=-1, keepdims=True) + EPS)
        scaled = gain_two[0:1, :] * dn2
        gain_sum[0:1, :] += jnp.sum(dn2 * r * inv, axis=0, keepdims=True)
        dr = (
            e_late[...].astype(f32)
            + inv * scaled
            - r * (inv * inv * inv * jnp.mean(scaled * r, axis=-1, keepdims=True))
        )
        dr_out[...] = dr
        er_out[...] = dr.astype(bf16)
        gain_grad[...] = gain_sum[...]

    @pl.when(step == tiles + 1)
    def _():
        long, cols = hidden // 2, grads.shape[1] // 2
        chunks = []
        for f in range(2):
            chunks += [(j * long, f * cols) for j in range(4)]
            chunks += [(2 * hidden + f * long, j * cols) for j in range(2)]

        def out_copy(c):
            return pltpu.make_async_copy(
                stage.at[c % 2], grads_out.at[pl.ds(c * long, long), :], out_sems.at[c % 2]
            )

        for c, (row, col) in enumerate(chunks):
            if c >= 2:
                out_copy(c - 2).wait()
            stage[c % 2] = grads[row : row + long, col : col + cols].astype(bf16)
            out_copy(c).start()
        for c in (len(chunks) - 2, len(chunks) - 1):
            out_copy(c).wait()


def block_rest(
    local, qa, entering, proj, gain, wout, res, e, gain_two, wwide, wdown, heads, dk, dv, collective_id
):
    rows, model = res.shape
    size = CHUNK
    tiles = rows // size
    hidden = wdown.shape[0]
    z_at = (2 * heads * dk + heads * dv) // (heads * dv)

    def rowwise(cols, lag, at=0):
        return pl.BlockSpec((size, cols), lambda n: (jnp.clip(n - lag, 0, tiles - 1), at))

    def kept(shape):
        return pl.BlockSpec(shape, lambda n: (0,) * len(shape), pipeline_mode=pl.Buffered(1))

    outs = [
        ((rows, heads * dv), bf16, rowwise(heads * dv, 0)),
        ((rows, model), bf16, rowwise(model, 1)),
        ((rows, model), f32, rowwise(model, 1)),
        ((rows, model), f32, rowwise(model, 2)),
        ((rows, model), bf16, rowwise(model, 2)),
        ((8, model), f32, whole((8, model))),
        ((6 * hidden, model // 2), bf16, pl.BlockSpec(memory_space=pl.ANY)),
    ]
    return pl.pallas_call(
        functools.partial(block_kernel, heads, dk, dv, tiles),
        grid=(tiles + 2,),
        in_specs=[
            rowwise(heads * dv, 0),
            rowwise(heads * dk, 0),
            kept((heads, dk, dv)),
            rowwise(heads * dv, 0, z_at),
            kept((8, dv)),
            kept(wout.shape),
            rowwise(model, 1),
            rowwise(model, 1),
            kept((8, model)),
            kept(wwide.shape),
            kept(wdown.shape),
            rowwise(model, 2),
        ],
        out_specs=[spec for _, _, spec in outs],
        out_shape=[jax.ShapeDtypeStruct(shape, kind) for shape, kind, _ in outs],
        scratch_shapes=[pltpu.VMEM((tiles, size, model), bf16)] * 4
        + [
            pltpu.VMEM((tiles, size, model), f32),
            pltpu.VMEM((size, hidden), bf16),
            pltpu.VMEM((size, 2 * hidden), bf16),
            pltpu.VMEM((3 * hidden, model), f32),
            pltpu.VMEM((2, hidden // 2, model // 2), bf16),
            pltpu.VMEM((8, model), f32),
            pltpu.SemaphoreType.DMA((2, tiles)),
            pltpu.SemaphoreType.DMA((2, tiles)),
            pltpu.SemaphoreType.DMA((2,)),
        ],
        compiler_params=pltpu.CompilerParams(
            collective_id=collective_id,
            has_side_effects=True,
            vmem_limit_bytes=60 * MIB,
            dimension_semantics=("arbitrary",),
        ),
        cost_estimate=pl.CostEstimate(
            flops=100 * 10**9, bytes_accessed=rows * model * 40, transcendentals=rows * hidden
        ),
    )(local, qa, entering, proj, gain, wout, res, e, gain_two, wwide, wdown, e)


def back_kernel(
    heads, dk, dv,
    er, local, qa, entering, zgate, gain, wout, qeff, wkey, ktail, cum,
    dz_out, do_out, gain_out, first, state, gain_sum,
):
    step = pl.program_id(0)
    size = er.shape[0]

    @pl.when(step == 0)
    def _():
        state[...] = jnp.zeros_like(state)
        gain_sum[...] = jnp.zeros_like(gain_sum)

    dy = mm_nt(er[...], wout[...])
    ends = cum[size - 1 : size, :]
    for h in range(heads):
        at = slice(h * dv, (h + 1) * dv)
        kat = slice(h * dk, (h + 1) * dk)
        z = zgate[:, at]
        sig = jax.nn.sigmoid(z)
        act = z * sig
        o = local[:, at] + mm(qa[:, kat], entering[h])
        so = lax.rsqrt(jnp.mean(o * o, axis=-1, keepdims=True) + EPS)
        normed = o * so
        g = dy[:, at]
        scaled = gain[0:1, :] * g
        gain_sum[0:1, :] += jnp.sum(g * normed * act, axis=0, keepdims=True)
        dz_out[:, at] = (scaled * normed * (sig * (1.0 + z * (1.0 - sig)))).astype(bf16)
        back = scaled * act
        dots = jnp.mean(back * o, axis=-1, keepdims=True)
        do = (so * back - o * (so * so * so * dots)).astype(bf16)
        do_out[:, at] = do
        after = state[h]
        kept = jnp.where(ends[:, START : START + 1] == 0.0, jnp.exp(ends[:, h : h + 1]), 0.0)
        pulled = mm(ktail[:, kat], after)
        now = kept * after + mm_tn(
            jnp.concatenate([qeff[:, kat], wkey[:, kat]], axis=0),
            jnp.concatenate([do, (-pulled).astype(bf16)], axis=0),
        )
        state[h] = now
        first[h] = now.astype(bf16)
    gain_out[...] = gain_sum[...]


def delta_back(er, local, qa, entering, proj, gain, wout, qeff, wkey, ktail, cum, heads, dk, dv):
    rows, model = er.shape
    size = CHUNK
    steps = rows // size
    z_at = (2 * heads * dk + heads * dv) // (heads * dv)

    def rowwise(cols, at=0):
        return pl.BlockSpec((size, cols), lambda n: (steps - 1 - n, at))

    outs = [
        ((rows, heads * dv), bf16, rowwise(heads * dv)),
        ((rows, heads * dv), bf16, rowwise(heads * dv)),
        ((8, dv), f32, whole((8, dv))),
        ((heads, dk, dv), bf16, whole((heads, dk, dv))),
    ]
    return pl.pallas_call(
        functools.partial(back_kernel, heads, dk, dv),
        grid=(steps,),
        in_specs=[
            rowwise(model),
            rowwise(heads * dv),
            rowwise(heads * dk),
            whole((heads, dk, dv)),
            rowwise(heads * dv, z_at),
            whole((8, dv)),
            whole(wout.shape),
            rowwise(heads * dk),
            rowwise(heads * dk),
            rowwise(heads * dk),
            rowwise(LANES),
        ],
        out_specs=[spec for _, _, spec in outs],
        out_shape=[jax.ShapeDtypeStruct(shape, kind) for shape, kind, _ in outs],
        scratch_shapes=[pltpu.VMEM((heads, dk, dv), f32), pltpu.VMEM((8, dv), f32)],
        compiler_params=vmem(),
        cost_estimate=pl.CostEstimate(
            flops=20 * rows * heads * dv * model,
            bytes_accessed=rows * heads * dv * 18,
            transcendentals=rows * heads * dv,
        ),
    )(er, local, qa, entering, proj, gain, wout, qeff, wkey, ktail, cum)


def grad_kernel(
    heads, dk, dv,
    proj, conv, ab, flags, cum_in, halo, taps, head, do_in, tinv, uval, wkey, states, entering, leaving,
    dproj, dab, tail_rows, head_rows, dtaps, dhead,
    state, ext, tap_sum, head_sum,
):
    step = pl.program_id(0)
    steps = pl.num_programs(0)
    size = proj.shape[0]
    width = proj.shape[1]
    every = range(heads)

    @pl.when(step == 0)
    def _():
        state[...] = leaving[...].astype(f32)
        ext[size : size + 8, :] = jnp.zeros((8, width), f32)
        tap_sum[...] = jnp.zeros_like(tap_sum)
        head_sum[...] = jnp.zeros_like(head_sum)

    @pl.when(step > 0)
    def _():
        ext[size : size + 8, :] = ext[0:8, :]

    fl = flags[...]
    raw = ab[...]
    beta_all = jax.nn.sigmoid(raw)
    cum = cum_in[...]
    gates = chunk_gates(cum, heads)
    row, col = grid_of(size, size)
    strict = row > col
    betas = [beta_all[:, heads + h : heads + h + 1] for h in every]

    cq = [conv[:, h * dk : (h + 1) * dk] for h in every]
    ck = [conv[:, (heads + h) * dk : (heads + h + 1) * dk] for h in every]
    vbase = 2 * heads * dk
    sq = [silu(c) for c in cq]
    sk = [silu(c) for c in ck]
    rq = [unit_scale(s) for s in sq]
    rk = [unit_scale(s) for s in sk]
    queries = [s * r * dk**-0.5 for s, r in zip(sq, rq)]
    keys = [s * r for s, r in zip(sk, rk)]
    q16 = [q.astype(bf16) for q in queries]
    k16 = [k.astype(bf16) for k in keys]
    kk = [mm_nt(k, k) for k in k16]
    qk = [mm_nt(q, k) for q, k in zip(q16, k16)]
    attend = [gates[h][0] * qk[h] for h in every]
    weak = [jnp.where(strict, gates[h][0] * kk[h], 0.0) for h in every]

    dsum_row = jnp.zeros((LANES, size), f32)
    dsum_col = jnp.zeros((size, LANES), f32)
    end_add = jnp.zeros((1, LANES), f32)
    dbeta_all = jnp.zeros((size, LANES), f32)
    lane = lax.broadcasted_iota(jnp.int32, (size, LANES), 1)
    lane_row = lax.broadcasted_iota(jnp.int32, (1, LANES), 1)
    sub = lax.broadcasted_iota(jnp.int32, (LANES, size), 0)

    starts, users, dos, dstates, dks16 = [], [], [], [], []
    for h in every:
        entry16 = entering[h]
        start = states[0, h, :, 0:dv].astype(f32) + mm(states[0, h, :, dv : dv + dk], entry16)
        start16 = start.astype(bf16)
        both = mm(jnp.concatenate([wkey[:, h * dk : (h + 1) * dk], k16[h]], axis=0), start16)
        starts.append((start, start16, both[size:]))
        users.append((uval[:, h * dv : (h + 1) * dv].astype(f32) - both[:size]).astype(bf16))
        dos.append(do_in[:, h * dv : (h + 1) * dv])
        dstates.append(state[h])
    d16 = [d.astype(bf16) for d in dstates]
    du = [
        mm_tn(attend[h], dos[h]) + mm(gates[h][2] * keys[h], d16[h]) for h in every
    ]
    dright = [mm_tn(tinv[:, h * size : (h + 1) * size], du[h]) for h in every]
    for h in every:
        decay, entry, tail, kept = gates[h]
        beta = betas[h]
        start, start16, recalled = starts[h]
        dr = dright[h]
        pair = jnp.concatenate([dos[h], dr.astype(bf16)], axis=0)
        wide = mm_nt(pair, jnp.concatenate([users[h], start16], axis=0))
        dattend = wide[:size, :size]
        dqe = wide[:size, size:]
        dlow = -wide[size:, :size]
        dke = -beta * wide[size:, size:]
        user_end = mm_nt(users[h], d16[h])
        state[h] = kept * dstates[h] + mm_tn(
            jnp.concatenate([entry * queries[h], -(beta * entry) * keys[h]], axis=0), pair
        )
        dqk = dattend * decay
        dkk = jnp.where(strict, dlow * decay, 0.0) * beta
        stack = jnp.concatenate([dqk, dkk], axis=0).astype(bf16)
        ahead = mm(stack, k16[h])
        behind = mm_tn(stack, jnp.concatenate([q16[h], k16[h]], axis=0))
        dq = ahead[:size] + entry * dqe
        dk_ = ahead[size:] + behind + entry * dke + tail * user_end
        base = vbase + h * dv
        cv = conv[:, base : base + dv]
        sigv = jax.nn.sigmoid(cv)
        value = cv * sigv
        ext[0:size, base : base + dv] = (beta * dr) * (sigv * (1.0 + cv * (1.0 - sigv)))
        dbeta = jnp.sum(dr * (value - entry * recalled), axis=-1, keepdims=True) + jnp.sum(
            dlow * weak[h], axis=-1, keepdims=True
        )
        lowmask = dlow * weak[h] * beta
        paired = dattend * attend[h] + lowmask
        dentry = jnp.sum(dqe * queries[h] + dke * keys[h], axis=-1, keepdims=True)
        dtail = jnp.sum(user_end * keys[h], axis=-1, keepdims=True) * tail
        dkept = jnp.sum(
            jnp.sum(start * dstates[h], axis=1, keepdims=True), axis=0, keepdims=True
        )
        col_add = jnp.sum(paired, axis=-1, keepdims=True) + dentry * entry - dtail
        dsum_col = jnp.where(lane == h, col_add, dsum_col)
        dsum_row = jnp.where(sub == h, jnp.sum(paired, axis=0, keepdims=True), dsum_row)
        end_add = jnp.where(
            lane_row == h, jnp.sum(dtail, axis=0, keepdims=True) + dkept * kept, end_add
        )
        dbeta_all = jnp.where(lane == heads + h, dbeta, dbeta_all)
        inner = jnp.sum(dq * sq[h], axis=-1, keepdims=True)
        scale = dk**-0.5 * rq[h]
        ds = scale * dq - sq[h] * (scale * rq[h] * rq[h] * inner)
        ext[0:size, h * dk : (h + 1) * dk] = ds * silu_grad(cq[h])
        inner = jnp.sum(dk_ * sk[h], axis=-1, keepdims=True)
        ds = rk[h] * dk_ - sk[h] * (rk[h] * rk[h] * rk[h] * inner)
        ext[0:size, (heads + h) * dk : (heads + h + 1) * dk] = ds * silu_grad(ck[h])

    dcum = dsum_col - jnp.transpose(dsum_row)
    final = lax.broadcasted_iota(jnp.int32, (size, LANES), 0) == size - 1
    dcum = dcum + jnp.where(final, end_add, 0.0)
    dlog = mm_hi((row <= col).astype(f32), dcum) * (1.0 - fl[:, START : START + 1])
    rate = jnp.exp(head[0:1, :])
    shifted = raw + head[1:2, :]
    dap = dlog * (-rate) * jax.nn.sigmoid(shifted)
    dbp = dbeta_all * beta_all * (1.0 - beta_all)
    dab[...] = jnp.where(lane < heads, dap, jnp.where(lane < 2 * heads, dbp, 0.0)).astype(bf16)
    head_sum[0:1, :] += jnp.sum(dlog * (-rate) * softplus(shifted), axis=0, keepdims=True)
    head_sum[1:2, :] += jnp.sum(dap, axis=0, keepdims=True)
    dhead[...] = head_sum[...]

    later = [jnp.broadcast_to(fl[:, AHEAD + s : AHEAD + s + 1], (size, LANES)) for s in (1, 2, 3)]
    for lo in range(0, width, LANES):
        at = slice(lo, lo + LANES)
        here = proj[:, at]
        own = ext[0:size, at]
        total = own * taps[3:4, at]
        tap_sum[3:4, at] += jnp.sum(own * here, axis=0, keepdims=True)
        for s in (1, 2, 3):
            moved = ext[s : s + size, at] * later[s - 1]
            total += moved * taps[3 - s : 4 - s, at]
            tap_sum[3 - s : 4 - s, at] += jnp.sum(moved * here, axis=0, keepdims=True)
        dproj[:, at] = total.astype(bf16)

        @pl.when(step == 0)
        def _():
            tail_rows[:, at] = total[size - 8 : size, :]

    @pl.when(step == steps - 1)
    def _():
        head_rows[...] = ext[0:8, :]
        sub8 = lax.broadcasted_iota(jnp.int32, (8, width), 0)
        for s in (1, 2, 3):
            ok = (sub8 < s).astype(f32) * fl[0:8, VALID + s : VALID + s + 1]
            before = pltpu.roll(halo[...], s, 0)
            tap_sum[3 - s : 4 - s, :] += jnp.sum(
                ext[0:8, :] * before * ok, axis=0, keepdims=True
            )

    dtaps[...] = tap_sum[...]


def delta_grad(
    proj, conv, flags, cum, halo, taps, head, do, tinv, uval, wkey, states, entering, leaving,
    heads, dk, dv,
):
    rows = proj.shape[0]
    size = CHUNK
    steps = rows // size
    width = 2 * heads * dk + heads * dv
    ab_at = (width + heads * dv) // LANES

    def rowwise(cols, at=0):
        return pl.BlockSpec((size, cols), lambda n: (steps - 1 - n, at))

    outs = [
        ((rows, width), bf16, rowwise(width)),
        ((rows, LANES), bf16, rowwise(LANES)),
        ((8, width), f32, whole((8, width))),
        ((8, width), f32, whole((8, width))),
        ((8, width), f32, whole((8, width))),
        ((8, LANES), f32, whole((8, LANES))),
    ]
    return pl.pallas_call(
        functools.partial(grad_kernel, heads, dk, dv),
        grid=(steps,),
        in_specs=[
            rowwise(width),
            rowwise(width),
            rowwise(LANES, ab_at),
            rowwise(LANES),
            rowwise(LANES),
            whole((8, width)),
            whole((8, width)),
            whole((8, LANES)),
            rowwise(heads * dv),
            rowwise(heads * size),
            rowwise(heads * dv),
            rowwise(heads * dk),
            pl.BlockSpec((1, heads, dk, dv + dk), lambda n: (steps - 1 - n, 0, 0, 0)),
            whole((heads, dk, dv)),
            whole((heads, dk, dv)),
        ],
        out_specs=[spec for _, _, spec in outs],
        out_shape=[jax.ShapeDtypeStruct(shape, kind) for shape, kind, _ in outs],
        scratch_shapes=[
            pltpu.VMEM((heads, dk, dv), f32),
            pltpu.VMEM((size + 8, width), f32),
            pltpu.VMEM((8, width), f32),
            pltpu.VMEM((8, LANES), f32),
        ],
        compiler_params=vmem(),
        cost_estimate=pl.CostEstimate(
            flops=rows * heads * 200 * size * (dv + dk + size),
            bytes_accessed=rows * width * 16,
            transcendentals=rows * width * 2,
        ),
    )(
        proj, conv, proj, flags, cum, halo, taps, head, do, tinv, uval, wkey, states, entering,
        leaving,
    )


def shifted(value, axis, distance):
    count = lax.axis_size(axis)
    route = [(i, i + distance) for i in range(count) if 0 <= i + distance < count]
    return lax.ppermute(value, axis, route)


def chain_kernel(forward, levels, *refs):
    if forward:
        own, out, mats, runs, arrived, send_sem, recv_sem = refs
    else:
        own, maps, out, runs, arrived, send_sem, recv_sem = refs
    heads, dk = own.shape[:2]
    dv = out.shape[2]
    count = lax.axis_size("ctx")
    me = lax.axis_index("ctx")
    place = me if forward else count - 1 - me
    way = 1 if forward else -1
    distances = [2**j for j in range(levels)] + [1]
    reaches = sorted(set(distances))
    barrier = pltpu.get_barrier_semaphore()
    known = jnp.int32(0)
    for d in reaches:
        for sign in (1, -1):
            there = (me + sign * d >= 0) & (me + sign * d < count)
            known = known + there.astype(jnp.int32)

            @pl.when(there)
            def _(sign=sign, d=d):
                pl.semaphore_signal(
                    barrier, inc=1, device_id={"ctx": me + sign * d},
                    device_id_type=pl.DeviceIdType.MESH,
                )

    pl.semaphore_wait(barrier, known)

    def copy(j, h):
        width = dv if j >= levels - 1 else own.shape[2]
        source = own if j == 0 else runs.at[j - 1]
        return pltpu.make_async_remote_copy(
            src_ref=source.at[h, :, pl.ds(0, width)],
            dst_ref=arrived.at[j, h, :, pl.ds(0, width)],
            send_sem=send_sem.at[j, h],
            recv_sem=recv_sem.at[j, h],
            device_id={"ctx": me + way * distances[j]},
            device_id_type=pl.DeviceIdType.MESH,
        )

    def send(j, h):
        @pl.when(place + distances[j] < count)
        def _():
            copy(j, h).start()

    for h in range(heads):
        send(0, h)
    for j in range(levels + 1):
        for h in range(heads):

            @pl.when(place >= distances[j])
            def _(j=j, h=h):
                copy(j, h).wait_recv()

            @pl.when(place < distances[j])
            def _(j=j, h=h):
                arrived[j, h] = jnp.zeros(arrived.shape[2:], bf16)

            if j == levels:
                out[h] = arrived[j, h, :, 0:dv]
                continue
            run = own[h] if j == 0 else runs[j - 1, h]
            if forward:
                matrix = run[:, dv:]
                width = dv if j == levels - 1 else dv + dk
                joined = mm(matrix, arrived[j, h, :, 0:width])
                runs[j, h, :, 0:dv] = (run[:, 0:dv].astype(f32) + joined[:, 0:dv]).astype(bf16)
                if j < levels - 1:
                    runs[j, h, :, dv : dv + dk] = joined[:, dv:].astype(bf16)
                    mats[j, h] = joined[:, dv:].astype(bf16)
            else:
                joined = mm_tn(maps[j, h], arrived[j, h])
                runs[j, h] = (run.astype(f32) + joined).astype(bf16)
            send(j + 1, h)
    for j in range(levels + 1):
        for h in range(heads):

            @pl.when(place + distances[j] < count)
            def _(j=j, h=h):
                copy(j, h).wait_send()


def chained(own, maps, dv, levels, collective_id):
    heads, dk, width = own.shape
    forward = maps is None
    spec = pl.BlockSpec(memory_space=pltpu.VMEM)
    shapes = [(heads, dk, dv)] + ([(max(levels - 1, 1), heads, dk, dk)] if forward else [])
    return pl.pallas_call(
        functools.partial(chain_kernel, forward, levels),
        in_specs=[spec] * (1 if forward else 2),
        out_specs=[spec] * len(shapes),
        out_shape=[jax.ShapeDtypeStruct(shape, bf16) for shape in shapes],
        scratch_shapes=[
            pltpu.VMEM((levels, heads, dk, width), bf16),
            pltpu.VMEM((levels + 1, heads, dk, width), bf16),
            pltpu.SemaphoreType.DMA((levels + 1, heads)),
            pltpu.SemaphoreType.DMA((levels + 1, heads)),
        ],
        compiler_params=pltpu.CompilerParams(
            collective_id=collective_id, has_side_effects=True, vmem_limit_bytes=24 * MIB
        ),
        cost_estimate=pl.CostEstimate(flops=25 * 10**9, bytes_accessed=own.size * 16, transcendentals=0),
    )(*([own] if forward else [own, maps]))


def levels_of(reach):
    levels = 1
    while 2**levels < reach:
        levels += 1
    return levels


def entering_state(own, dv, reach):
    levels = levels_of(reach)
    entering, mats = chained(own, None, dv, levels, 3)
    ahead = [own[:, :, dv:]] + [shifted(mats[j - 1], "ctx", 1 - 2**j) for j in range(1, levels)]
    return entering, jnp.stack(ahead)


def leaving_grad(own, ahead):
    return chained(own, ahead, own.shape[2], ahead.shape[0], 4)[0]


def summed_over_tp(part):
    count = lax.axis_size("tp")
    total = part.astype(f32)
    for d in range(1, count):
        route = [(i, (i + d) % count) for i in range(count)]
        total = total + lax.ppermute(part, "tp", route).astype(f32)
    return total


def swapped(value, axis, bit):
    return lax.ppermute(value, axis, [(i, i ^ bit) for i in range(lax.axis_size(axis))])


def sum_kernel(plan, *refs):
    count = len(plan)
    grads, outs = refs[:count], refs[count : 2 * count]
    refs = refs[2 * count :]
    own, fs_in, in_y, in_m, in_h, full = (refs[i * count : (i + 1) * count] for i in range(6))
    load_sem, send_sem, recv_sem = refs[6 * count :]
    fs = lax.axis_index("fs")
    me = lax.axis_index("ctx")
    y = lax.rem(me, 2)
    z = lax.div(me, 2)
    hub = lax.div(z, 2)
    inner = lax.rem(lax.div(z + 1, 2), 2)
    mate = z + 1 - 2 * lax.rem(z, 2)
    core = {"fs": 1 - fs}
    beside = {"ctx": z * 2 + 1 - y}
    paired = {"ctx": mate * 2 + y}
    across = {"ctx": (3 - z) * 2 + y}
    barrier = pltpu.get_barrier_semaphore()
    for partner in (core, beside, paired, across):
        pl.semaphore_signal(barrier, inc=1, device_id=partner, device_id_type=pl.DeviceIdType.MESH)
    pl.semaphore_wait(barrier, 4)

    segments = []
    for i, widths in enumerate(plan):
        lo = 0
        for w in widths:
            segments.append((i, slice(lo, lo + w)))
            lo += w
    total = len(segments)

    def rows(start, n):
        return pl.ds(pl.multiple_of(start, 16), n)

    def stages(g):
        i, at = segments[g]
        half = own[i].shape[0]
        q, e = half // 2, half // 4
        y_first = g % 2 == 0

        def remote(slot, src, dst, partner):
            return pltpu.make_async_remote_copy(
                src_ref=src,
                dst_ref=dst,
                send_sem=send_sem.at[g, slot],
                recv_sem=recv_sem.at[g, slot],
                device_id=partner,
                device_id_type=pl.DeviceIdType.MESH,
            )

        def moved(slot, source, target, start, n, partner):
            return remote(
                slot, source[i].at[rows(start, n), at], target[i].at[rows(start, n), at], partner
            )

        def add(target, one, two, start, n):
            step = 32 if n % 32 == 0 else 16

            def body(j, carry):
                r = rows(start + j * step, step)
                total = one[i][r, at].astype(f32) + two[i][r, at].astype(f32)
                target[i][r, at] = total.astype(bf16)
                return carry

            lax.fori_loop(0, n // step, body, 0)

        load = pltpu.make_async_copy(
            grads[i].at[rows(fs * half, half), at], own[i].at[:, at], load_sem.at[g]
        )
        unload = pltpu.make_async_copy(full[i].at[:, at], outs[i].at[:, at], load_sem.at[total + g])
        fs_copy = remote(0, grads[i].at[rows((1 - fs) * half, half), at], fs_in[i].at[:, at], core)
        if y_first:
            mine = y * q
            low_copy = moved(1, own, in_y, (1 - y) * q, q, beside)
            mate_copy = moved(2, own, in_m, mine, q, paired)
            hub_copy = moved(3, own, in_h, mine + (1 - hub) * e, e, across)
            back_hub = moved(4, full, full, mine + hub * e, e, across)
            back_low = moved(5, full, full, mine, q, beside)
            back_mate = moved(6, full, full, mine, q, paired)
        else:
            mine = hub * q
            mate_copy = moved(2, own, in_m, 0, half, paired)
            hub_copy = moved(3, own, in_h, (1 - hub) * q, q, across)
            low_copy = moved(1, own, in_y, mine + (1 - y) * e, e, beside)
            back_low = moved(5, full, full, mine + y * e, e, beside)
            back_hub = moved(4, full, full, mine, q, across)
            back_mate = moved(6, full, full, 0, half, paired)

        def begin():
            fs_copy.start()
            load.start()

        def finish():
            @pl.when(inner == 0)
            def _():
                mate_copy.wait_send()

            @pl.when(inner == 1)
            def _():
                back_mate.wait_send()

            unload.wait()

        def cores():
            load.wait()
            fs_copy.wait()
            add(own, own, fs_in, 0, half)

        if y_first:

            def s0():
                cores()
                low_copy.start()

            def s1():
                low_copy.wait()
                add(own, own, in_y, mine, q)

                @pl.when(inner == 0)
                def _():
                    mate_copy.start()

            def s2():
                @pl.when(inner == 1)
                def _():
                    mate_copy.wait_recv()
                    add(own, own, in_m, mine, q)
                    hub_copy.start()

            def s3():
                @pl.when(inner == 1)
                def _():
                    hub_copy.wait()
                    add(full, own, in_h, mine + hub * e, e)
                    back_hub.start()

            def s4():
                @pl.when(inner == 1)
                def _():
                    back_hub.wait()
                    back_mate.start()
                    back_low.start()

            def s5():
                @pl.when(inner == 0)
                def _():
                    back_mate.wait_recv()
                    back_low.start()

            def s6():
                back_low.wait()
                unload.start()

        else:

            def s0():
                cores()

                @pl.when(inner == 0)
                def _():
                    mate_copy.start()

            def s1():
                @pl.when(inner == 1)
                def _():
                    mate_copy.wait_recv()
                    add(own, own, in_m, 0, half)
                    hub_copy.start()

            def s2():
                @pl.when(inner == 1)
                def _():
                    hub_copy.wait()
                    add(own, own, in_h, mine, q)
                    low_copy.start()

            def s3():
                @pl.when(inner == 1)
                def _():
                    low_copy.wait()
                    add(full, own, in_y, mine + y * e, e)
                    back_low.start()

            def s4():
                @pl.when(inner == 1)
                def _():
                    back_low.wait()
                    back_hub.start()

            def s5():
                @pl.when(inner == 1)
                def _():
                    back_hub.wait()
                    back_mate.start()
                    unload.start()

            def s6():
                @pl.when(inner == 0)
                def _():
                    back_mate.wait_recv()
                    unload.start()

        return begin, (s0, s1, s2, s3, s4, s5, s6), finish

    work = [stages(g) for g in range(total)]
    for begin, _, _ in work:
        begin()
    for t in range(total + 6):
        for stage in range(7):
            if 0 <= t - stage < total:
                work[t - stage][1][stage]()
    for _, _, finish in work:
        finish()


def segment_widths(cols, rows, target=128 * 1024):
    tiles = cols // LANES
    parts = max(1, min(tiles, round(rows * cols / target)))
    return tuple((tiles * (j + 1) // parts - tiles * j // parts) * LANES for j in range(parts))


def reduced(grads, collective_id, micros):
    if lax.axis_size("ctx") != 8 or lax.axis_size("fs") != 2:
        parts = [lax.psum_scatter(g, "fs", scatter_dimension=0, tiled=True) for g in grads]
        return [lax.psum(part, "ctx") for part in parts]
    shapes = [(g.shape[0] // 2, g.shape[1]) for g in grads]
    plan = tuple(segment_widths(cols, half) for half, cols in shapes)
    total = sum(len(widths) for widths in plan)
    return pl.pallas_call(
        functools.partial(sum_kernel, plan),
        in_specs=[pl.BlockSpec(memory_space=pl.ANY)] * len(grads),
        out_specs=[pl.BlockSpec(memory_space=pl.ANY)] * len(grads),
        out_shape=[jax.ShapeDtypeStruct(shape, bf16) for shape in shapes],
        scratch_shapes=[pltpu.VMEM(shape, bf16) for shape in shapes] * 6
        + [
            pltpu.SemaphoreType.DMA((2 * total,)),
            pltpu.SemaphoreType.DMA((total, 7)),
            pltpu.SemaphoreType.DMA((total, 7)),
        ],
        compiler_params=pltpu.CompilerParams(
            collective_id=collective_id, has_side_effects=True, vmem_limit_bytes=56 * MIB
        ),
        cost_estimate=pl.CostEstimate(
            flops=micros * 10**9, bytes_accessed=4 * sum(g.size for g in grads), transcendentals=0
        ),
    )(*grads)


def scattered(grad):
    return lax.psum_scatter(grad, ("fs", "ctx"), scatter_dimension=0, tiled=True)


def reduced_little(little):
    mine = lax.axis_index("fs")
    give = lax.dynamic_slice_in_dim(little, 1 - mine, 1, 0)
    keep = lax.dynamic_slice_in_dim(little, mine, 1, 0)
    total = (keep + swapped(give, "fs", 1))[0]
    bit = 1
    while bit < lax.axis_size("ctx"):
        total = total + swapped(total, "ctx", bit)
        bit *= 2
    return total


def per_device(
    tokens, cotangent, lengths, order, mixer_gain, w_query, w_key, w_value, w_outgate, w_decay,
    w_beta, conv_query, conv_key, conv_value, decay_log, decay_bias, out_gain, w_output, mlp_gain,
    w_gate, w_up, w_down,
):
    rows, model = tokens.shape[1:]
    ctx = lax.axis_size("ctx")
    fs = lax.axis_size("fs")
    me = lax.axis_index("ctx")
    heads = decay_log.shape[0]
    dk = w_query.shape[1] // heads
    dv = w_value.shape[1] // heads
    key_cols, value_cols = heads * dk, heads * dv
    width = 2 * key_cols + value_cols
    hidden_cols = w_gate.shape[1]
    total = order.shape[1]
    peer = rows // ctx
    halo_rows = TAPS - 1
    sequences = lengths.shape[1]
    longest = 2 * total // (sequences + 1)
    reach = min(ctx - 1, -(-longest // rows))

    order_row = order[0]
    source_all = order_row // rows
    mine = (source_all == me).reshape(ctx, rows)
    upto = (jnp.arange(rows)[:, None] <= jnp.arange(rows)[None, :]).astype(bf16)
    rank_all = jnp.dot(mine.astype(bf16), upto, preferred_element_type=f32).astype(jnp.int32) - 1
    slots = jnp.arange(peer, dtype=jnp.int32)
    picked = mine[:, None, :] & (rank_all[:, None, :] == slots[None, :, None])
    local_all = (order_row - me * rows).reshape(ctx, 1, rows)
    send_order = jnp.sum(jnp.where(picked, local_all, 0), axis=2).reshape(rows)
    given = lax.dynamic_slice_in_dim(order_row, me * rows, rows)
    source = given // rows
    from_each = source[None, :] == jnp.arange(ctx, dtype=jnp.int32)[:, None]
    rank_here = jnp.dot(from_each.astype(bf16), upto, preferred_element_type=f32) - 1.0
    rank_here = jnp.sum(jnp.where(from_each, rank_here, 0.0), axis=0).astype(jnp.int32)
    recv_slot = source * peer + rank_here
    iota = jnp.arange(rows, dtype=jnp.int32)
    gather_send = (send_order[:, None] == iota[None, :]).astype(bf16)
    gather_recv = (recv_slot[:, None] == iota[None, :]).astype(bf16)

    def moved(maps, values, transposed=False):
        return lax.dot_general(
            maps, values, (((0 if transposed else 1,), (0,)), ((), ())), preferred_element_type=f32
        ).astype(bf16)

    def exchanged(values):
        return lax.all_to_all(values, "ctx", split_axis=0, concat_axis=0, tiled=True)

    def sent_to_packed(values):
        return exchanged(moved(gather_send, values))

    def sent_to_given(values):
        return exchanged(moved(gather_recv, values, True))

    resident = moved(gather_recv, sent_to_packed(tokens[0]))

    offsets = jnp.cumsum(lengths[0]) - lengths[0]
    positions = me * rows - halo_rows + jnp.arange(rows + 2 * halo_rows, dtype=jnp.int32)
    number = jnp.sum((offsets[None, :] <= positions[:, None]).astype(jnp.int32), axis=1)
    here = number[halo_rows : halo_rows + rows]
    fresh = jnp.any(offsets[None, :] == positions[halo_rows : halo_rows + rows, None], axis=1)
    columns = [jnp.zeros((rows,), f32)] * START + [fresh.astype(f32)]
    for s in range(1, TAPS):
        columns.append((number[halo_rows - s : halo_rows - s + rows] == here).astype(f32))
    for s in range(1, TAPS):
        columns.append((number[halo_rows + s : halo_rows + s + rows] == here).astype(f32))
    flags = jnp.stack(columns, axis=1)
    flags = jnp.pad(flags, ((0, 0), (0, LANES - flags.shape[1])))

    pad = jnp.zeros((w_decay.shape[0], LANES - 2 * heads), bf16)
    w_in = jnp.concatenate([w_query, w_key, w_value, w_outgate, w_decay, w_beta, pad], axis=1)
    w_in = lax.all_gather(w_in, "fs", axis=0, tiled=True)
    w_wide = lax.all_gather(jnp.concatenate([w_gate, w_up], axis=1), "fs", axis=0, tiled=True)
    w_down = lax.all_gather(w_down, "fs", axis=0, tiled=True)
    w_output = lax.all_gather(w_output, "fs", axis=0, tiled=True)
    small = jnp.concatenate(
        [
            conv_query.T.reshape(-1),
            conv_key.T.reshape(-1),
            conv_value.T.reshape(-1),
            mixer_gain,
            mlp_gain,
            out_gain,
        ]
    )
    small = lax.all_gather(small, "fs", axis=0).astype(f32)
    pieces, at = [], 0
    for channels in (conv_query.shape[0], conv_key.shape[0], conv_value.shape[0]):
        part = small[:, at : at + TAPS * channels].reshape(fs, TAPS, channels)
        pieces.append(part.transpose(1, 0, 2).reshape(TAPS, fs * channels))
        at += TAPS * channels
    taps = jnp.pad(jnp.concatenate(pieces, axis=1), ((0, 8 - TAPS), (0, 0)))
    gains = []
    for size in (mixer_gain.shape[0], mlp_gain.shape[0], out_gain.shape[0]):
        gains.append(small[:, at : at + size].reshape(-1))
        at += size
    gain_one, gain_two, gain_out = gains
    gain_rows = jnp.broadcast_to(gain_out[None, :], (8, dv))
    head = jnp.pad(
        jnp.stack([decay_log, decay_bias]), ((0, 6), (0, LANES - heads))
    )

    x = resident.astype(f32)
    inv_one = lax.rsqrt(jnp.mean(x * x, axis=-1, keepdims=True) + EPS)
    n1 = (x * inv_one * gain_one).astype(bf16)
    proj = jnp.dot(n1, w_in, preferred_element_type=f32)
    halo = shifted(proj[rows - 8 :, :width], "ctx", 1)
    conv, local, qa, states, tinv, uval, wkey, qeff, ktail, cum, last = delta_forward(
        proj, flags, halo, taps, head, heads, dk, dv
    )
    last, arrived = lax.optimization_barrier((last, sent_to_packed(cotangent[0])))
    e = moved(gather_recv, arrived)
    entering, ahead = entering_state(last, dv, reach)
    y1, down, r, dr, er, mlp_gain_sum, mlp_cat = block_rest(
        local, qa, entering, proj, gain_rows, w_output, resident, e,
        jnp.broadcast_to(gain_two[None, :], (8, model)), w_wide, w_down, heads, dk, dv, 2,
    )
    grad_mlp_gain = mlp_gain_sum[0]

    def outer(a, b):
        return lax.dot_general(
            a, b, (((0,), (0,)), ((), ())), preferred_element_type=f32
        ).astype(bf16)

    def halves(grad):
        return grad.reshape(fs, grad.shape[0] // fs, *grad.shape[1:])

    half = model // fs
    down_rows = hidden_cols // fs
    mlp_share = scattered(mlp_cat)
    result = (r + summed_over_tp(down)).astype(bf16)

    dz, do, dgain_out, first = delta_back(
        er, local, qa, entering, proj, gain_rows, w_output, qeff, wkey, ktail, cum, heads, dk, dv
    )
    leaving = leaving_grad(first, ahead)
    g_z = outer(n1, dz)
    g_o = outer(y1, er)
    dproj, dab, tail_rows, head_rows, dtaps, dhead = delta_grad(
        proj, conv, flags, cum, halo, taps, head, do, tinv, uval, wkey, states, entering, leaving,
        heads, dk, dv,
    )
    dproj, mlp_share, arrived = lax.optimization_barrier(
        (dproj, mlp_share, sent_to_given(result))
    )
    block_out = moved(gather_send, arrived, True)
    g_mlp_all = lax.all_gather(mlp_share, "ctx", axis=0, tiled=True)
    next_rows = shifted(head_rows, "ctx", -1)
    extra = jnp.zeros_like(tail_rows)
    for s in range(1, TAPS):
        part_s = jnp.concatenate([jnp.zeros((8 - s, width), f32), next_rows[:s]], axis=0)
        extra = extra + part_s * taps[TAPS - 1 - s] * flags[rows - 8 :, AHEAD + s][:, None]
    dproj = lax.dynamic_update_slice(dproj, (tail_rows + extra).astype(bf16), (rows - 8, 0))
    dall = jnp.concatenate([dproj, dz, dab], axis=1)
    dn1 = lax.dot_general(dall, w_in, (((1,), (1,)), ((), ())), preferred_element_type=f32)
    dn1 = summed_over_tp(dn1.astype(bf16))
    g_in = outer(n1, jnp.concatenate([dproj, dab], axis=1))
    g_in, g_z, g_o = reduced([g_in, g_z, g_o], 1, 110)
    dn1, g_in, g_z, g_o = lax.optimization_barrier((dn1, g_in, g_z, g_o))
    g_wide = jnp.swapaxes(g_mlp_all[: 2 * hidden_cols], 0, 1)
    g_down = g_mlp_all[2 * hidden_cols :].reshape(fs, down_rows, half)
    g_down = jnp.concatenate([g_down[j] for j in range(fs)], axis=1)
    grad_mixer_gain = jnp.sum(dn1 * x * inv_one, axis=0)
    scaled = gain_one * dn1
    grad_in = (
        dr
        + inv_one * scaled
        - x * (inv_one * inv_one * inv_one * jnp.mean(scaled * x, axis=-1, keepdims=True))
    ).astype(bf16)
    grad_tokens = moved(gather_send, sent_to_given(grad_in), True)

    def tap_part(lo, channels):
        return dtaps[:TAPS, lo : lo + channels].reshape(TAPS, fs, -1).transpose(1, 0, 2).reshape(fs, -1)

    share = summed_over_tp(jnp.sum(dgain_out, axis=0).astype(bf16))
    rates = jnp.broadcast_to(dhead[:2, :heads].reshape(1, 2 * heads), (fs, 2 * heads))
    little = jnp.concatenate(
        [
            tap_part(0, key_cols),
            tap_part(key_cols, key_cols),
            tap_part(2 * key_cols, value_cols),
            halves(grad_mixer_gain),
            halves(grad_mlp_gain),
            halves(share),
            rates,
        ],
        axis=1,
    )
    little = reduced_little(little)
    taken, at = [], 0
    for channels in (conv_query.shape[0], conv_key.shape[0], conv_value.shape[0]):
        taken.append(little[at : at + TAPS * channels].reshape(TAPS, channels).T)
        at += TAPS * channels
    for size in (mixer_gain.shape[0], mlp_gain.shape[0], out_gain.shape[0], heads, heads):
        taken.append(little[at : at + size])
        at += size
    g_cq, g_ck, g_cv, g_mixer, g_mlp, g_out_gain, g_log, g_bias = taken
    ends = [key_cols, 2 * key_cols, width, width + heads]
    g_query, g_key, g_value, g_decay, g_beta = (
        g_in[:, lo:hi].astype(f32) for lo, hi in zip([0] + ends, ends + [ends[-1] + heads])
    )
    return (
        block_out[None],
        grad_tokens[None],
        g_mixer,
        g_query,
        g_key,
        g_value,
        g_z.astype(f32),
        g_decay,
        g_beta,
        g_cq,
        g_ck,
        g_cv,
        g_log,
        g_bias,
        g_out_gain,
        g_o.astype(f32),
        g_mlp,
        g_wide[:, :hidden_cols].astype(f32),
        g_wide[:, hidden_cols:].astype(f32),
        g_down.astype(f32),
    )


def solution(mesh):
    split = P("fs", "ctx", None)
    cols = P("fs", "tp")
    both = P(("tp", "fs"), None)
    in_specs = (
        split, split, P("fs", None), P("fs", None), P("fs"),
        cols, cols, cols, cols, cols, cols,
        both, both, both, P("tp"), P("tp"), P("fs"), both, P("fs"), cols, cols, both,
    )
    out_specs = (
        split, split, P("fs"),
        cols, cols, cols, cols, cols, cols,
        both, both, both, P("tp"), P("tp"), P("fs"), both, P("fs"), cols, cols, both,
    )
    return jax.shard_map(
        per_device, mesh=mesh, in_specs=in_specs, out_specs=out_specs, check_vma=False
    )
```

```python
import functools

import jax
import jax.numpy as jnp
from jax import lax
from jax.experimental import pallas as pl
from jax.experimental.pallas import tpu as pltpu
from jax.sharding import PartitionSpec as P

TAPS = 4
CHUNK = 128
EPS = 1e-6
LANES = 128
START, VALID, AHEAD = 8, 8, 11
HI = lax.Precision.HIGHEST
bf16 = jnp.bfloat16
f32 = jnp.float32
MIB = 1024 * 1024


def mm(a, b):
    return jnp.dot(a.astype(bf16), b.astype(bf16), preferred_element_type=f32)


def mm_nt(a, b):
    return lax.dot_general(
        a.astype(bf16), b.astype(bf16), (((1,), (1,)), ((), ())), preferred_element_type=f32
    )


def mm_tn(a, b):
    return lax.dot_general(
        a.astype(bf16), b.astype(bf16), (((0,), (0,)), ((), ())), preferred_element_type=f32
    )


def mm_hi(a, b):
    return jnp.dot(a, b, precision=HI, preferred_element_type=f32)


def silu(x):
    return x * jax.nn.sigmoid(x)


def silu_grad(x):
    s = jax.nn.sigmoid(x)
    return s * (1.0 + x * (1.0 - s))


def softplus(x):
    return jnp.maximum(x, 0.0) + jnp.log1p(jnp.exp(-jnp.abs(x)))


def grid_of(rows, cols):
    return (
        lax.broadcasted_iota(jnp.int32, (rows, cols), 0),
        lax.broadcasted_iota(jnp.int32, (rows, cols), 1),
    )


def lower_inverses(systems):
    size = systems[0].shape[0]
    row, col = grid_of(size, size)
    eye = (row == col).astype(f32)
    first = ((row >> 1) == (col >> 1)) & (row > col)
    inverses = [eye - jnp.where(first, low, 0.0) for low in systems]
    level = 1
    while (1 << level) < size:
        block = (
            ((row >> (level + 1)) == (col >> (level + 1)))
            & (((row >> level) & 1) == 1)
            & (((col >> level) & 1) == 0)
        )
        parts = [mm(jnp.where(block, low, 0.0), inv) for low, inv in zip(systems, inverses)]
        inverses = [inv - mm(inv, part) for inv, part in zip(inverses, parts)]
        level += 1
    return inverses


def chunk_gates(cum, heads):
    size = cum.shape[0]
    row, col = grid_of(size, size)
    across = jnp.transpose(cum)
    seg_col = cum[:, START : START + 1]
    linked = (row >= col) & (seg_col == across[START : START + 1, :])
    from_start = seg_col == 0.0
    to_end = seg_col == cum[size - 1 : size, START : START + 1]
    out = []
    for h in range(heads):
        down = cum[:, h : h + 1]
        gap = jnp.where(linked, down - across[h : h + 1, :], 0.0)
        decay = jnp.where(linked, jnp.exp(gap), 0.0)
        entry = jnp.where(from_start, jnp.exp(down), 0.0)
        last = cum[size - 1 : size, h : h + 1]
        tail = jnp.where(to_end, jnp.exp(jnp.where(to_end, last - down, 0.0)), 0.0)
        out.append((decay, entry, tail, entry[size - 1 : size, :]))
    return out


def unit_scale(x):
    return lax.rsqrt(jnp.sum(x * x, axis=-1, keepdims=True) + EPS)


def forward_kernel(
    heads, dk, dv,
    proj, ab, flags, halo, taps, head,
    conv, local, qa, states, tinv, uval, wkey, qeff, ktail, cum_out, last,
    ext, state,
):
    step = pl.program_id(0)
    size = proj.shape[0]
    width = proj.shape[1]

    @pl.when(step == 0)
    def _():
        ext[0:8, :] = halo[...]
        row, col = grid_of(dk, dk)
        for h in range(heads):
            state[h, :, 0:dv] = jnp.zeros((dk, dv), f32)
            state[h, :, dv : dv + dk] = (row == col).astype(f32)

    @pl.when(step > 0)
    def _():
        ext[0:8, :] = ext[size : size + 8, :]

    ext[8 : 8 + size, :] = proj[...]
    fl = flags[...]
    valid = [jnp.broadcast_to(fl[:, VALID + s : VALID + s + 1], (size, LANES)) for s in (1, 2, 3)]
    for lo in range(0, width, LANES):
        at = slice(lo, lo + LANES)
        total = ext[8 : 8 + size, at] * taps[3:4, at]
        for s in (1, 2, 3):
            total += ext[8 - s : 8 - s + size, at] * taps[3 - s : 4 - s, at] * valid[s - 1]
        conv[:, at] = total

    raw = ab[...]
    lane = lax.broadcasted_iota(jnp.int32, (size, LANES), 1)
    log_decay = -jnp.exp(head[0:1, :]) * softplus(raw + head[1:2, :])
    row, col = grid_of(size, size)
    cum = mm_hi((row >= col).astype(f32), jnp.where(lane < heads, log_decay, fl))
    cum_out[...] = cum
    beta_all = jax.nn.sigmoid(raw)
    gates = chunk_gates(cum, heads)

    every = range(heads)
    betas = [beta_all[:, heads + h : heads + h + 1] for h in every]
    queries, keys, values = [], [], []
    for h in every:
        q = silu(conv[:, h * dk : (h + 1) * dk])
        k = silu(conv[:, (heads + h) * dk : (heads + h + 1) * dk])
        base = 2 * heads * dk + h * dv
        queries.append(q * unit_scale(q) * dk**-0.5)
        keys.append(k * unit_scale(k))
        values.append(silu(conv[:, base : base + dv]))
    keys16 = [k.astype(bf16) for k in keys]
    kk = [mm_nt(k, k) for k in keys16]
    qk = [mm_nt(q, k) for q, k in zip(queries, keys16)]
    strict = row > col
    systems = [jnp.where(strict, betas[h] * gates[h][0] * kk[h], 0.0) for h in every]
    inverses = lower_inverses(systems)
    solved = []
    for h in every:
        right = jnp.concatenate([betas[h] * values[h], (betas[h] * gates[h][1]) * keys[h]], axis=1)
        solved.append(mm(inverses[h], right))
    mixed = [mm(gates[h][0] * qk[h], solved[h]) for h in every]
    for h in every:
        before = state[h]
        before16 = before.astype(bf16)
        states[0, h] = before16
        w = solved[h][:, dv:].astype(bf16)
        q_now = (gates[h][1] * queries[h] - mixed[h][:, dv:]).astype(bf16)
        k_end = (gates[h][2] * keys[h]).astype(bf16)
        both = mm(jnp.concatenate([q_now, w], axis=0), before16)
        local[:, h * dv : (h + 1) * dv] = mixed[h][:, :dv] + both[:size, :dv]
        qa[:, h * dk : (h + 1) * dk] = both[:size, dv:].astype(bf16)
        fed = jnp.concatenate(
            [solved[h][:, :dv] - both[size:, :dv], -both[size:, dv:]], axis=1
        )
        after = gates[h][3] * before + mm_tn(k_end, fed)
        state[h] = after
        last[h] = after.astype(bf16)
        tinv[:, h * size : (h + 1) * size] = inverses[h].astype(bf16)
        uval[:, h * dv : (h + 1) * dv] = solved[h][:, :dv].astype(bf16)
        wkey[:, h * dk : (h + 1) * dk] = w
        qeff[:, h * dk : (h + 1) * dk] = q_now
        ktail[:, h * dk : (h + 1) * dk] = k_end


def vmem(limit=56):
    return pltpu.CompilerParams(vmem_limit_bytes=limit * MIB, dimension_semantics=("arbitrary",))


def whole(shape):
    return pl.BlockSpec(shape, lambda n: (0,) * len(shape))


def delta_forward(proj, flags, halo, taps, head, heads, dk, dv):
    rows = proj.shape[0]
    size = CHUNK
    steps = rows // size
    width = 2 * heads * dk + heads * dv
    ab_at = (width + heads * dv) // LANES

    def rowwise(cols):
        return pl.BlockSpec((size, cols), lambda n: (n, 0))

    outs = [
        ((rows, width), f32, rowwise(width)),
        ((rows, heads * dv), f32, rowwise(heads * dv)),
        ((rows, heads * dk), bf16, rowwise(heads * dk)),
        ((steps, heads, dk, dv + dk), bf16, pl.BlockSpec((1, heads, dk, dv + dk), lambda n: (n, 0, 0, 0))),
        ((rows, heads * size), bf16, rowwise(heads * size)),
        ((rows, heads * dv), bf16, rowwise(heads * dv)),
        ((rows, heads * dk), bf16, rowwise(heads * dk)),
        ((rows, heads * dk), bf16, rowwise(heads * dk)),
        ((rows, heads * dk), bf16, rowwise(heads * dk)),
        ((rows, LANES), f32, rowwise(LANES)),
        ((heads, dk, dv + dk), bf16, whole((heads, dk, dv + dk))),
    ]
    return pl.pallas_call(
        functools.partial(forward_kernel, heads, dk, dv),
        grid=(steps,),
        in_specs=[
            rowwise(width),
            pl.BlockSpec((size, LANES), lambda n: (n, ab_at)),
            rowwise(LANES),
            whole((8, width)),
            whole((8, width)),
            whole((8, LANES)),
        ],
        out_specs=[spec for _, _, spec in outs],
        out_shape=[jax.ShapeDtypeStruct(shape, kind) for shape, kind, _ in outs],
        scratch_shapes=[
            pltpu.VMEM((size + 8, width), f32),
            pltpu.VMEM((heads, dk, dv + dk), f32),
        ],
        compiler_params=vmem(),
        cost_estimate=pl.CostEstimate(
            flops=rows * heads * 40 * size * (dv + dk + size + size),
            bytes_accessed=rows * width * 14,
            transcendentals=rows * width * 2,
        ),
    )(proj, proj, flags, halo, taps, head)


def block_kernel(
    heads, dk, dv, tiles,
    local, qa, entering, zgate, gain, wout, res, e_now, gain_two, wwide, wdown, e_late,
    local_late, qa_late, zgate_late, qeff, wkey, ktail, cum,
    y_out, down_out, r_out, dr_out, er_out, gain_grad, grads_out,
    dz_out, do_out, out_gain_grad, first,
    part_own, part_in, dn_own, dn_in, r_keep, hid_out, dwide_out, grads, stage, gain_sum,
    state, out_gain_sum, part_sems, dn_sems, out_sems,
):
    step = pl.program_id(0)
    hidden = wdown.shape[0]
    partner = {"tp": 1 - lax.axis_index("tp")}

    def swap(own, arrived, sems, t):
        return pltpu.make_async_remote_copy(
            src_ref=own.at[t],
            dst_ref=arrived.at[t],
            send_sem=sems.at[0, t],
            recv_sem=sems.at[1, t],
            device_id=partner,
            device_id_type=pl.DeviceIdType.MESH,
        )

    @pl.when(step == 0)
    def _():
        barrier = pltpu.get_barrier_semaphore()
        pl.semaphore_signal(barrier, inc=1, device_id=partner, device_id_type=pl.DeviceIdType.MESH)
        pl.semaphore_wait(barrier, 1)
        gain_sum[...] = jnp.zeros_like(gain_sum)

        def clear(i, carry):
            grads[pl.ds(pl.multiple_of(i * 128, 128), 128), :] = jnp.zeros((128, grads.shape[1]), f32)
            return carry

        lax.fori_loop(0, grads.shape[0] // 128, clear, 0)

    @pl.when(step < tiles)
    def _():
        for h in range(heads):
            at = slice(h * dv, (h + 1) * dv)
            o = local[:, at] + mm(qa[:, h * dk : (h + 1) * dk], entering[h])
            so = lax.rsqrt(jnp.mean(o * o, axis=-1, keepdims=True) + EPS)
            y_out[:, at] = (o * so * gain[0:1, :] * silu(zgate[:, at])).astype(bf16)
        part_own[step] = mm(y_out[...], wout[...]).astype(bf16)
        swap(part_own, part_in, part_sems, step).start()

    @pl.when((step >= 1) & (step <= tiles))
    def _():
        t = step - 1
        swap(part_own, part_in, part_sems, t).wait()
        r = res[...].astype(f32) + part_own[t].astype(f32) + part_in[t].astype(f32)
        r_keep[t] = r
        r_out[...] = r
        inv = lax.rsqrt(jnp.mean(r * r, axis=-1, keepdims=True) + EPS)
        n2 = (r * inv * gain_two[0:1, :]).astype(bf16)
        gp = mm(n2, wwide[:, 0:hidden])
        up = mm(n2, wwide[:, hidden : 2 * hidden])
        dhid = mm_nt(e_now[...], wdown[...])
        sig = jax.nn.sigmoid(gp)
        act = gp * sig
        hid_out[...] = (act * up).astype(bf16)
        dwide_out[:, 0:hidden] = (dhid * up * (sig * (1.0 + gp * (1.0 - sig)))).astype(bf16)
        dwide_out[:, hidden : 2 * hidden] = (dhid * act).astype(bf16)
        dn_own[t] = mm_nt(dwide_out[...], wwide[...]).astype(bf16)
        swap(dn_own, dn_in, dn_sems, t).start()
        down_out[...] = mm(hid_out[...], wdown[...]).astype(bf16)
        for lo in range(0, 2 * hidden, 2 * LANES):
            at = slice(lo, lo + 2 * LANES)
            grads[at, :] += mm_tn(dwide_out[:, at], n2)
        for lo in range(0, hidden, LANES):
            at = slice(lo, lo + LANES)
            grads[2 * hidden + lo : 2 * hidden + lo + LANES, :] += mm_tn(hid_out[:, at], e_now[...])

    @pl.when(step >= 2)
    def _():
        t = step - 2
        swap(dn_own, dn_in, dn_sems, t).wait()
        dn2 = dn_own[t].astype(f32) + dn_in[t].astype(f32)
        r = r_keep[t]
        inv = lax.rsqrt(jnp.mean(r * r, axis=-1, keepdims=True) + EPS)
        scaled = gain_two[0:1, :] * dn2
        gain_sum[0:1, :] += jnp.sum(dn2 * r * inv, axis=0, keepdims=True)
        dr = (
            e_late[...].astype(f32)
            + inv * scaled
            - r * (inv * inv * inv * jnp.mean(scaled * r, axis=-1, keepdims=True))
        )
        dr_out[...] = dr
        er_out[...] = dr.astype(bf16)
        gain_grad[...] = gain_sum[...]
        back_step(
            heads, dk, dv, step == 2,
            er_out, local_late, qa_late, entering, zgate_late, gain, wout, qeff, wkey, ktail, cum,
            dz_out, do_out, out_gain_grad, first, state, out_gain_sum,
        )

    @pl.when(step == tiles + 1)
    def _():
        long, cols = hidden // 2, grads.shape[1] // 2
        chunks = []
        for f in range(2):
            chunks += [(j * long, f * cols) for j in range(4)]
            chunks += [(2 * hidden + f * long, j * cols) for j in range(2)]

        def out_copy(c):
            return pltpu.make_async_copy(
                stage.at[c % 2], grads_out.at[pl.ds(c * long, long), :], out_sems.at[c % 2]
            )

        for c, (row, col) in enumerate(chunks):
            if c >= 2:
                out_copy(c - 2).wait()
            stage[c % 2] = grads[row : row + long, col : col + cols].astype(bf16)
            out_copy(c).start()
        for c in (len(chunks) - 2, len(chunks) - 1):
            out_copy(c).wait()


def block_rest(
    local, qa, entering, proj, gain, wout, res, e, gain_two, wwide, wdown, qeff, wkey, ktail, cum,
    heads, dk, dv, collective_id,
):
    rows, model = res.shape
    size = CHUNK
    tiles = rows // size
    hidden = wdown.shape[0]
    z_at = (2 * heads * dk + heads * dv) // (heads * dv)

    def rowwise(cols, lag, at=0):
        return pl.BlockSpec((size, cols), lambda n: (tiles - 1 - jnp.clip(n - lag, 0, tiles - 1), at))

    def kept(shape):
        return pl.BlockSpec(shape, lambda n: (0,) * len(shape), pipeline_mode=pl.Buffered(1))

    outs = [
        ((rows, heads * dv), bf16, rowwise(heads * dv, 0)),
        ((rows, model), bf16, rowwise(model, 1)),
        ((rows, model), f32, rowwise(model, 1)),
        ((rows, model), f32, rowwise(model, 2)),
        ((rows, model), bf16, rowwise(model, 2)),
        ((8, model), f32, whole((8, model))),
        ((6 * hidden, model // 2), bf16, pl.BlockSpec(memory_space=pl.ANY)),
        ((rows, heads * dv), bf16, rowwise(heads * dv, 2)),
        ((rows, heads * dv), bf16, rowwise(heads * dv, 2)),
        ((8, dv), f32, whole((8, dv))),
        ((heads, dk, dv), bf16, whole((heads, dk, dv))),
    ]
    return pl.pallas_call(
        functools.partial(block_kernel, heads, dk, dv, tiles),
        grid=(tiles + 2,),
        in_specs=[
            rowwise(heads * dv, 0),
            rowwise(heads * dk, 0),
            kept((heads, dk, dv)),
            rowwise(heads * dv, 0, z_at),
            kept((8, dv)),
            kept(wout.shape),
            rowwise(model, 1),
            rowwise(model, 1),
            kept((8, model)),
            kept(wwide.shape),
            kept(wdown.shape),
            rowwise(model, 2),
            rowwise(heads * dv, 2),
            rowwise(heads * dk, 2),
            rowwise(heads * dv, 2, z_at),
            rowwise(heads * dk, 2),
            rowwise(heads * dk, 2),
            rowwise(heads * dk, 2),
            rowwise(LANES, 2),
        ],
        out_specs=[spec for _, _, spec in outs],
        out_shape=[jax.ShapeDtypeStruct(shape, kind) for shape, kind, _ in outs],
        scratch_shapes=[pltpu.VMEM((tiles, size, model), bf16)] * 4
        + [
            pltpu.VMEM((tiles, size, model), f32),
            pltpu.VMEM((size, hidden), bf16),
            pltpu.VMEM((size, 2 * hidden), bf16),
            pltpu.VMEM((3 * hidden, model), f32),
            pltpu.VMEM((2, hidden // 2, model // 2), bf16),
            pltpu.VMEM((8, model), f32),
            pltpu.VMEM((heads, dk, dv), f32),
            pltpu.VMEM((8, dv), f32),
            pltpu.SemaphoreType.DMA((2, tiles)),
            pltpu.SemaphoreType.DMA((2, tiles)),
            pltpu.SemaphoreType.DMA((2,)),
        ],
        compiler_params=pltpu.CompilerParams(
            collective_id=collective_id,
            has_side_effects=True,
            vmem_limit_bytes=61 * MIB,
            dimension_semantics=("arbitrary",),
        ),
        cost_estimate=pl.CostEstimate(
            flops=100 * 10**9, bytes_accessed=rows * model * 40, transcendentals=rows * hidden
        ),
    )(
        local, qa, entering, proj, gain, wout, res, e, gain_two, wwide, wdown, e,
        local, qa, proj, qeff, wkey, ktail, cum,
    )


def back_step(
    heads, dk, dv, begins,
    er, local, qa, entering, zgate, gain, wout, qeff, wkey, ktail, cum,
    dz_out, do_out, gain_out, first, state, gain_sum,
):
    size = er.shape[0]

    @pl.when(begins)
    def _():
        state[...] = jnp.zeros_like(state)
        gain_sum[...] = jnp.zeros_like(gain_sum)

    dy = mm_nt(er[...], wout[...])
    ends = cum[size - 1 : size, :]
    for h in range(heads):
        at = slice(h * dv, (h + 1) * dv)
        kat = slice(h * dk, (h + 1) * dk)
        z = zgate[:, at]
        sig = jax.nn.sigmoid(z)
        act = z * sig
        o = local[:, at] + mm(qa[:, kat], entering[h])
        so = lax.rsqrt(jnp.mean(o * o, axis=-1, keepdims=True) + EPS)
        normed = o * so
        g = dy[:, at]
        scaled = gain[0:1, :] * g
        gain_sum[0:1, :] += jnp.sum(g * normed * act, axis=0, keepdims=True)
        dz_out[:, at] = (scaled * normed * (sig * (1.0 + z * (1.0 - sig)))).astype(bf16)
        back = scaled * act
        dots = jnp.mean(back * o, axis=-1, keepdims=True)
        do = (so * back - o * (so * so * so * dots)).astype(bf16)
        do_out[:, at] = do
        after = state[h]
        kept = jnp.where(ends[:, START : START + 1] == 0.0, jnp.exp(ends[:, h : h + 1]), 0.0)
        pulled = mm(ktail[:, kat], after)
        now = kept * after + mm_tn(
            jnp.concatenate([qeff[:, kat], wkey[:, kat]], axis=0),
            jnp.concatenate([do, (-pulled).astype(bf16)], axis=0),
        )
        state[h] = now
        first[h] = now.astype(bf16)
    gain_out[...] = gain_sum[...]


def grad_kernel(
    heads, dk, dv,
    proj, conv, ab, flags, cum_in, halo, taps, head, do_in, tinv, uval, wkey, states, entering, leaving,
    dproj, dab, tail_rows, head_rows, dtaps, dhead,
    state, ext, tap_sum, head_sum,
):
    step = pl.program_id(0)
    steps = pl.num_programs(0)
    size = proj.shape[0]
    width = proj.shape[1]
    every = range(heads)

    @pl.when(step == 0)
    def _():
        state[...] = leaving[...].astype(f32)
        ext[size : size + 8, :] = jnp.zeros((8, width), f32)
        tap_sum[...] = jnp.zeros_like(tap_sum)
        head_sum[...] = jnp.zeros_like(head_sum)

    @pl.when(step > 0)
    def _():
        ext[size : size + 8, :] = ext[0:8, :]

    fl = flags[...]
    raw = ab[...]
    beta_all = jax.nn.sigmoid(raw)
    cum = cum_in[...]
    gates = chunk_gates(cum, heads)
    row, col = grid_of(size, size)
    strict = row > col
    betas = [beta_all[:, heads + h : heads + h + 1] for h in every]

    cq = [conv[:, h * dk : (h + 1) * dk] for h in every]
    ck = [conv[:, (heads + h) * dk : (heads + h + 1) * dk] for h in every]
    vbase = 2 * heads * dk
    sq = [silu(c) for c in cq]
    sk = [silu(c) for c in ck]
    rq = [unit_scale(s) for s in sq]
    rk = [unit_scale(s) for s in sk]
    queries = [s * r * dk**-0.5 for s, r in zip(sq, rq)]
    keys = [s * r for s, r in zip(sk, rk)]
    q16 = [q.astype(bf16) for q in queries]
    k16 = [k.astype(bf16) for k in keys]
    kk = [mm_nt(k, k) for k in k16]
    qk = [mm_nt(q, k) for q, k in zip(q16, k16)]
    attend = [gates[h][0] * qk[h] for h in every]
    weak = [jnp.where(strict, gates[h][0] * kk[h], 0.0) for h in every]

    dsum_row = jnp.zeros((LANES, size), f32)
    dsum_col = jnp.zeros((size, LANES), f32)
    end_add = jnp.zeros((1, LANES), f32)
    dbeta_all = jnp.zeros((size, LANES), f32)
    lane = lax.broadcasted_iota(jnp.int32, (size, LANES), 1)
    lane_row = lax.broadcasted_iota(jnp.int32, (1, LANES), 1)
    sub = lax.broadcasted_iota(jnp.int32, (LANES, size), 0)

    starts, users, dos, dstates, dks16 = [], [], [], [], []
    for h in every:
        entry16 = entering[h]
        start = states[0, h, :, 0:dv].astype(f32) + mm(states[0, h, :, dv : dv + dk], entry16)
        start16 = start.astype(bf16)
        both = mm(jnp.concatenate([wkey[:, h * dk : (h + 1) * dk], k16[h]], axis=0), start16)
        starts.append((start, start16, both[size:]))
        users.append((uval[:, h * dv : (h + 1) * dv].astype(f32) - both[:size]).astype(bf16))
        dos.append(do_in[:, h * dv : (h + 1) * dv])
        dstates.append(state[h])
    d16 = [d.astype(bf16) for d in dstates]
    du = [
        mm_tn(attend[h], dos[h]) + mm(gates[h][2] * keys[h], d16[h]) for h in every
    ]
    dright = [mm_tn(tinv[:, h * size : (h + 1) * size], du[h]) for h in every]
    for h in every:
        decay, entry, tail, kept = gates[h]
        beta = betas[h]
        start, start16, recalled = starts[h]
        dr = dright[h]
        pair = jnp.concatenate([dos[h], dr.astype(bf16)], axis=0)
        wide = mm_nt(pair, jnp.concatenate([users[h], start16], axis=0))
        dattend = wide[:size, :size]
        dqe = wide[:size, size:]
        dlow = -wide[size:, :size]
        dke = -beta * wide[size:, size:]
        user_end = mm_nt(users[h], d16[h])
        state[h] = kept * dstates[h] + mm_tn(
            jnp.concatenate([entry * queries[h], -(beta * entry) * keys[h]], axis=0), pair
        )
        dqk = dattend * decay
        dkk = jnp.where(strict, dlow * decay, 0.0) * beta
        stack = jnp.concatenate([dqk, dkk], axis=0).astype(bf16)
        ahead = mm(stack, k16[h])
        behind = mm_tn(stack, jnp.concatenate([q16[h], k16[h]], axis=0))
        dq = ahead[:size] + entry * dqe
        dk_ = ahead[size:] + behind + entry * dke + tail * user_end
        base = vbase + h * dv
        cv = conv[:, base : base + dv]
        sigv = jax.nn.sigmoid(cv)
        value = cv * sigv
        ext[0:size, base : base + dv] = (beta * dr) * (sigv * (1.0 + cv * (1.0 - sigv)))
        dbeta = jnp.sum(dr * (value - entry * recalled), axis=-1, keepdims=True) + jnp.sum(
            dlow * weak[h], axis=-1, keepdims=True
        )
        lowmask = dlow * weak[h] * beta
        paired = dattend * attend[h] + lowmask
        dentry = jnp.sum(dqe * queries[h] + dke * keys[h], axis=-1, keepdims=True)
        dtail = jnp.sum(user_end * keys[h], axis=-1, keepdims=True) * tail
        dkept = jnp.sum(
            jnp.sum(start * dstates[h], axis=1, keepdims=True), axis=0, keepdims=True
        )
        col_add = jnp.sum(paired, axis=-1, keepdims=True) + dentry * entry - dtail
        dsum_col = jnp.where(lane == h, col_add, dsum_col)
        dsum_row = jnp.where(sub == h, jnp.sum(paired, axis=0, keepdims=True), dsum_row)
        end_add = jnp.where(
            lane_row == h, jnp.sum(dtail, axis=0, keepdims=True) + dkept * kept, end_add
        )
        dbeta_all = jnp.where(lane == heads + h, dbeta, dbeta_all)
        inner = jnp.sum(dq * sq[h], axis=-1, keepdims=True)
        scale = dk**-0.5 * rq[h]
        ds = scale * dq - sq[h] * (scale * rq[h] * rq[h] * inner)
        ext[0:size, h * dk : (h + 1) * dk] = ds * silu_grad(cq[h])
        inner = jnp.sum(dk_ * sk[h], axis=-1, keepdims=True)
        ds = rk[h] * dk_ - sk[h] * (rk[h] * rk[h] * rk[h] * inner)
        ext[0:size, (heads + h) * dk : (heads + h + 1) * dk] = ds * silu_grad(ck[h])

    dcum = dsum_col - jnp.transpose(dsum_row)
    final = lax.broadcasted_iota(jnp.int32, (size, LANES), 0) == size - 1
    dcum = dcum + jnp.where(final, end_add, 0.0)
    dlog = mm_hi((row <= col).astype(f32), dcum) * (1.0 - fl[:, START : START + 1])
    rate = jnp.exp(head[0:1, :])
    shifted = raw + head[1:2, :]
    dap = dlog * (-rate) * jax.nn.sigmoid(shifted)
    dbp = dbeta_all * beta_all * (1.0 - beta_all)
    dab[...] = jnp.where(lane < heads, dap, jnp.where(lane < 2 * heads, dbp, 0.0)).astype(bf16)
    head_sum[0:1, :] += jnp.sum(dlog * (-rate) * softplus(shifted), axis=0, keepdims=True)
    head_sum[1:2, :] += jnp.sum(dap, axis=0, keepdims=True)
    dhead[...] = head_sum[...]

    later = [jnp.broadcast_to(fl[:, AHEAD + s : AHEAD + s + 1], (size, LANES)) for s in (1, 2, 3)]
    for lo in range(0, width, LANES):
        at = slice(lo, lo + LANES)
        here = proj[:, at]
        own = ext[0:size, at]
        total = own * taps[3:4, at]
        tap_sum[3:4, at] += jnp.sum(own * here, axis=0, keepdims=True)
        for s in (1, 2, 3):
            moved = ext[s : s + size, at] * later[s - 1]
            total += moved * taps[3 - s : 4 - s, at]
            tap_sum[3 - s : 4 - s, at] += jnp.sum(moved * here, axis=0, keepdims=True)
        dproj[:, at] = total.astype(bf16)

        @pl.when(step == 0)
        def _():
            tail_rows[:, at] = total[size - 8 : size, :]

    @pl.when(step == steps - 1)
    def _():
        head_rows[...] = ext[0:8, :]
        sub8 = lax.broadcasted_iota(jnp.int32, (8, width), 0)
        for s in (1, 2, 3):
            ok = (sub8 < s).astype(f32) * fl[0:8, VALID + s : VALID + s + 1]
            before = pltpu.roll(halo[...], s, 0)
            tap_sum[3 - s : 4 - s, :] += jnp.sum(
                ext[0:8, :] * before * ok, axis=0, keepdims=True
            )

    dtaps[...] = tap_sum[...]


def delta_grad(
    proj, conv, flags, cum, halo, taps, head, do, tinv, uval, wkey, states, entering, leaving,
    heads, dk, dv,
):
    rows = proj.shape[0]
    size = CHUNK
    steps = rows // size
    width = 2 * heads * dk + heads * dv
    ab_at = (width + heads * dv) // LANES

    def rowwise(cols, at=0):
        return pl.BlockSpec((size, cols), lambda n: (steps - 1 - n, at))

    outs = [
        ((rows, width), bf16, rowwise(width)),
        ((rows, LANES), bf16, rowwise(LANES)),
        ((8, width), f32, whole((8, width))),
        ((8, width), f32, whole((8, width))),
        ((8, width), f32, whole((8, width))),
        ((8, LANES), f32, whole((8, LANES))),
    ]
    return pl.pallas_call(
        functools.partial(grad_kernel, heads, dk, dv),
        grid=(steps,),
        in_specs=[
            rowwise(width),
            rowwise(width),
            rowwise(LANES, ab_at),
            rowwise(LANES),
            rowwise(LANES),
            whole((8, width)),
            whole((8, width)),
            whole((8, LANES)),
            rowwise(heads * dv),
            rowwise(heads * size),
            rowwise(heads * dv),
            rowwise(heads * dk),
            pl.BlockSpec((1, heads, dk, dv + dk), lambda n: (steps - 1 - n, 0, 0, 0)),
            whole((heads, dk, dv)),
            whole((heads, dk, dv)),
        ],
        out_specs=[spec for _, _, spec in outs],
        out_shape=[jax.ShapeDtypeStruct(shape, kind) for shape, kind, _ in outs],
        scratch_shapes=[
            pltpu.VMEM((heads, dk, dv), f32),
            pltpu.VMEM((size + 8, width), f32),
            pltpu.VMEM((8, width), f32),
            pltpu.VMEM((8, LANES), f32),
        ],
        compiler_params=vmem(),
        cost_estimate=pl.CostEstimate(
            flops=rows * heads * 200 * size * (dv + dk + size),
            bytes_accessed=rows * width * 16,
            transcendentals=rows * width * 2,
        ),
    )(
        proj, conv, proj, flags, cum, halo, taps, head, do, tinv, uval, wkey, states, entering,
        leaving,
    )


def shifted(value, axis, distance):
    count = lax.axis_size(axis)
    route = [(i, i + distance) for i in range(count) if 0 <= i + distance < count]
    return lax.ppermute(value, axis, route)


def chain_kernel(forward, levels, *refs):
    if forward:
        own, out, mats, runs, arrived, kept, send_sem, recv_sem, mat_sems = refs
    else:
        own, maps, out, runs, arrived, send_sem, recv_sem = refs
    heads, dk = own.shape[:2]
    dv = out.shape[2]
    count = lax.axis_size("ctx")
    me = lax.axis_index("ctx")
    place = me if forward else count - 1 - me
    way = 1 if forward else -1
    distances = [2**j for j in range(levels)] + [1]
    behind = [2 ** (j + 1) - 1 for j in range(levels - 1)] if forward else []
    reaches = sorted(set(distances + behind))
    barrier = pltpu.get_barrier_semaphore()
    known = jnp.int32(0)
    for d in reaches:
        for sign in (1, -1):
            there = (me + sign * d >= 0) & (me + sign * d < count)
            known = known + there.astype(jnp.int32)

            @pl.when(there)
            def _(sign=sign, d=d):
                pl.semaphore_signal(
                    barrier, inc=1, device_id={"ctx": me + sign * d},
                    device_id_type=pl.DeviceIdType.MESH,
                )

    pl.semaphore_wait(barrier, known)

    def copy(j, h):
        width = dv if j >= levels - 1 else own.shape[2]
        source = own if j == 0 else runs.at[j - 1]
        return pltpu.make_async_remote_copy(
            src_ref=source.at[h, :, pl.ds(0, width)],
            dst_ref=arrived.at[j, h, :, pl.ds(0, width)],
            send_sem=send_sem.at[j, h],
            recv_sem=recv_sem.at[j, h],
            device_id={"ctx": me + way * distances[j]},
            device_id_type=pl.DeviceIdType.MESH,
        )

    def send(j, h):
        @pl.when(place + distances[j] < count)
        def _():
            copy(j, h).start()

    def mat_copy(j, h):
        return pltpu.make_async_remote_copy(
            src_ref=kept.at[j, h],
            dst_ref=kept.at[levels + j, h],
            send_sem=mat_sems.at[0, j, h],
            recv_sem=mat_sems.at[1, j, h],
            device_id={"ctx": me - behind[j]},
            device_id_type=pl.DeviceIdType.MESH,
        )

    for h in range(heads):
        send(0, h)
    for j in range(levels + 1):
        for h in range(heads):

            @pl.when(place >= distances[j])
            def _(j=j, h=h):
                copy(j, h).wait_recv()

            @pl.when(place < distances[j])
            def _(j=j, h=h):
                arrived[j, h] = jnp.zeros(arrived.shape[2:], bf16)

            if j == levels:
                out[h] = arrived[j, h, :, 0:dv]
                continue
            run = own[h] if j == 0 else runs[j - 1, h]
            if forward:
                matrix = run[:, dv:]
                width = dv if j == levels - 1 else dv + dk
                joined = mm(matrix, arrived[j, h, :, 0:width])
                runs[j, h, :, 0:dv] = (run[:, 0:dv].astype(f32) + joined[:, 0:dv]).astype(bf16)
                if j < levels - 1:
                    runs[j, h, :, dv : dv + dk] = joined[:, dv:].astype(bf16)
                    kept[j, h] = joined[:, dv:].astype(bf16)

                    @pl.when(me >= behind[j])
                    def _(j=j, h=h):
                        mat_copy(j, h).start()
            else:
                joined = mm_tn(maps[j, h], arrived[j, h])
                runs[j, h] = (run.astype(f32) + joined).astype(bf16)
            send(j + 1, h)
    for j in range(levels + 1):
        for h in range(heads):

            @pl.when(place + distances[j] < count)
            def _(j=j, h=h):
                copy(j, h).wait_send()
    if forward:
        for h in range(heads):
            mats[0, h] = own[h, :, dv:]
        for j, d in enumerate(behind):
            for h in range(heads):

                @pl.when(me + d < count)
                def _(j=j, h=h):
                    mat_copy(j, h).wait_recv()
                    mats[j + 1, h] = kept[levels + j, h]

                @pl.when(me + d >= count)
                def _(j=j, h=h):
                    mats[j + 1, h] = jnp.zeros(mats.shape[2:], bf16)

                @pl.when(me >= d)
                def _(j=j, h=h):
                    mat_copy(j, h).wait_send()


def chained(own, maps, dv, levels, collective_id):
    heads, dk, width = own.shape
    forward = maps is None
    spec = pl.BlockSpec(memory_space=pltpu.VMEM)
    shapes = [(heads, dk, dv)] + ([(levels, heads, dk, dk)] if forward else [])
    return pl.pallas_call(
        functools.partial(chain_kernel, forward, levels),
        in_specs=[spec] * (1 if forward else 2),
        out_specs=[spec] * len(shapes),
        out_shape=[jax.ShapeDtypeStruct(shape, bf16) for shape in shapes],
        scratch_shapes=[
            pltpu.VMEM((levels, heads, dk, width), bf16),
            pltpu.VMEM((levels + 1, heads, dk, width), bf16),
        ]
        + ([pltpu.VMEM((2 * levels, heads, dk, dk), bf16)] if forward else [])
        + [
            pltpu.SemaphoreType.DMA((levels + 1, heads)),
            pltpu.SemaphoreType.DMA((levels + 1, heads)),
        ]
        + ([pltpu.SemaphoreType.DMA((2, levels, heads))] if forward else []),
        compiler_params=pltpu.CompilerParams(
            collective_id=collective_id, has_side_effects=True, vmem_limit_bytes=24 * MIB
        ),
        cost_estimate=pl.CostEstimate(flops=25 * 10**9, bytes_accessed=own.size * 16, transcendentals=0),
    )(*([own] if forward else [own, maps]))


def levels_of(reach):
    levels = 1
    while 2**levels < reach:
        levels += 1
    return levels


def entering_state(own, dv, reach):
    levels = levels_of(reach)
    return chained(own, None, dv, levels, 3)


def leaving_grad(own, ahead):
    return chained(own, ahead, own.shape[2], ahead.shape[0], 4)[0]


def summed_over_tp(part):
    return added(part, over_tp(part))


def over_tp(part):
    count = lax.axis_size("tp")
    routes = [[(i, (i + d) % count) for i in range(count)] for d in range(1, count)]
    return [lax.ppermute(part, "tp", route) for route in routes]


def added(part, others):
    total = part.astype(f32)
    for other in others:
        total = total + other.astype(f32)
    return total


def swapped(value, axis, bit):
    return lax.ppermute(value, axis, [(i, i ^ bit) for i in range(lax.axis_size(axis))])


def sum_kernel(plan, *refs):
    count = len(plan)
    grads, outs = refs[:count], refs[count : 2 * count]
    refs = refs[2 * count :]
    own, fs_in, in_y, in_m, in_h, full = (refs[i * count : (i + 1) * count] for i in range(6))
    load_sem, send_sem, recv_sem = refs[6 * count :]
    fs = lax.axis_index("fs")
    me = lax.axis_index("ctx")
    y = lax.rem(me, 2)
    z = lax.div(me, 2)
    hub = lax.div(z, 2)
    inner = lax.rem(lax.div(z + 1, 2), 2)
    mate = z + 1 - 2 * lax.rem(z, 2)
    core = {"fs": 1 - fs}
    beside = {"ctx": z * 2 + 1 - y}
    paired = {"ctx": mate * 2 + y}
    across = {"ctx": (3 - z) * 2 + y}
    barrier = pltpu.get_barrier_semaphore()
    for partner in (core, beside, paired, across):
        pl.semaphore_signal(barrier, inc=1, device_id=partner, device_id_type=pl.DeviceIdType.MESH)
    pl.semaphore_wait(barrier, 4)

    segments = []
    for i, widths in enumerate(plan):
        lo = 0
        for w in widths:
            segments.append((i, slice(lo, lo + w)))
            lo += w
    total = len(segments)

    def rows(start, n):
        return pl.ds(pl.multiple_of(start, 16), n)

    def stages(g):
        i, at = segments[g]
        half = own[i].shape[0]
        q, e = half // 2, half // 4
        y_first = g % 2 == 0

        def remote(slot, src, dst, partner):
            return pltpu.make_async_remote_copy(
                src_ref=src,
                dst_ref=dst,
                send_sem=send_sem.at[g, slot],
                recv_sem=recv_sem.at[g, slot],
                device_id=partner,
                device_id_type=pl.DeviceIdType.MESH,
            )

        def moved(slot, source, target, start, n, partner):
            return remote(
                slot, source[i].at[rows(start, n), at], target[i].at[rows(start, n), at], partner
            )

        def add(target, one, two, start, n):
            step = 32 if n % 32 == 0 else 16

            def body(j, carry):
                r = rows(start + j * step, step)
                total = one[i][r, at].astype(f32) + two[i][r, at].astype(f32)
                target[i][r, at] = total.astype(target[i].dtype)
                return carry

            lax.fori_loop(0, n // step, body, 0)

        load = pltpu.make_async_copy(
            grads[i].at[rows(fs * half, half), at], own[i].at[:, at], load_sem.at[g]
        )
        unload = pltpu.make_async_copy(full[i].at[:, at], outs[i].at[:, at], load_sem.at[total + g])
        fs_copy = remote(0, grads[i].at[rows((1 - fs) * half, half), at], fs_in[i].at[:, at], core)
        if y_first:
            mine = y * q
            low_copy = moved(1, own, in_y, (1 - y) * q, q, beside)
            mate_copy = moved(2, own, in_m, mine, q, paired)
            hub_copy = moved(3, own, in_h, mine + (1 - hub) * e, e, across)
            back_hub = moved(4, full, full, mine + hub * e, e, across)
            back_low = moved(5, full, full, mine, q, beside)
            back_mate = moved(6, full, full, mine, q, paired)
        else:
            mine = hub * q
            mate_copy = moved(2, own, in_m, 0, half, paired)
            hub_copy = moved(3, own, in_h, (1 - hub) * q, q, across)
            low_copy = moved(1, own, in_y, mine + (1 - y) * e, e, beside)
            back_low = moved(5, full, full, mine + y * e, e, beside)
            back_hub = moved(4, full, full, mine, q, across)
            back_mate = moved(6, full, full, 0, half, paired)

        def begin():
            fs_copy.start()
            load.start()

        def finish():
            @pl.when(inner == 0)
            def _():
                mate_copy.wait_send()

            @pl.when(inner == 1)
            def _():
                back_mate.wait_send()

            unload.wait()

        def cores():
            load.wait()
            fs_copy.wait()
            add(own, own, fs_in, 0, half)

        if y_first:

            def s0():
                cores()
                low_copy.start()

            def s1():
                low_copy.wait()
                add(own, own, in_y, mine, q)

                @pl.when(inner == 0)
                def _():
                    mate_copy.start()

            def s2():
                @pl.when(inner == 1)
                def _():
                    mate_copy.wait_recv()
                    add(own, own, in_m, mine, q)
                    hub_copy.start()

            def s3():
                @pl.when(inner == 1)
                def _():
                    hub_copy.wait()
                    add(full, own, in_h, mine + hub * e, e)
                    back_hub.start()

            def s4():
                @pl.when(inner == 1)
                def _():
                    back_hub.wait()
                    back_mate.start()
                    back_low.start()

            def s5():
                @pl.when(inner == 0)
                def _():
                    back_mate.wait_recv()
                    back_low.start()

            def s6():
                back_low.wait()
                unload.start()

        else:

            def s0():
                cores()

                @pl.when(inner == 0)
                def _():
                    mate_copy.start()

            def s1():
                @pl.when(inner == 1)
                def _():
                    mate_copy.wait_recv()
                    add(own, own, in_m, 0, half)
                    hub_copy.start()

            def s2():
                @pl.when(inner == 1)
                def _():
                    hub_copy.wait()
                    add(own, own, in_h, mine, q)
                    low_copy.start()

            def s3():
                @pl.when(inner == 1)
                def _():
                    low_copy.wait()
                    add(full, own, in_y, mine + y * e, e)
                    back_low.start()

            def s4():
                @pl.when(inner == 1)
                def _():
                    back_low.wait()
                    back_hub.start()

            def s5():
                @pl.when(inner == 1)
                def _():
                    back_hub.wait()
                    back_mate.start()
                    unload.start()

            def s6():
                @pl.when(inner == 0)
                def _():
                    back_mate.wait_recv()
                    unload.start()

        return begin, (s0, s1, s2, s3, s4, s5, s6), finish

    work = [stages(g) for g in range(total)]
    for begin, _, _ in work:
        begin()
    for t in range(total + 6):
        for stage in range(7):
            if 0 <= t - stage < total:
                work[t - stage][1][stage]()
    for _, _, finish in work:
        finish()


def segment_widths(cols, rows, target=128 * 1024):
    tiles = cols // LANES
    parts = max(1, min(tiles, round(rows * cols / target)))
    return tuple((tiles * (j + 1) // parts - tiles * j // parts) * LANES for j in range(parts))


def reduced(grads, collective_id, micros):
    if lax.axis_size("ctx") != 8 or lax.axis_size("fs") != 2:
        parts = [lax.psum_scatter(g, "fs", scatter_dimension=0, tiled=True) for g in grads]
        return [lax.psum(part, "ctx") for part in parts]
    shapes = [(g.shape[0] // 2, g.shape[1]) for g in grads]
    plan = tuple(segment_widths(cols, half) for half, cols in shapes)
    total = sum(len(widths) for widths in plan)
    return pl.pallas_call(
        functools.partial(sum_kernel, plan),
        in_specs=[pl.BlockSpec(memory_space=pl.ANY)] * len(grads),
        out_specs=[pl.BlockSpec(memory_space=pl.ANY)] * len(grads),
        out_shape=[jax.ShapeDtypeStruct(shape, g.dtype) for shape, g in zip(shapes, grads)],
        scratch_shapes=[pltpu.VMEM(shape, g.dtype) for shape, g in zip(shapes, grads)] * 6
        + [
            pltpu.SemaphoreType.DMA((2 * total,)),
            pltpu.SemaphoreType.DMA((total, 7)),
            pltpu.SemaphoreType.DMA((total, 7)),
        ],
        compiler_params=pltpu.CompilerParams(
            collective_id=collective_id, has_side_effects=True, vmem_limit_bytes=56 * MIB
        ),
        cost_estimate=pl.CostEstimate(
            flops=micros * 10**9, bytes_accessed=4 * sum(g.size for g in grads), transcendentals=0
        ),
    )(*grads)


def scattered(grad):
    return lax.psum_scatter(grad, ("fs", "ctx"), scatter_dimension=0, tiled=True)


def per_device(
    tokens, cotangent, lengths, order, mixer_gain, w_query, w_key, w_value, w_outgate, w_decay,
    w_beta, conv_query, conv_key, conv_value, decay_log, decay_bias, out_gain, w_output, mlp_gain,
    w_gate, w_up, w_down,
):
    rows, model = tokens.shape[1:]
    ctx = lax.axis_size("ctx")
    fs = lax.axis_size("fs")
    me = lax.axis_index("ctx")
    heads = decay_log.shape[0]
    dk = w_query.shape[1] // heads
    dv = w_value.shape[1] // heads
    key_cols, value_cols = heads * dk, heads * dv
    width = 2 * key_cols + value_cols
    hidden_cols = w_gate.shape[1]
    total = order.shape[1]
    peer = rows // ctx
    halo_rows = TAPS - 1
    sequences = lengths.shape[1]
    longest = 2 * total // (sequences + 1)
    reach = min(ctx - 1, -(-longest // rows))

    order_row = order[0]
    source_all = order_row // rows
    mine = (source_all == me).reshape(ctx, rows)
    upto = (jnp.arange(rows)[:, None] <= jnp.arange(rows)[None, :]).astype(bf16)
    rank_all = jnp.dot(mine.astype(bf16), upto, preferred_element_type=f32).astype(jnp.int32) - 1
    slots = jnp.arange(peer, dtype=jnp.int32)
    picked = mine[:, None, :] & (rank_all[:, None, :] == slots[None, :, None])
    local_all = (order_row - me * rows).reshape(ctx, 1, rows)
    send_order = jnp.sum(jnp.where(picked, local_all, 0), axis=2).reshape(rows)
    given = lax.dynamic_slice_in_dim(order_row, me * rows, rows)
    source = given // rows
    from_each = source[None, :] == jnp.arange(ctx, dtype=jnp.int32)[:, None]
    rank_here = jnp.dot(from_each.astype(bf16), upto, preferred_element_type=f32) - 1.0
    rank_here = jnp.sum(jnp.where(from_each, rank_here, 0.0), axis=0).astype(jnp.int32)
    recv_slot = source * peer + rank_here
    iota = jnp.arange(rows, dtype=jnp.int32)
    gather_send = (send_order[:, None] == iota[None, :]).astype(bf16)
    gather_recv = (recv_slot[:, None] == iota[None, :]).astype(bf16)

    def moved(maps, values, transposed=False):
        return lax.dot_general(
            maps, values, (((0 if transposed else 1,), (0,)), ((), ())), preferred_element_type=f32
        ).astype(bf16)

    def exchanged(values):
        return lax.all_to_all(values, "ctx", split_axis=0, concat_axis=0, tiled=True)

    sent = moved(gather_send, tokens[0])
    offsets = jnp.cumsum(lengths[0]) - lengths[0]
    positions = me * rows - halo_rows + jnp.arange(rows + 2 * halo_rows, dtype=jnp.int32)
    number = jnp.sum((offsets[None, :] <= positions[:, None]).astype(jnp.int32), axis=1)
    here = number[halo_rows : halo_rows + rows]
    fresh = jnp.any(offsets[None, :] == positions[halo_rows : halo_rows + rows, None], axis=1)
    columns = [jnp.zeros((rows,), f32)] * START + [fresh.astype(f32)]
    for s in range(1, TAPS):
        columns.append((number[halo_rows - s : halo_rows - s + rows] == here).astype(f32))
    for s in range(1, TAPS):
        columns.append((number[halo_rows + s : halo_rows + s + rows] == here).astype(f32))
    flags = jnp.stack(columns, axis=1)
    flags = jnp.pad(flags, ((0, 0), (0, LANES - flags.shape[1])))

    pad = jnp.zeros((w_decay.shape[0], LANES - 2 * heads), bf16)
    w_in = jnp.concatenate([w_query, w_key, w_value, w_outgate, w_decay, w_beta, pad], axis=1)
    sent, w_in = lax.optimization_barrier((sent, w_in))
    w_in = lax.all_gather(w_in, "fs", axis=0, tiled=True)
    resident = moved(gather_recv, exchanged(sent))
    w_wide = lax.all_gather(jnp.concatenate([w_gate, w_up], axis=1), "fs", axis=0, tiled=True)
    w_down = lax.all_gather(w_down, "fs", axis=0, tiled=True)
    w_output = lax.all_gather(w_output, "fs", axis=0, tiled=True)
    small = jnp.concatenate(
        [
            conv_query.T.reshape(-1),
            conv_key.T.reshape(-1),
            conv_value.T.reshape(-1),
            mixer_gain,
            mlp_gain,
            out_gain,
        ]
    )
    small = lax.all_gather(small, "fs", axis=0).astype(f32)
    pieces, at = [], 0
    for channels in (conv_query.shape[0], conv_key.shape[0], conv_value.shape[0]):
        part = small[:, at : at + TAPS * channels].reshape(fs, TAPS, channels)
        pieces.append(part.transpose(1, 0, 2).reshape(TAPS, fs * channels))
        at += TAPS * channels
    taps = jnp.pad(jnp.concatenate(pieces, axis=1), ((0, 8 - TAPS), (0, 0)))
    gains = []
    for size in (mixer_gain.shape[0], mlp_gain.shape[0], out_gain.shape[0]):
        gains.append(small[:, at : at + size].reshape(-1))
        at += size
    gain_one, gain_two, gain_out = gains
    gain_rows = jnp.broadcast_to(gain_out[None, :], (8, dv))
    head = jnp.pad(
        jnp.stack([decay_log, decay_bias]), ((0, 6), (0, LANES - heads))
    )

    x = resident.astype(f32)
    inv_one = lax.rsqrt(jnp.mean(x * x, axis=-1, keepdims=True) + EPS)
    n1 = (x * inv_one * gain_one).astype(bf16)
    proj = jnp.dot(n1, w_in, preferred_element_type=f32)
    halo = shifted(proj[rows - 8 :, :width], "ctx", 1)
    conv, local, qa, states, tinv, uval, wkey, qeff, ktail, cum, last = delta_forward(
        proj, flags, halo, taps, head, heads, dk, dv
    )
    last, arrived = lax.optimization_barrier((last, exchanged(moved(gather_send, cotangent[0]))))
    e = moved(gather_recv, arrived)
    entering, ahead = entering_state(last, dv, reach)
    y1, down, r, dr, er, mlp_gain_sum, mlp_cat, dz, do, dgain_out, first = block_rest(
        local, qa, entering, proj, gain_rows, w_output, resident, e,
        jnp.broadcast_to(gain_two[None, :], (8, model)), w_wide, w_down, qeff, wkey, ktail, cum,
        heads, dk, dv, 2,
    )
    grad_mlp_gain = mlp_gain_sum[0]

    def outer(a, b):
        return lax.dot_general(
            a, b, (((0,), (0,)), ((), ())), preferred_element_type=f32
        ).astype(bf16)

    def halves(grad):
        return grad.reshape(fs, grad.shape[0] // fs, *grad.shape[1:])

    half = model // fs
    down_rows = hidden_cols // fs
    mlp_share = scattered(mlp_cat)

    leaving = leaving_grad(first, ahead)
    dproj, dab, tail_rows, head_rows, dtaps, dhead = delta_grad(
        proj, conv, flags, cum, halo, taps, head, do, tinv, uval, wkey, states, entering, leaving,
        heads, dk, dv,
    )
    dproj, down_other = lax.optimization_barrier((dproj, over_tp(down)))
    next_rows = shifted(head_rows, "ctx", -1)
    extra = jnp.zeros_like(tail_rows)
    for s in range(1, TAPS):
        part_s = jnp.concatenate([jnp.zeros((8 - s, width), f32), next_rows[:s]], axis=0)
        extra = extra + part_s * taps[TAPS - 1 - s] * flags[rows - 8 :, AHEAD + s][:, None]
    dproj = lax.dynamic_update_slice(dproj, (tail_rows + extra).astype(bf16), (rows - 8, 0))
    dall = jnp.concatenate([dproj, dz, dab], axis=1)
    dn1 = lax.dot_general(dall, w_in, (((1,), (1,)), ((), ())), preferred_element_type=f32)
    dn1_own, dz, y1, down_other = lax.optimization_barrier(
        (dn1.astype(bf16), dz, y1, down_other)
    )
    dn1_other = over_tp(dn1_own)
    g_in = outer(n1, jnp.concatenate([dproj, dab], axis=1))
    g_z = outer(n1, dz)
    g_o = outer(y1, er)
    g_in, mlp_share = lax.optimization_barrier((g_in, mlp_share))
    g_mlp_all = lax.all_gather(mlp_share, "ctx", axis=0, tiled=True)
    result = (r + added(down, down_other)).astype(bf16)
    block_rows = exchanged(moved(gather_recv, result, True))
    def tap_part(lo, channels):
        return dtaps[:TAPS, lo : lo + channels].reshape(TAPS, fs, -1).transpose(1, 0, 2).reshape(fs, -1)

    share = jnp.sum(dgain_out, axis=0)
    rates = jnp.broadcast_to(dhead[:2, :heads].reshape(1, 2 * heads), (fs, 2 * heads))
    own_mixer_gain = jnp.sum(dn1_own.astype(f32) * x * inv_one, axis=0)
    little = jnp.concatenate(
        [
            tap_part(0, key_cols),
            tap_part(key_cols, key_cols),
            tap_part(2 * key_cols, value_cols),
            halves(own_mixer_gain),
            halves(grad_mlp_gain),
            halves(share),
            rates,
        ],
        axis=1,
    )
    little_rows = -(-little.shape[1] // (64 * LANES)) * 64
    little = jnp.pad(little, ((0, 0), (0, little_rows * LANES - little.shape[1])))
    little = little.reshape(fs * little_rows, LANES)
    little, g_in, g_z, g_o = reduced([little, g_in, g_z, g_o], 1, 110)
    dn1_other, block_rows, little, g_in, g_z, g_o = lax.optimization_barrier(
        (dn1_other, block_rows, little, g_in, g_z, g_o)
    )
    dn1 = added(dn1_own, dn1_other)
    little = little.reshape(-1)
    unit = jnp.eye(hidden_cols, dtype=bf16)
    g_gate, g_up = (
        lax.dot_general(
            g_mlp_all[lo : lo + hidden_cols], unit, (((0,), (0,)), ((), ())),
            preferred_element_type=f32,
        )
        for lo in (0, hidden_cols)
    )
    g_down = g_mlp_all[2 * hidden_cols :].reshape(fs, down_rows, half)
    g_down = jnp.concatenate([g_down[j] for j in range(fs)], axis=1)
    scaled = gain_one * dn1
    grad_in = (
        dr
        + inv_one * scaled
        - x * (inv_one * inv_one * inv_one * jnp.mean(scaled * x, axis=-1, keepdims=True))
    ).astype(bf16)
    token_rows = exchanged(moved(gather_recv, grad_in, True))

    taken, at = [], 0
    for channels in (conv_query.shape[0], conv_key.shape[0], conv_value.shape[0]):
        taken.append(little[at : at + TAPS * channels].reshape(TAPS, channels).T)
        at += TAPS * channels
    for size in (mixer_gain.shape[0], mlp_gain.shape[0], out_gain.shape[0], heads, heads):
        taken.append(little[at : at + size])
        at += size
    g_cq, g_ck, g_cv, g_mixer, g_mlp, g_out_gain, g_log, g_bias = taken
    ends_tp = summed_over_tp(jnp.concatenate([g_mixer, g_out_gain]))
    g_mixer, g_out_gain = ends_tp[: g_mixer.shape[0]], ends_tp[g_mixer.shape[0] :]
    ends = [key_cols, 2 * key_cols, width, width + heads]
    g_query, g_key, g_value, g_decay, g_beta = (
        g_in[:, lo:hi].astype(f32) for lo, hi in zip([0] + ends, ends + [ends[-1] + heads])
    )
    outs = (
        moved(gather_send, block_rows, True)[None],
        g_mixer,
        g_query,
        g_key,
        g_value,
        g_z.astype(f32),
        g_decay,
        g_beta,
        g_cq,
        g_ck,
        g_cv,
        g_log,
        g_bias,
        g_out_gain,
        g_o.astype(f32),
        g_mlp,
        g_gate,
        g_up,
        g_down.astype(f32),
    )
    token_rows, outs = lax.optimization_barrier((token_rows, outs))
    grad_tokens = moved(gather_send, token_rows, True)[None]
    return (outs[0], grad_tokens) + outs[1:]


def solution(mesh):
    split = P("fs", "ctx", None)
    cols = P("fs", "tp")
    both = P(("tp", "fs"), None)
    in_specs = (
        split, split, P("fs", None), P("fs", None), P("fs"),
        cols, cols, cols, cols, cols, cols,
        both, both, both, P("tp"), P("tp"), P("fs"), both, P("fs"), cols, cols, both,
    )
    out_specs = (
        split, split, P("fs"),
        cols, cols, cols, cols, cols, cols,
        both, both, both, P("tp"), P("tp"), P("fs"), both, P("fs"), cols, cols, both,
    )
    return jax.shard_map(
        per_device, mesh=mesh, in_specs=in_specs, out_specs=out_specs, check_vma=False
    )
```

```python
import functools

import jax
import jax.numpy as jnp
from jax import lax
from jax.experimental import pallas as pl
from jax.experimental.pallas import tpu as pltpu
from jax.sharding import PartitionSpec as P

TAPS = 4
CHUNK = 128
EPS = 1e-6
LANES = 128
START, VALID, AHEAD = 8, 8, 11
HI = lax.Precision.HIGHEST
bf16 = jnp.bfloat16
f32 = jnp.float32
MIB = 1024 * 1024


def mm(a, b):
    return jnp.dot(a.astype(bf16), b.astype(bf16), preferred_element_type=f32)


def mm_nt(a, b):
    return lax.dot_general(
        a.astype(bf16), b.astype(bf16), (((1,), (1,)), ((), ())), preferred_element_type=f32
    )


def mm_tn(a, b):
    return lax.dot_general(
        a.astype(bf16), b.astype(bf16), (((0,), (0,)), ((), ())), preferred_element_type=f32
    )


def mm_hi(a, b):
    return jnp.dot(a, b, precision=HI, preferred_element_type=f32)


def silu(x):
    return x * jax.nn.sigmoid(x)


def silu_grad(x):
    s = jax.nn.sigmoid(x)
    return s * (1.0 + x * (1.0 - s))


def softplus(x):
    return jnp.maximum(x, 0.0) + jnp.log1p(jnp.exp(-jnp.abs(x)))


def grid_of(rows, cols):
    return (
        lax.broadcasted_iota(jnp.int32, (rows, cols), 0),
        lax.broadcasted_iota(jnp.int32, (rows, cols), 1),
    )


def lower_inverses(systems):
    size = systems[0].shape[0]
    row, col = grid_of(size, size)
    eye = (row == col).astype(f32)
    first = ((row >> 1) == (col >> 1)) & (row > col)
    inverses = [eye - jnp.where(first, low, 0.0) for low in systems]
    level = 1
    while (1 << level) < size:
        block = (
            ((row >> (level + 1)) == (col >> (level + 1)))
            & (((row >> level) & 1) == 1)
            & (((col >> level) & 1) == 0)
        )
        parts = [mm(jnp.where(block, low, 0.0), inv) for low, inv in zip(systems, inverses)]
        inverses = [inv - mm(inv, part) for inv, part in zip(inverses, parts)]
        level += 1
    return inverses


def chunk_gates(cum, heads):
    size = cum.shape[0]
    row, col = grid_of(size, size)
    across = jnp.transpose(cum)
    seg_col = cum[:, START : START + 1]
    linked = (row >= col) & (seg_col == across[START : START + 1, :])
    from_start = seg_col == 0.0
    to_end = seg_col == cum[size - 1 : size, START : START + 1]
    out = []
    for h in range(heads):
        down = cum[:, h : h + 1]
        gap = jnp.where(linked, down - across[h : h + 1, :], 0.0)
        decay = jnp.where(linked, jnp.exp(gap), 0.0)
        entry = jnp.where(from_start, jnp.exp(down), 0.0)
        last = cum[size - 1 : size, h : h + 1]
        tail = jnp.where(to_end, jnp.exp(jnp.where(to_end, last - down, 0.0)), 0.0)
        out.append((decay, entry, tail, entry[size - 1 : size, :]))
    return out


def unit_scale(x):
    return lax.rsqrt(jnp.sum(x * x, axis=-1, keepdims=True) + EPS)


def forward_kernel(
    heads, dk, dv,
    proj, ab, flags, halo, taps, head,
    conv, local, qa, states, tinv, uval, wkey, qeff, ktail, cum_out, last,
    ext, state,
):
    step = pl.program_id(0)
    size = proj.shape[0]
    width = proj.shape[1]

    @pl.when(step == 0)
    def _():
        ext[0:8, :] = halo[...]
        row, col = grid_of(dk, dk)
        for h in range(heads):
            state[h, :, 0:dv] = jnp.zeros((dk, dv), f32)
            state[h, :, dv : dv + dk] = (row == col).astype(f32)

    @pl.when(step > 0)
    def _():
        ext[0:8, :] = ext[size : size + 8, :]

    ext[8 : 8 + size, :] = proj[...]
    fl = flags[...]
    valid = [jnp.broadcast_to(fl[:, VALID + s : VALID + s + 1], (size, LANES)) for s in (1, 2, 3)]
    for lo in range(0, width, LANES):
        at = slice(lo, lo + LANES)
        total = ext[8 : 8 + size, at] * taps[3:4, at]
        for s in (1, 2, 3):
            total += ext[8 - s : 8 - s + size, at] * taps[3 - s : 4 - s, at] * valid[s - 1]
        conv[:, at] = total

    raw = ab[...]
    lane = lax.broadcasted_iota(jnp.int32, (size, LANES), 1)
    log_decay = -jnp.exp(head[0:1, :]) * softplus(raw + head[1:2, :])
    row, col = grid_of(size, size)
    cum = mm_hi((row >= col).astype(f32), jnp.where(lane < heads, log_decay, fl))
    cum_out[...] = cum
    beta_all = jax.nn.sigmoid(raw)
    gates = chunk_gates(cum, heads)

    every = range(heads)
    betas = [beta_all[:, heads + h : heads + h + 1] for h in every]
    queries, keys, values = [], [], []
    for h in every:
        q = silu(conv[:, h * dk : (h + 1) * dk])
        k = silu(conv[:, (heads + h) * dk : (heads + h + 1) * dk])
        base = 2 * heads * dk + h * dv
        queries.append(q * unit_scale(q) * dk**-0.5)
        keys.append(k * unit_scale(k))
        values.append(silu(conv[:, base : base + dv]))
    keys16 = [k.astype(bf16) for k in keys]
    kk = [mm_nt(k, k) for k in keys16]
    qk = [mm_nt(q, k) for q, k in zip(queries, keys16)]
    strict = row > col
    systems = [jnp.where(strict, betas[h] * gates[h][0] * kk[h], 0.0) for h in every]
    inverses = lower_inverses(systems)
    solved = []
    for h in every:
        right = jnp.concatenate([betas[h] * values[h], (betas[h] * gates[h][1]) * keys[h]], axis=1)
        solved.append(mm(inverses[h], right))
    mixed = [mm(gates[h][0] * qk[h], solved[h]) for h in every]
    for h in every:
        before = state[h]
        before16 = before.astype(bf16)
        states[0, h] = before16
        w = solved[h][:, dv:].astype(bf16)
        q_now = (gates[h][1] * queries[h] - mixed[h][:, dv:]).astype(bf16)
        k_end = (gates[h][2] * keys[h]).astype(bf16)
        both = mm(jnp.concatenate([q_now, w], axis=0), before16)
        local[:, h * dv : (h + 1) * dv] = mixed[h][:, :dv] + both[:size, :dv]
        qa[:, h * dk : (h + 1) * dk] = both[:size, dv:].astype(bf16)
        fed = jnp.concatenate(
            [solved[h][:, :dv] - both[size:, :dv], -both[size:, dv:]], axis=1
        )
        after = gates[h][3] * before + mm_tn(k_end, fed)
        state[h] = after
        last[h] = after.astype(bf16)
        tinv[:, h * size : (h + 1) * size] = inverses[h].astype(bf16)
        uval[:, h * dv : (h + 1) * dv] = solved[h][:, :dv].astype(bf16)
        wkey[:, h * dk : (h + 1) * dk] = w
        qeff[:, h * dk : (h + 1) * dk] = q_now
        ktail[:, h * dk : (h + 1) * dk] = k_end


def vmem(limit=56):
    return pltpu.CompilerParams(vmem_limit_bytes=limit * MIB, dimension_semantics=("arbitrary",))


def whole(shape):
    return pl.BlockSpec(shape, lambda n: (0,) * len(shape))


def delta_forward(proj, flags, halo, taps, head, heads, dk, dv):
    rows = proj.shape[0]
    size = CHUNK
    steps = rows // size
    width = 2 * heads * dk + heads * dv
    ab_at = (width + heads * dv) // LANES

    def rowwise(cols):
        return pl.BlockSpec((size, cols), lambda n: (n, 0))

    outs = [
        ((rows, width), f32, rowwise(width)),
        ((rows, heads * dv), f32, rowwise(heads * dv)),
        ((rows, heads * dk), bf16, rowwise(heads * dk)),
        ((steps, heads, dk, dv + dk), bf16, pl.BlockSpec((1, heads, dk, dv + dk), lambda n: (n, 0, 0, 0))),
        ((rows, heads * size), bf16, rowwise(heads * size)),
        ((rows, heads * dv), bf16, rowwise(heads * dv)),
        ((rows, heads * dk), bf16, rowwise(heads * dk)),
        ((rows, heads * dk), bf16, rowwise(heads * dk)),
        ((rows, heads * dk), bf16, rowwise(heads * dk)),
        ((rows, LANES), f32, rowwise(LANES)),
        ((heads, dk, dv + dk), bf16, whole((heads, dk, dv + dk))),
    ]
    return pl.pallas_call(
        functools.partial(forward_kernel, heads, dk, dv),
        grid=(steps,),
        in_specs=[
            rowwise(width),
            pl.BlockSpec((size, LANES), lambda n: (n, ab_at)),
            rowwise(LANES),
            whole((8, width)),
            whole((8, width)),
            whole((8, LANES)),
        ],
        out_specs=[spec for _, _, spec in outs],
        out_shape=[jax.ShapeDtypeStruct(shape, kind) for shape, kind, _ in outs],
        scratch_shapes=[
            pltpu.VMEM((size + 8, width), f32),
            pltpu.VMEM((heads, dk, dv + dk), f32),
        ],
        compiler_params=vmem(),
        cost_estimate=pl.CostEstimate(
            flops=rows * heads * 40 * size * (dv + dk + size + size),
            bytes_accessed=rows * width * 14,
            transcendentals=rows * width * 2,
        ),
    )(proj, proj, flags, halo, taps, head)


def block_kernel(
    heads, dk, dv, tiles,
    local, qa, entering, zgate, gain, wout, res, e_now, gain_two, wwide, wdown, e_late,
    local_late, qa_late, zgate_late, qeff, wkey, ktail, cum,
    y_out, down_out, r_out, dr_out, er_out, gain_grad, grads_out,
    dz_out, do_out, out_gain_grad, first,
    part_own, part_in, dn_own, dn_in, r_keep, hid_out, dwide_out, grads, stage, gain_sum,
    state, out_gain_sum, part_sems, dn_sems, out_sems,
):
    step = pl.program_id(0)
    hidden = wdown.shape[0]
    partner = {"tp": 1 - lax.axis_index("tp")}

    def swap(own, arrived, sems, t):
        return pltpu.make_async_remote_copy(
            src_ref=own.at[t],
            dst_ref=arrived.at[t],
            send_sem=sems.at[0, t],
            recv_sem=sems.at[1, t],
            device_id=partner,
            device_id_type=pl.DeviceIdType.MESH,
        )

    @pl.when(step == 0)
    def _():
        barrier = pltpu.get_barrier_semaphore()
        pl.semaphore_signal(barrier, inc=1, device_id=partner, device_id_type=pl.DeviceIdType.MESH)
        pl.semaphore_wait(barrier, 1)
        gain_sum[...] = jnp.zeros_like(gain_sum)

        def clear(i, carry):
            grads[pl.ds(pl.multiple_of(i * 128, 128), 128), :] = jnp.zeros((128, grads.shape[1]), f32)
            return carry

        lax.fori_loop(0, grads.shape[0] // 128, clear, 0)

    @pl.when(step < tiles)
    def _():
        for h in range(heads):
            at = slice(h * dv, (h + 1) * dv)
            o = local[:, at] + mm(qa[:, h * dk : (h + 1) * dk], entering[h])
            so = lax.rsqrt(jnp.mean(o * o, axis=-1, keepdims=True) + EPS)
            y_out[:, at] = (o * so * gain[0:1, :] * silu(zgate[:, at])).astype(bf16)
        part_own[step] = mm(y_out[...], wout[...]).astype(bf16)
        swap(part_own, part_in, part_sems, step).start()

    @pl.when((step >= 1) & (step <= tiles))
    def _():
        t = step - 1
        swap(part_own, part_in, part_sems, t).wait()
        r = res[...].astype(f32) + part_own[t].astype(f32) + part_in[t].astype(f32)
        r_keep[t] = r
        r_out[...] = r
        inv = lax.rsqrt(jnp.mean(r * r, axis=-1, keepdims=True) + EPS)
        n2 = (r * inv * gain_two[0:1, :]).astype(bf16)
        gp = mm(n2, wwide[:, 0:hidden])
        up = mm(n2, wwide[:, hidden : 2 * hidden])
        dhid = mm_nt(e_now[...], wdown[...])
        sig = jax.nn.sigmoid(gp)
        act = gp * sig
        hid_out[...] = (act * up).astype(bf16)
        dwide_out[:, 0:hidden] = (dhid * up * (sig * (1.0 + gp * (1.0 - sig)))).astype(bf16)
        dwide_out[:, hidden : 2 * hidden] = (dhid * act).astype(bf16)
        dn_own[t] = mm_nt(dwide_out[...], wwide[...]).astype(bf16)
        swap(dn_own, dn_in, dn_sems, t).start()
        down_out[...] = mm(hid_out[...], wdown[...]).astype(bf16)
        for lo in range(0, 2 * hidden, 2 * LANES):
            at = slice(lo, lo + 2 * LANES)
            grads[at, :] += mm_tn(dwide_out[:, at], n2)
        for lo in range(0, hidden, LANES):
            at = slice(lo, lo + LANES)
            grads[2 * hidden + lo : 2 * hidden + lo + LANES, :] += mm_tn(hid_out[:, at], e_now[...])

    @pl.when(step >= 2)
    def _():
        t = step - 2
        swap(dn_own, dn_in, dn_sems, t).wait()
        dn2 = dn_own[t].astype(f32) + dn_in[t].astype(f32)
        r = r_keep[t]
        inv = lax.rsqrt(jnp.mean(r * r, axis=-1, keepdims=True) + EPS)
        scaled = gain_two[0:1, :] * dn2
        gain_sum[0:1, :] += jnp.sum(dn2 * r * inv, axis=0, keepdims=True)
        dr = (
            e_late[...].astype(f32)
            + inv * scaled
            - r * (inv * inv * inv * jnp.mean(scaled * r, axis=-1, keepdims=True))
        )
        dr_out[...] = dr
        er_out[...] = dr.astype(bf16)
        gain_grad[...] = gain_sum[...]
        back_step(
            heads, dk, dv, step == 2,
            er_out, local_late, qa_late, entering, zgate_late, gain, wout, qeff, wkey, ktail, cum,
            dz_out, do_out, out_gain_grad, first, state, out_gain_sum,
        )

    @pl.when(step == tiles + 1)
    def _():
        long, cols = hidden // 2, grads.shape[1] // 2
        chunks = []
        for f in range(2):
            chunks += [(j * long, f * cols) for j in range(4)]
            chunks += [(2 * hidden + f * long, j * cols) for j in range(2)]

        def out_copy(c):
            return pltpu.make_async_copy(
                stage.at[c % 2], grads_out.at[pl.ds(c * long, long), :], out_sems.at[c % 2]
            )

        for c, (row, col) in enumerate(chunks):
            if c >= 2:
                out_copy(c - 2).wait()
            stage[c % 2] = grads[row : row + long, col : col + cols].astype(bf16)
            out_copy(c).start()
        for c in (len(chunks) - 2, len(chunks) - 1):
            out_copy(c).wait()


def block_rest(
    local, qa, entering, proj, gain, wout, res, e, gain_two, wwide, wdown, qeff, wkey, ktail, cum,
    heads, dk, dv, collective_id,
):
    rows, model = res.shape
    size = CHUNK
    tiles = rows // size
    hidden = wdown.shape[0]
    z_at = (2 * heads * dk + heads * dv) // (heads * dv)

    def rowwise(cols, lag, at=0):
        return pl.BlockSpec((size, cols), lambda n: (tiles - 1 - jnp.clip(n - lag, 0, tiles - 1), at))

    def kept(shape):
        return pl.BlockSpec(shape, lambda n: (0,) * len(shape), pipeline_mode=pl.Buffered(1))

    outs = [
        ((rows, heads * dv), bf16, rowwise(heads * dv, 0)),
        ((rows, model), bf16, rowwise(model, 1)),
        ((rows, model), f32, rowwise(model, 1)),
        ((rows, model), f32, rowwise(model, 2)),
        ((rows, model), bf16, rowwise(model, 2)),
        ((8, model), f32, whole((8, model))),
        ((6 * hidden, model // 2), bf16, pl.BlockSpec(memory_space=pl.ANY)),
        ((rows, heads * dv), bf16, rowwise(heads * dv, 2)),
        ((rows, heads * dv), bf16, rowwise(heads * dv, 2)),
        ((8, dv), f32, whole((8, dv))),
        ((heads, dk, dv), bf16, whole((heads, dk, dv))),
    ]
    return pl.pallas_call(
        functools.partial(block_kernel, heads, dk, dv, tiles),
        grid=(tiles + 2,),
        in_specs=[
            rowwise(heads * dv, 0),
            rowwise(heads * dk, 0),
            kept((heads, dk, dv)),
            rowwise(heads * dv, 0, z_at),
            kept((8, dv)),
            kept(wout.shape),
            rowwise(model, 1),
            rowwise(model, 1),
            kept((8, model)),
            kept(wwide.shape),
            kept(wdown.shape),
            rowwise(model, 2),
            rowwise(heads * dv, 2),
            rowwise(heads * dk, 2),
            rowwise(heads * dv, 2, z_at),
            rowwise(heads * dk, 2),
            rowwise(heads * dk, 2),
            rowwise(heads * dk, 2),
            rowwise(LANES, 2),
        ],
        out_specs=[spec for _, _, spec in outs],
        out_shape=[jax.ShapeDtypeStruct(shape, kind) for shape, kind, _ in outs],
        scratch_shapes=[pltpu.VMEM((tiles, size, model), bf16)] * 4
        + [
            pltpu.VMEM((tiles, size, model), f32),
            pltpu.VMEM((size, hidden), bf16),
            pltpu.VMEM((size, 2 * hidden), bf16),
            pltpu.VMEM((3 * hidden, model), f32),
            pltpu.VMEM((2, hidden // 2, model // 2), bf16),
            pltpu.VMEM((8, model), f32),
            pltpu.VMEM((heads, dk, dv), f32),
            pltpu.VMEM((8, dv), f32),
            pltpu.SemaphoreType.DMA((2, tiles)),
            pltpu.SemaphoreType.DMA((2, tiles)),
            pltpu.SemaphoreType.DMA((2,)),
        ],
        compiler_params=pltpu.CompilerParams(
            collective_id=collective_id,
            has_side_effects=True,
            vmem_limit_bytes=61 * MIB,
            dimension_semantics=("arbitrary",),
        ),
        cost_estimate=pl.CostEstimate(
            flops=100 * 10**9, bytes_accessed=rows * model * 40, transcendentals=rows * hidden
        ),
    )(
        local, qa, entering, proj, gain, wout, res, e, gain_two, wwide, wdown, e,
        local, qa, proj, qeff, wkey, ktail, cum,
    )


def back_step(
    heads, dk, dv, begins,
    er, local, qa, entering, zgate, gain, wout, qeff, wkey, ktail, cum,
    dz_out, do_out, gain_out, first, state, gain_sum,
):
    size = er.shape[0]

    @pl.when(begins)
    def _():
        state[...] = jnp.zeros_like(state)
        gain_sum[...] = jnp.zeros_like(gain_sum)

    dy = mm_nt(er[...], wout[...])
    ends = cum[size - 1 : size, :]
    for h in range(heads):
        at = slice(h * dv, (h + 1) * dv)
        kat = slice(h * dk, (h + 1) * dk)
        z = zgate[:, at]
        sig = jax.nn.sigmoid(z)
        act = z * sig
        o = local[:, at] + mm(qa[:, kat], entering[h])
        so = lax.rsqrt(jnp.mean(o * o, axis=-1, keepdims=True) + EPS)
        normed = o * so
        g = dy[:, at]
        scaled = gain[0:1, :] * g
        gain_sum[0:1, :] += jnp.sum(g * normed * act, axis=0, keepdims=True)
        dz_out[:, at] = (scaled * normed * (sig * (1.0 + z * (1.0 - sig)))).astype(bf16)
        back = scaled * act
        dots = jnp.mean(back * o, axis=-1, keepdims=True)
        do = (so * back - o * (so * so * so * dots)).astype(bf16)
        do_out[:, at] = do
        after = state[h]
        kept = jnp.where(ends[:, START : START + 1] == 0.0, jnp.exp(ends[:, h : h + 1]), 0.0)
        pulled = mm(ktail[:, kat], after)
        now = kept * after + mm_tn(
            jnp.concatenate([qeff[:, kat], wkey[:, kat]], axis=0),
            jnp.concatenate([do, (-pulled).astype(bf16)], axis=0),
        )
        state[h] = now
        first[h] = now.astype(bf16)
    gain_out[...] = gain_sum[...]


def grad_kernel(
    heads, dk, dv,
    proj, conv, ab, flags, cum_in, halo, taps, head, do_in, tinv, uval, wkey, states, entering, leaving,
    dproj, dab, tail_rows, head_rows, dtaps, dhead,
    state, ext, tap_sum, head_sum,
):
    step = pl.program_id(0)
    steps = pl.num_programs(0)
    size = proj.shape[0]
    width = proj.shape[1]
    every = range(heads)

    @pl.when(step == 0)
    def _():
        state[...] = leaving[...].astype(f32)
        ext[size : size + 8, :] = jnp.zeros((8, width), f32)
        tap_sum[...] = jnp.zeros_like(tap_sum)
        head_sum[...] = jnp.zeros_like(head_sum)

    @pl.when(step > 0)
    def _():
        ext[size : size + 8, :] = ext[0:8, :]

    fl = flags[...]
    raw = ab[...]
    beta_all = jax.nn.sigmoid(raw)
    cum = cum_in[...]
    gates = chunk_gates(cum, heads)
    row, col = grid_of(size, size)
    strict = row > col
    betas = [beta_all[:, heads + h : heads + h + 1] for h in every]

    cq = [conv[:, h * dk : (h + 1) * dk] for h in every]
    ck = [conv[:, (heads + h) * dk : (heads + h + 1) * dk] for h in every]
    vbase = 2 * heads * dk
    sq = [silu(c) for c in cq]
    sk = [silu(c) for c in ck]
    rq = [unit_scale(s) for s in sq]
    rk = [unit_scale(s) for s in sk]
    queries = [s * r * dk**-0.5 for s, r in zip(sq, rq)]
    keys = [s * r for s, r in zip(sk, rk)]
    q16 = [q.astype(bf16) for q in queries]
    k16 = [k.astype(bf16) for k in keys]
    kk = [mm_nt(k, k) for k in k16]
    qk = [mm_nt(q, k) for q, k in zip(q16, k16)]
    attend = [gates[h][0] * qk[h] for h in every]
    weak = [jnp.where(strict, gates[h][0] * kk[h], 0.0) for h in every]

    dsum_row = jnp.zeros((LANES, size), f32)
    dsum_col = jnp.zeros((size, LANES), f32)
    end_add = jnp.zeros((1, LANES), f32)
    dbeta_all = jnp.zeros((size, LANES), f32)
    lane = lax.broadcasted_iota(jnp.int32, (size, LANES), 1)
    lane_row = lax.broadcasted_iota(jnp.int32, (1, LANES), 1)
    sub = lax.broadcasted_iota(jnp.int32, (LANES, size), 0)

    starts, users, dos, dstates, dks16 = [], [], [], [], []
    for h in every:
        entry16 = entering[h]
        start = states[0, h, :, 0:dv].astype(f32) + mm(states[0, h, :, dv : dv + dk], entry16)
        start16 = start.astype(bf16)
        both = mm(jnp.concatenate([wkey[:, h * dk : (h + 1) * dk], k16[h]], axis=0), start16)
        starts.append((start, start16, both[size:]))
        users.append((uval[:, h * dv : (h + 1) * dv].astype(f32) - both[:size]).astype(bf16))
        dos.append(do_in[:, h * dv : (h + 1) * dv])
        dstates.append(state[h])
    d16 = [d.astype(bf16) for d in dstates]
    du = [
        mm_tn(attend[h], dos[h]) + mm(gates[h][2] * keys[h], d16[h]) for h in every
    ]
    dright = [mm_tn(tinv[:, h * size : (h + 1) * size], du[h]) for h in every]
    for h in every:
        decay, entry, tail, kept = gates[h]
        beta = betas[h]
        start, start16, recalled = starts[h]
        dr = dright[h]
        pair = jnp.concatenate([dos[h], dr.astype(bf16)], axis=0)
        wide = mm_nt(pair, jnp.concatenate([users[h], start16], axis=0))
        dattend = wide[:size, :size]
        dqe = wide[:size, size:]
        dlow = -wide[size:, :size]
        dke = -beta * wide[size:, size:]
        user_end = mm_nt(users[h], d16[h])
        state[h] = kept * dstates[h] + mm_tn(
            jnp.concatenate([entry * queries[h], -(beta * entry) * keys[h]], axis=0), pair
        )
        dqk = dattend * decay
        dkk = jnp.where(strict, dlow * decay, 0.0) * beta
        stack = jnp.concatenate([dqk, dkk], axis=0).astype(bf16)
        ahead = mm(stack, k16[h])
        behind = mm_tn(stack, jnp.concatenate([q16[h], k16[h]], axis=0))
        dq = ahead[:size] + entry * dqe
        dk_ = ahead[size:] + behind + entry * dke + tail * user_end
        base = vbase + h * dv
        cv = conv[:, base : base + dv]
        sigv = jax.nn.sigmoid(cv)
        value = cv * sigv
        ext[0:size, base : base + dv] = (beta * dr) * (sigv * (1.0 + cv * (1.0 - sigv)))
        dbeta = jnp.sum(dr * (value - entry * recalled), axis=-1, keepdims=True) + jnp.sum(
            dlow * weak[h], axis=-1, keepdims=True
        )
        lowmask = dlow * weak[h] * beta
        paired = dattend * attend[h] + lowmask
        dentry = jnp.sum(dqe * queries[h] + dke * keys[h], axis=-1, keepdims=True)
        dtail = jnp.sum(user_end * keys[h], axis=-1, keepdims=True) * tail
        dkept = jnp.sum(
            jnp.sum(start * dstates[h], axis=1, keepdims=True), axis=0, keepdims=True
        )
        col_add = jnp.sum(paired, axis=-1, keepdims=True) + dentry * entry - dtail
        dsum_col = jnp.where(lane == h, col_add, dsum_col)
        dsum_row = jnp.where(sub == h, jnp.sum(paired, axis=0, keepdims=True), dsum_row)
        end_add = jnp.where(
            lane_row == h, jnp.sum(dtail, axis=0, keepdims=True) + dkept * kept, end_add
        )
        dbeta_all = jnp.where(lane == heads + h, dbeta, dbeta_all)
        inner = jnp.sum(dq * sq[h], axis=-1, keepdims=True)
        scale = dk**-0.5 * rq[h]
        ds = scale * dq - sq[h] * (scale * rq[h] * rq[h] * inner)
        ext[0:size, h * dk : (h + 1) * dk] = ds * silu_grad(cq[h])
        inner = jnp.sum(dk_ * sk[h], axis=-1, keepdims=True)
        ds = rk[h] * dk_ - sk[h] * (rk[h] * rk[h] * rk[h] * inner)
        ext[0:size, (heads + h) * dk : (heads + h + 1) * dk] = ds * silu_grad(ck[h])

    dcum = dsum_col - jnp.transpose(dsum_row)
    final = lax.broadcasted_iota(jnp.int32, (size, LANES), 0) == size - 1
    dcum = dcum + jnp.where(final, end_add, 0.0)
    dlog = mm_hi((row <= col).astype(f32), dcum) * (1.0 - fl[:, START : START + 1])
    rate = jnp.exp(head[0:1, :])
    shifted = raw + head[1:2, :]
    dap = dlog * (-rate) * jax.nn.sigmoid(shifted)
    dbp = dbeta_all * beta_all * (1.0 - beta_all)
    dab[...] = jnp.where(lane < heads, dap, jnp.where(lane < 2 * heads, dbp, 0.0)).astype(bf16)
    head_sum[0:1, :] += jnp.sum(dlog * (-rate) * softplus(shifted), axis=0, keepdims=True)
    head_sum[1:2, :] += jnp.sum(dap, axis=0, keepdims=True)
    dhead[...] = head_sum[...]

    later = [jnp.broadcast_to(fl[:, AHEAD + s : AHEAD + s + 1], (size, LANES)) for s in (1, 2, 3)]
    for lo in range(0, width, LANES):
        at = slice(lo, lo + LANES)
        here = proj[:, at]
        own = ext[0:size, at]
        total = own * taps[3:4, at]
        tap_sum[3:4, at] += jnp.sum(own * here, axis=0, keepdims=True)
        for s in (1, 2, 3):
            moved = ext[s : s + size, at] * later[s - 1]
            total += moved * taps[3 - s : 4 - s, at]
            tap_sum[3 - s : 4 - s, at] += jnp.sum(moved * here, axis=0, keepdims=True)
        dproj[:, at] = total.astype(bf16)

        @pl.when(step == 0)
        def _():
            tail_rows[:, at] = total[size - 8 : size, :]

    @pl.when(step == steps - 1)
    def _():
        head_rows[...] = ext[0:8, :]
        sub8 = lax.broadcasted_iota(jnp.int32, (8, width), 0)
        for s in (1, 2, 3):
            ok = (sub8 < s).astype(f32) * fl[0:8, VALID + s : VALID + s + 1]
            before = pltpu.roll(halo[...], s, 0)
            tap_sum[3 - s : 4 - s, :] += jnp.sum(
                ext[0:8, :] * before * ok, axis=0, keepdims=True
            )

    dtaps[...] = tap_sum[...]


def delta_grad(
    proj, conv, flags, cum, halo, taps, head, do, tinv, uval, wkey, states, entering, leaving,
    heads, dk, dv,
):
    rows = proj.shape[0]
    size = CHUNK
    steps = rows // size
    width = 2 * heads * dk + heads * dv
    ab_at = (width + heads * dv) // LANES

    def rowwise(cols, at=0):
        return pl.BlockSpec((size, cols), lambda n: (steps - 1 - n, at))

    outs = [
        ((rows, width), bf16, rowwise(width)),
        ((rows, LANES), bf16, rowwise(LANES)),
        ((8, width), f32, whole((8, width))),
        ((8, width), f32, whole((8, width))),
        ((8, width), f32, whole((8, width))),
        ((8, LANES), f32, whole((8, LANES))),
    ]
    return pl.pallas_call(
        functools.partial(grad_kernel, heads, dk, dv),
        grid=(steps,),
        in_specs=[
            rowwise(width),
            rowwise(width),
            rowwise(LANES, ab_at),
            rowwise(LANES),
            rowwise(LANES),
            whole((8, width)),
            whole((8, width)),
            whole((8, LANES)),
            rowwise(heads * dv),
            rowwise(heads * size),
            rowwise(heads * dv),
            rowwise(heads * dk),
            pl.BlockSpec((1, heads, dk, dv + dk), lambda n: (steps - 1 - n, 0, 0, 0)),
            whole((heads, dk, dv)),
            whole((heads, dk, dv)),
        ],
        out_specs=[spec for _, _, spec in outs],
        out_shape=[jax.ShapeDtypeStruct(shape, kind) for shape, kind, _ in outs],
        scratch_shapes=[
            pltpu.VMEM((heads, dk, dv), f32),
            pltpu.VMEM((size + 8, width), f32),
            pltpu.VMEM((8, width), f32),
            pltpu.VMEM((8, LANES), f32),
        ],
        compiler_params=vmem(),
        cost_estimate=pl.CostEstimate(
            flops=rows * heads * 200 * size * (dv + dk + size),
            bytes_accessed=rows * width * 16,
            transcendentals=rows * width * 2,
        ),
    )(
        proj, conv, proj, flags, cum, halo, taps, head, do, tinv, uval, wkey, states, entering,
        leaving,
    )


def shifted(value, axis, distance):
    count = lax.axis_size(axis)
    route = [(i, i + distance) for i in range(count) if 0 <= i + distance < count]
    return lax.ppermute(value, axis, route)


def chain_kernel(forward, levels, *refs):
    if forward:
        own, out, mats, runs, arrived, kept, send_sem, recv_sem, mat_sems = refs
    else:
        own, maps, out, runs, arrived, send_sem, recv_sem = refs
    heads, dk = own.shape[:2]
    dv = out.shape[2]
    count = lax.axis_size("ctx")
    me = lax.axis_index("ctx")
    place = me if forward else count - 1 - me
    way = 1 if forward else -1
    distances = [2**j for j in range(levels)] + [1]
    behind = [2 ** (j + 1) - 1 for j in range(levels - 1)] if forward else []
    reaches = sorted(set(distances + behind))
    barrier = pltpu.get_barrier_semaphore()
    known = jnp.int32(0)
    for d in reaches:
        for sign in (1, -1):
            there = (me + sign * d >= 0) & (me + sign * d < count)
            known = known + there.astype(jnp.int32)

            @pl.when(there)
            def _(sign=sign, d=d):
                pl.semaphore_signal(
                    barrier, inc=1, device_id={"ctx": me + sign * d},
                    device_id_type=pl.DeviceIdType.MESH,
                )

    pl.semaphore_wait(barrier, known)

    def copy(j, h):
        width = dv if j >= levels - 1 else own.shape[2]
        source = own if j == 0 else runs.at[j - 1]
        return pltpu.make_async_remote_copy(
            src_ref=source.at[h, :, pl.ds(0, width)],
            dst_ref=arrived.at[j, h, :, pl.ds(0, width)],
            send_sem=send_sem.at[j, h],
            recv_sem=recv_sem.at[j, h],
            device_id={"ctx": me + way * distances[j]},
            device_id_type=pl.DeviceIdType.MESH,
        )

    def send(j, h):
        @pl.when(place + distances[j] < count)
        def _():
            copy(j, h).start()

    def mat_copy(j, h):
        return pltpu.make_async_remote_copy(
            src_ref=kept.at[j, h],
            dst_ref=kept.at[levels + j, h],
            send_sem=mat_sems.at[0, j, h],
            recv_sem=mat_sems.at[1, j, h],
            device_id={"ctx": me - behind[j]},
            device_id_type=pl.DeviceIdType.MESH,
        )

    for h in range(heads):
        send(0, h)
    for j in range(levels + 1):
        for h in range(heads):

            @pl.when(place >= distances[j])
            def _(j=j, h=h):
                copy(j, h).wait_recv()

            @pl.when(place < distances[j])
            def _(j=j, h=h):
                arrived[j, h] = jnp.zeros(arrived.shape[2:], bf16)

            if j == levels:
                out[h] = arrived[j, h, :, 0:dv]
                continue
            run = own[h] if j == 0 else runs[j - 1, h]
            if forward:
                matrix = run[:, dv:]
                width = dv if j == levels - 1 else dv + dk
                joined = mm(matrix, arrived[j, h, :, 0:width])
                runs[j, h, :, 0:dv] = (run[:, 0:dv].astype(f32) + joined[:, 0:dv]).astype(bf16)
                if j < levels - 1:
                    runs[j, h, :, dv : dv + dk] = joined[:, dv:].astype(bf16)
                    kept[j, h] = joined[:, dv:].astype(bf16)

                    @pl.when(me >= behind[j])
                    def _(j=j, h=h):
                        mat_copy(j, h).start()
            else:
                joined = mm_tn(maps[j, h], arrived[j, h])
                runs[j, h] = (run.astype(f32) + joined).astype(bf16)
            send(j + 1, h)
    for j in range(levels + 1):
        for h in range(heads):

            @pl.when(place + distances[j] < count)
            def _(j=j, h=h):
                copy(j, h).wait_send()
    if forward:
        for h in range(heads):
            mats[0, h] = own[h, :, dv:]
        for j, d in enumerate(behind):
            for h in range(heads):

                @pl.when(me + d < count)
                def _(j=j, h=h):
                    mat_copy(j, h).wait_recv()
                    mats[j + 1, h] = kept[levels + j, h]

                @pl.when(me + d >= count)
                def _(j=j, h=h):
                    mats[j + 1, h] = jnp.zeros(mats.shape[2:], bf16)

                @pl.when(me >= d)
                def _(j=j, h=h):
                    mat_copy(j, h).wait_send()


def chained(own, maps, dv, levels, collective_id):
    heads, dk, width = own.shape
    forward = maps is None
    spec = pl.BlockSpec(memory_space=pltpu.VMEM)
    shapes = [(heads, dk, dv)] + ([(levels, heads, dk, dk)] if forward else [])
    return pl.pallas_call(
        functools.partial(chain_kernel, forward, levels),
        in_specs=[spec] * (1 if forward else 2),
        out_specs=[spec] * len(shapes),
        out_shape=[jax.ShapeDtypeStruct(shape, bf16) for shape in shapes],
        scratch_shapes=[
            pltpu.VMEM((levels, heads, dk, width), bf16),
            pltpu.VMEM((levels + 1, heads, dk, width), bf16),
        ]
        + ([pltpu.VMEM((2 * levels, heads, dk, dk), bf16)] if forward else [])
        + [
            pltpu.SemaphoreType.DMA((levels + 1, heads)),
            pltpu.SemaphoreType.DMA((levels + 1, heads)),
        ]
        + ([pltpu.SemaphoreType.DMA((2, levels, heads))] if forward else []),
        compiler_params=pltpu.CompilerParams(
            collective_id=collective_id, has_side_effects=True, vmem_limit_bytes=24 * MIB
        ),
        cost_estimate=pl.CostEstimate(flops=25 * 10**9, bytes_accessed=own.size * 16, transcendentals=0),
    )(*([own] if forward else [own, maps]))


def levels_of(reach):
    levels = 1
    while 2**levels < reach:
        levels += 1
    return levels


def entering_state(own, dv, reach):
    levels = levels_of(reach)
    return chained(own, None, dv, levels, 3)


def leaving_grad(own, ahead):
    return chained(own, ahead, own.shape[2], ahead.shape[0], 4)[0]


def summed_over_tp(part):
    return added(part, over_tp(part))


def over_tp(part):
    count = lax.axis_size("tp")
    routes = [[(i, (i + d) % count) for i in range(count)] for d in range(1, count)]
    return [lax.ppermute(part, "tp", route) for route in routes]


def added(part, others):
    total = part.astype(f32)
    for other in others:
        total = total + other.astype(f32)
    return total


def swapped(value, axis, bit):
    return lax.ppermute(value, axis, [(i, i ^ bit) for i in range(lax.axis_size(axis))])


def sum_kernel(plan, *refs):
    count = len(plan)
    grads, outs = refs[:count], refs[count : 2 * count]
    refs = refs[2 * count :]
    own, fs_in, in_y, in_m, in_h, full = (refs[i * count : (i + 1) * count] for i in range(6))
    load_sem, send_sem, recv_sem = refs[6 * count :]
    fs = lax.axis_index("fs")
    me = lax.axis_index("ctx")
    y = lax.rem(me, 2)
    z = lax.div(me, 2)
    hub = lax.div(z, 2)
    inner = lax.rem(lax.div(z + 1, 2), 2)
    mate = z + 1 - 2 * lax.rem(z, 2)
    core = {"fs": 1 - fs}
    beside = {"ctx": z * 2 + 1 - y}
    paired = {"ctx": mate * 2 + y}
    across = {"ctx": (3 - z) * 2 + y}
    barrier = pltpu.get_barrier_semaphore()
    for partner in (core, beside, paired, across):
        pl.semaphore_signal(barrier, inc=1, device_id=partner, device_id_type=pl.DeviceIdType.MESH)
    pl.semaphore_wait(barrier, 4)

    segments = []
    for i, widths in enumerate(plan):
        lo = 0
        for w in widths:
            segments.append((i, slice(lo, lo + w)))
            lo += w
    total = len(segments)

    def rows(start, n):
        return pl.ds(pl.multiple_of(start, 16), n)

    def stages(g):
        i, at = segments[g]
        half = own[i].shape[0]
        q, e = half // 2, half // 4
        y_first = g % 2 == 0

        def remote(slot, src, dst, partner):
            return pltpu.make_async_remote_copy(
                src_ref=src,
                dst_ref=dst,
                send_sem=send_sem.at[g, slot],
                recv_sem=recv_sem.at[g, slot],
                device_id=partner,
                device_id_type=pl.DeviceIdType.MESH,
            )

        def moved(slot, source, target, start, n, partner):
            return remote(
                slot, source[i].at[rows(start, n), at], target[i].at[rows(start, n), at], partner
            )

        def add(target, one, two, start, n):
            step = 32 if n % 32 == 0 else 16

            def body(j, carry):
                r = rows(start + j * step, step)
                total = one[i][r, at].astype(f32) + two[i][r, at].astype(f32)
                target[i][r, at] = total.astype(target[i].dtype)
                return carry

            lax.fori_loop(0, n // step, body, 0)

        load = pltpu.make_async_copy(
            grads[i].at[rows(fs * half, half), at], own[i].at[:, at], load_sem.at[g]
        )
        unload = pltpu.make_async_copy(full[i].at[:, at], outs[i].at[:, at], load_sem.at[total + g])
        fs_copy = remote(0, grads[i].at[rows((1 - fs) * half, half), at], fs_in[i].at[:, at], core)
        if y_first:
            mine = y * q
            low_copy = moved(1, own, in_y, (1 - y) * q, q, beside)
            mate_copy = moved(2, own, in_m, mine, q, paired)
            hub_copy = moved(3, own, in_h, mine + (1 - hub) * e, e, across)
            back_hub = moved(4, full, full, mine + hub * e, e, across)
            back_low = moved(5, full, full, mine, q, beside)
            back_mate = moved(6, full, full, mine, q, paired)
        else:
            mine = hub * q
            mate_copy = moved(2, own, in_m, 0, half, paired)
            hub_copy = moved(3, own, in_h, (1 - hub) * q, q, across)
            low_copy = moved(1, own, in_y, mine + (1 - y) * e, e, beside)
            back_low = moved(5, full, full, mine + y * e, e, beside)
            back_hub = moved(4, full, full, mine, q, across)
            back_mate = moved(6, full, full, 0, half, paired)

        def begin():
            fs_copy.start()
            load.start()

        def finish():
            @pl.when(inner == 0)
            def _():
                mate_copy.wait_send()

            @pl.when(inner == 1)
            def _():
                back_mate.wait_send()

            unload.wait()

        def cores():
            load.wait()
            fs_copy.wait()
            add(own, own, fs_in, 0, half)

        if y_first:

            def s0():
                cores()
                low_copy.start()

            def s1():
                low_copy.wait()
                add(own, own, in_y, mine, q)

                @pl.when(inner == 0)
                def _():
                    mate_copy.start()

            def s2():
                @pl.when(inner == 1)
                def _():
                    mate_copy.wait_recv()
                    add(own, own, in_m, mine, q)
                    hub_copy.start()

            def s3():
                @pl.when(inner == 1)
                def _():
                    hub_copy.wait()
                    add(full, own, in_h, mine + hub * e, e)
                    back_hub.start()

            def s4():
                @pl.when(inner == 1)
                def _():
                    back_hub.wait()
                    back_mate.start()
                    back_low.start()

            def s5():
                @pl.when(inner == 0)
                def _():
                    back_mate.wait_recv()
                    back_low.start()

            def s6():
                back_low.wait()
                unload.start()

        else:

            def s0():
                cores()

                @pl.when(inner == 0)
                def _():
                    mate_copy.start()

            def s1():
                @pl.when(inner == 1)
                def _():
                    mate_copy.wait_recv()
                    add(own, own, in_m, 0, half)
                    hub_copy.start()

            def s2():
                @pl.when(inner == 1)
                def _():
                    hub_copy.wait()
                    add(own, own, in_h, mine, q)
                    low_copy.start()

            def s3():
                @pl.when(inner == 1)
                def _():
                    low_copy.wait()
                    add(full, own, in_y, mine + y * e, e)
                    back_low.start()

            def s4():
                @pl.when(inner == 1)
                def _():
                    back_low.wait()
                    back_hub.start()

            def s5():
                @pl.when(inner == 1)
                def _():
                    back_hub.wait()
                    back_mate.start()
                    unload.start()

            def s6():
                @pl.when(inner == 0)
                def _():
                    back_mate.wait_recv()
                    unload.start()

        return begin, (s0, s1, s2, s3, s4, s5, s6), finish

    work = [stages(g) for g in range(total)]
    for begin, _, _ in work:
        begin()
    for t in range(total + 6):
        for stage in range(7):
            if 0 <= t - stage < total:
                work[t - stage][1][stage]()
    for _, _, finish in work:
        finish()


def segment_widths(cols, rows, target=128 * 1024):
    tiles = cols // LANES
    parts = max(1, min(tiles, round(rows * cols / target)))
    return tuple((tiles * (j + 1) // parts - tiles * j // parts) * LANES for j in range(parts))


def reduced(grads, collective_id, micros):
    if lax.axis_size("ctx") != 8 or lax.axis_size("fs") != 2:
        parts = [lax.psum_scatter(g, "fs", scatter_dimension=0, tiled=True) for g in grads]
        return [lax.psum(part, "ctx") for part in parts]
    shapes = [(g.shape[0] // 2, g.shape[1]) for g in grads]
    plan = tuple(segment_widths(cols, half) for half, cols in shapes)
    total = sum(len(widths) for widths in plan)
    return pl.pallas_call(
        functools.partial(sum_kernel, plan),
        in_specs=[pl.BlockSpec(memory_space=pl.ANY)] * len(grads),
        out_specs=[pl.BlockSpec(memory_space=pl.ANY)] * len(grads),
        out_shape=[jax.ShapeDtypeStruct(shape, g.dtype) for shape, g in zip(shapes, grads)],
        scratch_shapes=[pltpu.VMEM(shape, g.dtype) for shape, g in zip(shapes, grads)] * 6
        + [
            pltpu.SemaphoreType.DMA((2 * total,)),
            pltpu.SemaphoreType.DMA((total, 7)),
            pltpu.SemaphoreType.DMA((total, 7)),
        ],
        compiler_params=pltpu.CompilerParams(
            collective_id=collective_id, has_side_effects=True, vmem_limit_bytes=56 * MIB
        ),
        cost_estimate=pl.CostEstimate(
            flops=micros * 10**9, bytes_accessed=4 * sum(g.size for g in grads), transcendentals=0
        ),
    )(*grads)


def scattered(grad):
    return lax.psum_scatter(grad, ("fs", "ctx"), scatter_dimension=0, tiled=True)


def per_device(
    tokens, cotangent, lengths, order, mixer_gain, w_query, w_key, w_value, w_outgate, w_decay,
    w_beta, conv_query, conv_key, conv_value, decay_log, decay_bias, out_gain, w_output, mlp_gain,
    w_gate, w_up, w_down,
):
    rows, model = tokens.shape[1:]
    ctx = lax.axis_size("ctx")
    fs = lax.axis_size("fs")
    me = lax.axis_index("ctx")
    heads = decay_log.shape[0]
    dk = w_query.shape[1] // heads
    dv = w_value.shape[1] // heads
    key_cols, value_cols = heads * dk, heads * dv
    width = 2 * key_cols + value_cols
    hidden_cols = w_gate.shape[1]
    total = order.shape[1]
    peer = rows // ctx
    halo_rows = TAPS - 1
    sequences = lengths.shape[1]
    longest = 2 * total // (sequences + 1)
    reach = min(ctx - 1, -(-longest // rows))

    order_row = order[0]
    source_all = order_row // rows
    mine = (source_all == me).reshape(ctx, rows)
    upto = (jnp.arange(rows)[:, None] <= jnp.arange(rows)[None, :]).astype(bf16)
    rank_all = jnp.dot(mine.astype(bf16), upto, preferred_element_type=f32).astype(jnp.int32) - 1
    slots = jnp.arange(peer, dtype=jnp.int32)
    picked = mine[:, None, :] & (rank_all[:, None, :] == slots[None, :, None])
    local_all = (order_row - me * rows).reshape(ctx, 1, rows)
    send_order = jnp.sum(jnp.where(picked, local_all, 0), axis=2).reshape(rows)
    given = lax.dynamic_slice_in_dim(order_row, me * rows, rows)
    source = given // rows
    from_each = source[None, :] == jnp.arange(ctx, dtype=jnp.int32)[:, None]
    rank_here = jnp.dot(from_each.astype(bf16), upto, preferred_element_type=f32) - 1.0
    rank_here = jnp.sum(jnp.where(from_each, rank_here, 0.0), axis=0).astype(jnp.int32)
    recv_slot = source * peer + rank_here
    iota = jnp.arange(rows, dtype=jnp.int32)
    gather_send = (send_order[:, None] == iota[None, :]).astype(bf16)
    gather_recv = (recv_slot[:, None] == iota[None, :]).astype(bf16)

    def moved(maps, values, transposed=False):
        return lax.dot_general(
            maps, values, (((0 if transposed else 1,), (0,)), ((), ())), preferred_element_type=f32
        ).astype(bf16)

    def exchanged(values):
        return lax.all_to_all(values, "ctx", split_axis=0, concat_axis=0, tiled=True)

    sent = moved(gather_send, tokens[0])
    offsets = jnp.cumsum(lengths[0]) - lengths[0]
    positions = me * rows - halo_rows + jnp.arange(rows + 2 * halo_rows, dtype=jnp.int32)
    number = jnp.sum((offsets[None, :] <= positions[:, None]).astype(jnp.int32), axis=1)
    here = number[halo_rows : halo_rows + rows]
    fresh = jnp.any(offsets[None, :] == positions[halo_rows : halo_rows + rows, None], axis=1)
    columns = [jnp.zeros((rows,), f32)] * START + [fresh.astype(f32)]
    for s in range(1, TAPS):
        columns.append((number[halo_rows - s : halo_rows - s + rows] == here).astype(f32))
    for s in range(1, TAPS):
        columns.append((number[halo_rows + s : halo_rows + s + rows] == here).astype(f32))
    flags = jnp.stack(columns, axis=1)
    flags = jnp.pad(flags, ((0, 0), (0, LANES - flags.shape[1])))

    pad = jnp.zeros((w_decay.shape[0], LANES - 2 * heads), bf16)
    w_in = jnp.concatenate([w_query, w_key, w_value, w_outgate, w_decay, w_beta, pad], axis=1)
    sent, w_in = lax.optimization_barrier((sent, w_in))
    w_in = lax.all_gather(w_in, "fs", axis=0, tiled=True)
    resident = moved(gather_recv, exchanged(sent))
    w_wide = lax.all_gather(jnp.concatenate([w_gate, w_up], axis=1), "fs", axis=0, tiled=True)
    w_down = lax.all_gather(w_down, "fs", axis=0, tiled=True)
    w_output = lax.all_gather(w_output, "fs", axis=0, tiled=True)
    small = jnp.concatenate(
        [
            conv_query.T.reshape(-1),
            conv_key.T.reshape(-1),
            conv_value.T.reshape(-1),
            mixer_gain,
            mlp_gain,
            out_gain,
        ]
    )
    small = lax.all_gather(small, "fs", axis=0).astype(f32)
    pieces, at = [], 0
    for channels in (conv_query.shape[0], conv_key.shape[0], conv_value.shape[0]):
        part = small[:, at : at + TAPS * channels].reshape(fs, TAPS, channels)
        pieces.append(part.transpose(1, 0, 2).reshape(TAPS, fs * channels))
        at += TAPS * channels
    taps = jnp.pad(jnp.concatenate(pieces, axis=1), ((0, 8 - TAPS), (0, 0)))
    gains = []
    for size in (mixer_gain.shape[0], mlp_gain.shape[0], out_gain.shape[0]):
        gains.append(small[:, at : at + size].reshape(-1))
        at += size
    gain_one, gain_two, gain_out = gains
    gain_rows = jnp.broadcast_to(gain_out[None, :], (8, dv))
    head = jnp.pad(
        jnp.stack([decay_log, decay_bias]), ((0, 6), (0, LANES - heads))
    )

    x = resident.astype(f32)
    inv_one = lax.rsqrt(jnp.mean(x * x, axis=-1, keepdims=True) + EPS)
    n1 = (x * inv_one * gain_one).astype(bf16)
    proj = jnp.dot(n1, w_in, preferred_element_type=f32)
    halo = shifted(proj[rows - 8 :, :width], "ctx", 1)
    conv, local, qa, states, tinv, uval, wkey, qeff, ktail, cum, last = delta_forward(
        proj, flags, halo, taps, head, heads, dk, dv
    )
    last, arrived = lax.optimization_barrier((last, exchanged(moved(gather_send, cotangent[0]))))
    e = moved(gather_recv, arrived)
    entering, ahead = entering_state(last, dv, reach)
    y1, down, r, dr, er, mlp_gain_sum, mlp_cat, dz, do, dgain_out, first = block_rest(
        local, qa, entering, proj, gain_rows, w_output, resident, e,
        jnp.broadcast_to(gain_two[None, :], (8, model)), w_wide, w_down, qeff, wkey, ktail, cum,
        heads, dk, dv, 2,
    )
    grad_mlp_gain = mlp_gain_sum[0]

    def outer(a, b):
        return lax.dot_general(
            a, b, (((0,), (0,)), ((), ())), preferred_element_type=f32
        ).astype(bf16)

    def halves(grad):
        return grad.reshape(fs, grad.shape[0] // fs, *grad.shape[1:])

    half = model // fs
    down_rows = hidden_cols // fs

    leaving = leaving_grad(first, ahead)
    leaving, mlp_cat = lax.optimization_barrier((leaving, mlp_cat))
    mlp_share = scattered(mlp_cat)
    dproj, dab, tail_rows, head_rows, dtaps, dhead = delta_grad(
        proj, conv, flags, cum, halo, taps, head, do, tinv, uval, wkey, states, entering, leaving,
        heads, dk, dv,
    )
    dproj, down_other = lax.optimization_barrier((dproj, over_tp(down)))
    next_rows = shifted(head_rows, "ctx", -1)
    extra = jnp.zeros_like(tail_rows)
    for s in range(1, TAPS):
        part_s = jnp.concatenate([jnp.zeros((8 - s, width), f32), next_rows[:s]], axis=0)
        extra = extra + part_s * taps[TAPS - 1 - s] * flags[rows - 8 :, AHEAD + s][:, None]
    dproj = lax.dynamic_update_slice(dproj, (tail_rows + extra).astype(bf16), (rows - 8, 0))
    dall = jnp.concatenate([dproj, dz, dab], axis=1)
    dn1 = lax.dot_general(dall, w_in, (((1,), (1,)), ((), ())), preferred_element_type=f32)
    dn1_own, dz, y1, down_other = lax.optimization_barrier(
        (dn1.astype(bf16), dz, y1, down_other)
    )
    dn1_other = over_tp(dn1_own)
    g_in = outer(n1, jnp.concatenate([dproj, dab], axis=1))
    g_z = outer(n1, dz)
    g_o = outer(y1, er)
    g_in, mlp_share = lax.optimization_barrier((g_in, mlp_share))
    g_mlp_all = lax.all_gather(mlp_share, "ctx", axis=0, tiled=True)
    result = (r + added(down, down_other)).astype(bf16)
    block_rows = exchanged(moved(gather_recv, result, True))
    def tap_part(lo, channels):
        return dtaps[:TAPS, lo : lo + channels].reshape(TAPS, fs, -1).transpose(1, 0, 2).reshape(fs, -1)

    share = jnp.sum(dgain_out, axis=0)
    rates = jnp.broadcast_to(dhead[:2, :heads].reshape(1, 2 * heads), (fs, 2 * heads))
    own_mixer_gain = jnp.sum(dn1_own.astype(f32) * x * inv_one, axis=0)
    little = jnp.concatenate(
        [
            tap_part(0, key_cols),
            tap_part(key_cols, key_cols),
            tap_part(2 * key_cols, value_cols),
            halves(own_mixer_gain),
            halves(grad_mlp_gain),
            halves(share),
            rates,
        ],
        axis=1,
    )
    little_rows = -(-little.shape[1] // (64 * LANES)) * 64
    little = jnp.pad(little, ((0, 0), (0, little_rows * LANES - little.shape[1])))
    little = little.reshape(fs * little_rows, LANES)
    little, g_in, g_z, g_o = reduced([little, g_in, g_z, g_o], 1, 110)
    dn1_other, block_rows, little, g_in, g_z, g_o = lax.optimization_barrier(
        (dn1_other, block_rows, little, g_in, g_z, g_o)
    )
    dn1 = added(dn1_own, dn1_other)
    little = little.reshape(-1)
    unit = jnp.eye(hidden_cols, dtype=bf16)
    g_gate, g_up = (
        lax.dot_general(
            g_mlp_all[lo : lo + hidden_cols], unit, (((0,), (0,)), ((), ())),
            preferred_element_type=f32,
        )
        for lo in (0, hidden_cols)
    )
    g_down = g_mlp_all[2 * hidden_cols :].reshape(fs, down_rows, half)
    g_down = jnp.concatenate([g_down[j] for j in range(fs)], axis=1)
    scaled = gain_one * dn1
    grad_in = (
        dr
        + inv_one * scaled
        - x * (inv_one * inv_one * inv_one * jnp.mean(scaled * x, axis=-1, keepdims=True))
    ).astype(bf16)
    token_rows = exchanged(moved(gather_recv, grad_in, True))

    taken, at = [], 0
    for channels in (conv_query.shape[0], conv_key.shape[0], conv_value.shape[0]):
        taken.append(little[at : at + TAPS * channels].reshape(TAPS, channels).T)
        at += TAPS * channels
    for size in (mixer_gain.shape[0], mlp_gain.shape[0], out_gain.shape[0], heads, heads):
        taken.append(little[at : at + size])
        at += size
    g_cq, g_ck, g_cv, g_mixer, g_mlp, g_out_gain, g_log, g_bias = taken
    ends_tp = summed_over_tp(jnp.concatenate([g_mixer, g_out_gain]))
    g_mixer, g_out_gain = ends_tp[: g_mixer.shape[0]], ends_tp[g_mixer.shape[0] :]
    ends = [key_cols, 2 * key_cols, width, width + heads]
    g_query, g_key, g_value, g_decay, g_beta = (
        g_in[:, lo:hi].astype(f32) for lo, hi in zip([0] + ends, ends + [ends[-1] + heads])
    )
    outs = (
        moved(gather_send, block_rows, True)[None],
        g_mixer,
        g_query,
        g_key,
        g_value,
        g_z.astype(f32),
        g_decay,
        g_beta,
        g_cq,
        g_ck,
        g_cv,
        g_log,
        g_bias,
        g_out_gain,
        g_o.astype(f32),
        g_mlp,
        g_gate,
        g_up,
        g_down.astype(f32),
    )
    token_rows, outs = lax.optimization_barrier((token_rows, outs))
    grad_tokens = moved(gather_send, token_rows, True)[None]
    return (outs[0], grad_tokens) + outs[1:]


def solution(mesh):
    split = P("fs", "ctx", None)
    cols = P("fs", "tp")
    both = P(("tp", "fs"), None)
    in_specs = (
        split, split, P("fs", None), P("fs", None), P("fs"),
        cols, cols, cols, cols, cols, cols,
        both, both, both, P("tp"), P("tp"), P("fs"), both, P("fs"), cols, cols, both,
    )
    out_specs = (
        split, split, P("fs"),
        cols, cols, cols, cols, cols, cols,
        both, both, both, P("tp"), P("tp"), P("fs"), both, P("fs"), cols, cols, both,
    )
    return jax.shard_map(
        per_device, mesh=mesh, in_specs=in_specs, out_specs=out_specs, check_vma=False
    )
```
